32 devices in a mesh: dp: 8 (over z, x), blk: 4 (over y, core).
Axes of the slice: x: 2, y: 2, z: 4, core: 2. Of those that a mesh axis runs over, the one named last changes fastest.
Arguments:
- inputs: bfloat16 [8, 1536, 768], P('dp', 'blk'), may hold values from -6 to 6
- clip_ids: int32 [8, 1536], P('dp', 'blk'), may hold values from 0 to 5, as said below
- ln1_gain: bfloat16 [768], P(('dp', 'blk')), may hold values from 0.5 to 1.5
- ln1_bias: bfloat16 [768], P(('dp', 'blk')), may hold values from -4 to 4
- w_qkv: bfloat16 [768, 2304], P(('dp', 'blk')), may hold values from -0.21875 to 0.21875
- qv_bias: bfloat16 [1536], P(('dp', 'blk')), may hold values from -6 to 6
- w_out: bfloat16 [768, 768], P(('dp', 'blk')), may hold values from -6 to 6
- out_bias: bfloat16 [768], P(('dp', 'blk')), may hold values from -4 to 4
- ln2_gain: bfloat16 [768], P(('dp', 'blk')), may hold values from 0.5 to 1.5
- ln2_bias: bfloat16 [768], P(('dp', 'blk')), may hold values from -4 to 4
- w_up: bfloat16 [768, 3072], P(('dp', 'blk')), may hold values from -0.21875 to 0.21875
- up_bias: bfloat16 [3072], P(('dp', 'blk')), may hold values from -4 to 4
- w_down: bfloat16 [3072, 768], P(('dp', 'blk')), may hold values from -0.109375 to 0.109375
- down_bias: bfloat16 [768], P(('dp', 'blk')), may hold values from -4 to 4
- out_grad: bfloat16 [8, 1536, 768], P('dp', 'blk'), may hold values from -6 to 6
Outputs:
- output: bfloat16 [8, 1536, 768], P('dp', 'blk')
- input_grad: float32 [8, 1536, 768], P('dp', 'blk')
- ln1_gain_grad: float32 [768], P(('dp', 'blk'))
- ln1_bias_grad: float32 [768], P(('dp', 'blk'))
- w_qkv_grad: float32 [768, 2304], P(('dp', 'blk'))
- qv_bias_grad: float32 [1536], P(('dp', 'blk'))
- w_out_grad: float32 [768, 768], P(('dp', 'blk'))
- out_bias_grad: float32 [768], P(('dp', 'blk'))
- ln2_gain_grad: float32 [768], P(('dp', 'blk'))
- ln2_bias_grad: float32 [768], P(('dp', 'blk'))
- w_up_grad: float32 [768, 3072], P(('dp', 'blk'))
- up_bias_grad: float32 [3072], P(('dp', 'blk'))
- w_down_grad: float32 [3072, 768], P(('dp', 'blk'))
- down_bias_grad: float32 [768], P(('dp', 'blk'))
The draws below stay inside these ranges and needn't reach their ends.
Inputs may be any that keep to these rules, and one draw needn't show every extreme that they name: `clip_ids`: in each sequence the clip numbers start at 0 and rise by 0 or 1 from one patch to the next. One sequence holds three clips or fewer, one of which begins among its first 192 patches and ends among its last 192; every other sequence holds exactly six clips, the k-th boundary within 64 patches of k * 256.
All inputs are finite; a program needn't handle non-finite values.
Results may differ from the reference program's by a relative error of at most 0.014.
Values may be sent and summed in bfloat16 or wider, within the bound.
No kernel may reach another device: no remote copies, remote signals or barrier semaphores. Data moves between devices by JAX's collectives and lax.ppermute only.
A program may use at most 192 MiB of HBM per device.

```python
import jax
import jax.numpy as jnp
from jax import lax

D = 768
HEADS = 12
HEAD_DIM = 64
FF = 3072
TOK_DEV = 384
SEQ = 1536
SEQS = 8


def draw_clip_ids(key, part):
    key = jax.random.fold_in(key, 7)
    first_key, last_key, jitter_key, pick_key = jax.random.split(key, 4)
    position = jnp.arange(SEQ, dtype=jnp.int32)[None, :, None]
    spread = SEQ // 24
    base = jnp.arange(1, 6, dtype=jnp.int32) * SEQ // 6
    jitter = jax.random.randint(jitter_key, (SEQS, 5), -spread, spread + 1, dtype=jnp.int32)
    packed_bounds = base[None, :] + jitter
    opening = jax.random.randint(first_key, (SEQS, 1), 1, max(2, TOK_DEV // 2), dtype=jnp.int32)
    closing = jax.random.randint(last_key, (SEQS, 1), SEQ - max(1, TOK_DEV // 2), SEQ, dtype=jnp.int32)
    beyond = jnp.full((SEQS, 3), SEQ, dtype=jnp.int32)
    spanning_bounds = jnp.concatenate([opening, closing + 1, beyond], axis=1)
    chosen = jax.random.randint(pick_key, (), 0, SEQS, dtype=jnp.int32)
    is_chosen = (jnp.arange(SEQS, dtype=jnp.int32) == chosen)[:, None]
    bounds = jnp.where(is_chosen, spanning_bounds, packed_bounds)
    return jnp.sum((position >= bounds[:, None, :]).astype(jnp.int32), axis=2).astype(jnp.int32)


def levels(key, extent, cuts, least, high):
    factor_of, own = 1.0, jax.random.fold_in(key, 6)
    for dim, shards_of in cuts:
        steps = jnp.exp(jax.random.uniform(jax.random.fold_in(own, dim), (shards_of,), jnp.float32, least / len(cuts), high / len(cuts)))
        factor_of = factor_of * jnp.repeat(steps, extent[dim] // shards_of).reshape([-1 if axis == dim else 1 for axis in range(len(extent))])
    return factor_of


def noise(stream_key, shape, scale, limit, cuts=(), kind=jnp.bfloat16):
    values = scale * jax.random.normal(stream_key, shape, jnp.float32)
    if cuts:
        values = values * levels(stream_key, shape, cuts, -0.22, 0.18)
    return jnp.clip(values, -limit, limit).astype(kind)


def setup_inputs(seed: int = 0) -> dict:
    streams_of = jax.random.split(jax.random.key(seed), 16)
    return {
        "inputs": noise(streams_of[0], (SEQS, SEQ, D), 1.0, 6.0, ((0, 8), (1, 4))),
        "clip_ids": draw_clip_ids(jax.random.fold_in(streams_of[15], 71), 0),
        "ln1_gain": jnp.clip(1.0 + 0.1 * jax.random.normal(streams_of[2], (D,), jnp.float32), 0.5, 1.5).astype(jnp.bfloat16),
        "ln1_bias": noise(streams_of[3], (D,), 0.3, 4.0, ((0, 32),)),
        "w_qkv": noise(streams_of[4], (D, 3 * D), D ** -0.5, 0.21875, ((0, 32),)),
        "qv_bias": noise(streams_of[5], (2 * D,), 0.5, 6.0, ((0, 32),)),
        "w_out": noise(streams_of[6], (D, D), (max(1, 2 * D // SEQ)) ** -0.5, 6.0, ((0, 32),)),
        "out_bias": noise(streams_of[7], (D,), 0.3, 4.0, ((0, 32),)),
        "ln2_gain": jnp.clip(1.0 + 0.1 * jax.random.normal(streams_of[8], (D,), jnp.float32), 0.5, 1.5).astype(jnp.bfloat16),
        "ln2_bias": noise(streams_of[9], (D,), 0.3, 4.0, ((0, 32),)),
        "w_up": noise(streams_of[10], (D, FF), D ** -0.5, 0.21875, ((0, 32),)),
        "up_bias": noise(streams_of[11], (FF,), 0.3, 4.0, ((0, 32),)),
        "w_down": noise(streams_of[12], (FF, D), FF ** -0.5, 0.109375, ((0, 32),)),
        "down_bias": noise(streams_of[13], (D,), 0.3, 4.0, ((0, 32),)),
        "out_grad": noise(streams_of[14], (SEQS, SEQ, D), 1.0, 6.0, ((0, 8), (1, 4))),
    }


@jax.custom_vjp
def low(v):
    return lax.optimization_barrier(v.astype(jnp.bfloat16)).astype(jnp.float32)

@jax.custom_vjp
def low_back(v):
    return v

def low_keep(v):
    return (low(v), None)

def low_pass(kept, grad):
    return (grad,)

def back_keep(v):
    return (v, None)

def back_low(kept, grad):
    return (low(grad),)
low.defvjp(low_keep, low_pass)
low_back.defvjp(back_keep, back_low)
norm_eps = 1e-06
masked_fill = -1e+30
highest = lax.Precision.HIGHEST

def norm_rows(values, gain_vec, shift_vec):
    row_mean = lax.optimization_barrier(jnp.mean(values, axis=-1, keepdims=True))
    centered = values - row_mean
    variance = lax.optimization_barrier(jnp.mean(centered * centered, axis=-1, keepdims=True))
    return centered * lax.rsqrt(variance + norm_eps) * gain_vec + shift_vec

def dot_high(left_side, right_side):
    return jnp.dot(left_side, right_side, precision=highest, preferred_element_type=jnp.float32)

def attend_block(query_block, clip_block, key_rows, value_rows, clip_row):
    raw_scores = low_back(jnp.einsum('qhd,khd->hqk', query_block, key_rows, precision=highest))
    scores = raw_scores * HEAD_DIM ** (-0.5)
    visible = (clip_block[:, None] == clip_row[None, :])[None]
    masked = jnp.where(visible, scores, masked_fill)
    row_max = lax.optimization_barrier(jnp.max(masked, axis=-1, keepdims=True))
    weights = jnp.where(visible, jnp.exp(masked - row_max), 0.0)
    row_total = lax.optimization_barrier(jnp.sum(weights, axis=-1, keepdims=True))
    summed = jnp.einsum('hqk,khd->hqd', low(weights), value_rows, precision=highest)
    return jnp.transpose(summed / row_total, (1, 0, 2))

def attend_sequence(operands):
    queries, key_rows, value_rows, clip_row = operands
    query_rows = 512 if SEQ % 512 == 0 else SEQ
    block_count = SEQ // query_rows
    query_blocks = queries.reshape(block_count, query_rows, HEADS, HEAD_DIM)
    clip_blocks = clip_row.reshape(block_count, query_rows)

    def one_block(block_pair):
        return attend_block(block_pair[0], block_pair[1], key_rows, value_rows, clip_row)
    return lax.map(jax.checkpoint(one_block), (query_blocks, clip_blocks)).reshape(SEQ, D)

def layer_forward(inputs, ln1_gain, ln1_bias, w_qkv, qv_bias, w_out, out_bias, ln2_gain, ln2_bias, w_up, up_bias, w_down, down_bias, clip_ids):
    token_rows = inputs.reshape(SEQS * SEQ, D)
    normed_one = low(norm_rows(token_rows, ln1_gain, ln1_bias))
    mixed = dot_high(normed_one, w_qkv)
    queries = low_back(low(mixed[:, :D] + qv_bias[:D]))
    key_rows = low_back(low(mixed[:, D:2 * D]))
    value_rows = low_back(low(mixed[:, 2 * D:] + qv_bias[D:]))
    head_shape = (SEQS, SEQ, HEADS, HEAD_DIM)
    attended = lax.map(attend_sequence, (queries.reshape(head_shape), key_rows.reshape(head_shape), value_rows.reshape(head_shape), clip_ids))
    attended = low_back(low(attended.reshape(SEQS * SEQ, D)))
    branch = low_back(dot_high(attended, w_out) + out_bias)
    after_attn = token_rows + branch
    normed_two = low(norm_rows(after_attn, ln2_gain, ln2_bias))
    hidden = low_back(dot_high(normed_two, w_up) + up_bias)
    active = low(jax.nn.gelu(hidden, approximate=False))
    result = after_attn + dot_high(active, w_down) + down_bias
    return result.reshape(SEQS, SEQ, D)

def reference(inputs, clip_ids, ln1_gain, ln1_bias, w_qkv, qv_bias, w_out, out_bias, ln2_gain, ln2_bias, w_up, up_bias, w_down, down_bias, out_grad):
    params = tuple((weight_in.astype(jnp.float32) for weight_in in (ln1_gain, ln1_bias, w_qkv, qv_bias, w_out, out_bias, ln2_gain, ln2_bias, w_up, up_bias, w_down, down_bias)))

    def forward(*floats):
        return layer_forward(*floats, clip_ids)
    result, pullback = jax.vjp(forward, inputs.astype(jnp.float32), *params)
    grads = pullback(out_grad.astype(jnp.float32))
    return (result.astype(jnp.bfloat16), grads[0], grads[1], grads[2], grads[3], grads[4], grads[5], grads[6], grads[7], grads[8], grads[9], grads[10], grads[11], grads[12])
```

```python
import functools
import math

import jax
import jax.numpy as jnp
from jax import lax
from jax.experimental import pallas as pl
from jax.experimental.pallas import tpu as pltpu
from jax.sharding import PartitionSpec as P

HEAD_DIM = 64
NORM_EPS = 1e-06
LOG2E = math.log2(math.e)
f32 = jnp.float32
bf16 = jnp.bfloat16
AXES = ("dp", "blk")


def mm(a, b, dims=((1,), (0,))):
    return lax.dot_general(a, b, (dims, ((), ())), preferred_element_type=f32)


class Grid:
    def __init__(self, dp, blk):
        self.core = 2
        self.q = blk // 2
        self.x = 2
        self.z = dp // 2
        self.size = {"z": self.z, "x": self.x, "q": self.q, "c": 2}
        me_dp, me_blk = lax.axis_index("dp"), lax.axis_index("blk")
        self.me = {
            "z": me_dp // 2,
            "x": me_dp % 2,
            "q": me_blk // 2,
            "c": me_blk % 2,
        }

    def pairs(self, axis, step):
        out = []
        for z in range(self.z):
            for x in range(self.x):
                for q in range(self.q):
                    for c in range(2):
                        at = {"z": z, "x": x, "q": q, "c": c}
                        to = dict(at)
                        to[axis] = (at[axis] + step) % self.size[axis]
                        out.append((self.flat(at), self.flat(to)))
        return out

    def flat(self, at):
        return ((at["z"] * self.x + at["x"]) * self.q + at["q"]) * 2 + at["c"]

    def shift(self, value, axis, step):
        return lax.ppermute(value, AXES, self.pairs(axis, step))

    def gather(self, value, axis):
        n, me = self.size[axis], self.me[axis]
        got = [value] + [self.shift(value, axis, k) for k in range(1, n)]
        rows = []
        for j in range(n):
            pick = got[0]
            for k in range(1, n):
                pick = jnp.where((me - k) % n == j, got[k], pick)
            rows.append(pick)
        return jnp.stack(rows)

    def scatter(self, value, axis, dim):
        n, me = self.size[axis], self.me[axis]
        take = lambda j: lax.dynamic_index_in_dim(value, j, dim, keepdims=False)
        total = take(me).astype(f32)
        for k in range(1, n):
            part = take((me + k) % n).astype(bf16)
            total = total + self.shift(part, axis, k).astype(f32)
        return total


def gather_chips(grid, value, order):
    at = []
    for axis in order:
        value = grid.gather(value, axis)
        at.insert(0, axis)
    perm = [at.index(a) for a in ("z", "x", "q")]
    return jnp.transpose(value, perm + list(range(3, value.ndim)))


def scatter_chips(grid, value, order):
    at = ["z", "x", "q"]
    for axis in order:
        dim = at.index(axis)
        value = grid.scatter(value, axis, dim)
        at.pop(dim)
    return value


def first_lanes(head):
    lane = lax.broadcasted_iota(jnp.int32, (1, 2 * HEAD_DIM), 1)
    return lane < HEAD_DIM if head == 0 else lane >= HEAD_DIM


def chunk_of(rows):
    return 1536 if rows % 1536 == 0 else rows


def attn_fwd_kernel(q_ref, k_ref, v_ref, hot_ref, pen_ref, o_ref, lse_ref):
    total_keys = k_ref.shape[0]
    chunk = chunk_of(total_keys)
    steps = total_keys // chunk
    query_rows = q_ref.shape[0]
    query, hot = q_ref[...], hot_ref[...]
    outs = []
    for head in range(2):
        sel = first_lanes(head)
        q_aug = jnp.where(sel, query, hot)

        def scores(rows):
            k_aug = jnp.where(sel, k_ref[rows, :], pen_ref[rows, :])
            return mm(k_aug, q_aug, ((1,), (1,)))

        def weigh(rows, s, top):
            p = jnp.exp2(s - top)
            added = mm(v_ref[rows, :], p.astype(bf16), ((0,), (0,)))
            return jnp.sum(p, axis=0, keepdims=True), added

        if steps == 1:
            s = scores(slice(0, chunk))
            top = jnp.max(s, axis=0, keepdims=True)
            total, acc = weigh(slice(0, chunk), s, top)
        else:

            def step(i, carry):
                top, total, acc = carry
                rows = pl.ds(pl.multiple_of(i * chunk, chunk), chunk)
                s = scores(rows)
                new_top = jnp.maximum(top, jnp.max(s, axis=0, keepdims=True))
                more, added = weigh(rows, s, new_top)
                fade = jnp.exp2(top - new_top)
                return new_top, total * fade + more, acc * fade + added

            top, total, acc = lax.fori_loop(
                0,
                steps,
                step,
                (
                    jnp.full((1, query_rows), -1e30, f32),
                    jnp.zeros((1, query_rows), f32),
                    jnp.zeros((2 * HEAD_DIM, query_rows), f32),
                ),
            )
        outs.append((acc / total)[head * HEAD_DIM : (head + 1) * HEAD_DIM])
        lse_ref[0, head : head + 1, :] = top + jnp.log2(total)
    o_ref[...] = jnp.concatenate(outs, axis=0).T


def attn_fwd(queries, keys, values, hot, pen):
    rows, width = queries.shape
    total_keys = keys.shape[0]
    pairs = width // 128
    block = 256 if rows % 256 == 0 else rows
    cost = pl.CostEstimate(
        flops=4 * rows * total_keys * width * 4,
        bytes_accessed=(rows * 3 + total_keys * 2) * width * 2,
        transcendentals=rows * total_keys * width // 64,
    )
    return pl.pallas_call(
        attn_fwd_kernel,
        grid=(pairs, rows // block),
        in_specs=[
            pl.BlockSpec((block, 128), lambda p, i: (i, p)),
            pl.BlockSpec((total_keys, 128), lambda p, i: (0, p)),
            pl.BlockSpec((total_keys, 128), lambda p, i: (0, p)),
            pl.BlockSpec((block, 128), lambda p, i: (i, 0)),
            pl.BlockSpec((total_keys, 128), lambda p, i: (0, 0)),
        ],
        out_specs=[
            pl.BlockSpec((block, 128), lambda p, i: (i, p)),
            pl.BlockSpec((1, 2, block), lambda p, i: (p, 0, i)),
        ],
        out_shape=[
            jax.ShapeDtypeStruct((rows, width), f32),
            jax.ShapeDtypeStruct((pairs, 2, rows), f32),
        ],
        compiler_params=pltpu.CompilerParams(vmem_limit_bytes=56 * 2**20),
        cost_estimate=cost,
        name="attn_fwd",
    )(queries, keys, values, hot, pen)


def attn_bwd_kernel(
    q_ref, k_ref, v_ref, hot_ref, pen_ref, o_ref, do_ref, lse_ref, dq_ref, dk_ref, dv_ref, dk_acc, dv_acc
):
    total_keys = k_ref.shape[0]
    chunk = chunk_of(total_keys)
    steps = total_keys // chunk
    at, last = pl.program_id(1), pl.num_programs(1) - 1
    query, hot, grad = q_ref[...], hot_ref[...], do_ref[...]

    @pl.when(at == 0)
    def _():
        dk_acc[...] = jnp.zeros_like(dk_acc)
        dv_acc[...] = jnp.zeros_like(dv_acc)

    flipped = (grad.astype(f32) * o_ref[...]).T
    zero = jnp.zeros_like(query)

    def step(rows):
        keys, values, pen = k_ref[rows, :], v_ref[rows, :], pen_ref[rows, :]
        dq = None
        dk = dk_acc[rows, :]
        dv = dv_acc[rows, :]
        for head in range(2):
            sel = first_lanes(head)
            delta = jnp.sum(
                flipped[head * HEAD_DIM : (head + 1) * HEAD_DIM], axis=0, keepdims=True
            )
            k_aug = jnp.where(sel, keys, pen)
            s = mm(k_aug, jnp.where(sel, query, hot), ((1,), (1,)))
            p = jnp.exp2(s - lse_ref[0, head : head + 1, :])
            grad_h = jnp.where(sel, grad, zero)
            dp = mm(values, grad_h, ((1,), (1,)))
            ds = (p * (dp - delta)).astype(bf16)
            dv = dv + mm(p.astype(bf16), grad_h)
            dk = dk + mm(ds, jnp.where(sel, query, zero))
            part = mm(keys, ds, ((0,), (0,)))
            part = part[head * HEAD_DIM : (head + 1) * HEAD_DIM]
            dq = part if dq is None else jnp.concatenate([dq, part], axis=0)
        dk_acc[rows, :] = dk
        dv_acc[rows, :] = dv
        return dq

    if steps == 1:
        dq = step(slice(0, chunk))
    else:
        dq = lax.fori_loop(
            0,
            steps,
            lambda i, total: total + step(pl.ds(pl.multiple_of(i * chunk, chunk), chunk)),
            jnp.zeros((2 * HEAD_DIM, query.shape[0]), f32),
        )
    dq_ref[...] = (dq.T * HEAD_DIM**-0.5).astype(bf16)

    @pl.when(at == last)
    def _():
        dk_ref[...] = (dk_acc[...] * (1.0 / LOG2E)).astype(bf16)
        dv_ref[...] = dv_acc[...].astype(bf16)


def attn_bwd(queries, keys, values, hot, pen, attended, d_attended, lse):
    rows, width = queries.shape
    total_keys = keys.shape[0]
    pairs = width // 128
    block = 256 if rows % 256 == 0 else rows
    by_query = pl.BlockSpec((block, 128), lambda p, i: (i, p))
    by_key = pl.BlockSpec((total_keys, 128), lambda p, i: (0, p))
    cost = pl.CostEstimate(
        flops=10 * rows * total_keys * width * 4,
        bytes_accessed=(rows * 5 + total_keys * 4) * width * 2,
        transcendentals=rows * total_keys * width // 64,
    )
    return pl.pallas_call(
        attn_bwd_kernel,
        grid=(pairs, rows // block),
        in_specs=[
            by_query,
            by_key,
            by_key,
            pl.BlockSpec((block, 128), lambda p, i: (i, 0)),
            pl.BlockSpec((total_keys, 128), lambda p, i: (0, 0)),
            by_query,
            by_query,
            pl.BlockSpec((1, 2, block), lambda p, i: (p, 0, i)),
        ],
        out_specs=[by_query, by_key, by_key],
        out_shape=[
            jax.ShapeDtypeStruct((rows, width), bf16),
            jax.ShapeDtypeStruct((total_keys, width), bf16),
            jax.ShapeDtypeStruct((total_keys, width), bf16),
        ],
        scratch_shapes=[pltpu.VMEM((total_keys, 128), f32), pltpu.VMEM((total_keys, 128), f32)],
        compiler_params=pltpu.CompilerParams(vmem_limit_bytes=56 * 2**20),
        cost_estimate=cost,
        name="attn_bwd",
    )(queries, keys, values, hot, pen, attended, d_attended, lse)


def ff_kernel(
    h2_ref, dy_ref, up_ref, down_ref, bias_ref, out_in, dh_in, gdown_ref, gup_ref, gbias_ref, out_ref, dh_ref, act_s, dhid_s, h2t_s
):
    @pl.when(pl.program_id(0) == 0)
    def _():
        h2t_s[...] = h2_ref[...].T
        out_ref[...] = out_in[...]
        dh_ref[...] = dh_in[...]

    rows = h2_ref.shape[0]
    part = 256
    w_up, w_down = up_ref[...], down_ref[...]
    for at in range(0, rows, part):
        here = slice(at, at + part)
        hidden = mm(h2_ref[here, :], w_up) + bias_ref[...]
        phi = 0.5 * (1.0 + lax.erf(hidden * (0.5**0.5)))
        dens = jnp.exp(-0.5 * hidden * hidden) * (1.0 / math.sqrt(2.0 * math.pi))
        act_s[here, :] = (hidden * phi).astype(bf16)
        d_act = mm(dy_ref[here, :], w_down, ((1,), (1,)))
        dhid_s[here, :] = (d_act * (phi + hidden * dens)).astype(bf16)
    act, d_hidden = act_s[...], dhid_s[...]
    gdown_ref[...] = mm(act, dy_ref[...], ((0,), (0,))).astype(bf16)
    gup_ref[...] = mm(h2t_s[...], d_hidden).astype(bf16)
    gbias_ref[...] = jnp.sum(d_hidden.astype(f32), axis=0, keepdims=True)
    out_ref[...] += mm(act, w_down)
    dh_ref[...] += mm(d_hidden, w_up, ((1,), (1,)))


def feed_forward(h2, dy, w_up, w_down, up_bias, out_in, dh_in):
    rows, width = h2.shape
    units = w_up.shape[1]
    tile = 256
    whole = pl.BlockSpec((rows, width), lambda j: (0, 0))
    cols = pl.BlockSpec((width, tile), lambda j: (0, j))
    vec = pl.BlockSpec((1, tile), lambda j: (0, j))
    lines = pl.BlockSpec((tile, width), lambda j: (j, 0))
    cost = pl.CostEstimate(
        flops=12 * rows * width * units,
        bytes_accessed=8 * units * width + 12 * rows * width,
        transcendentals=2 * rows * units,
    )
    return pl.pallas_call(
        ff_kernel,
        grid=(units // tile,),
        in_specs=[whole, whole, cols, lines, vec, whole, whole],
        out_specs=[lines, cols, vec, whole, whole],
        out_shape=[
            jax.ShapeDtypeStruct((units, width), bf16),
            jax.ShapeDtypeStruct((width, units), bf16),
            jax.ShapeDtypeStruct((1, units), f32),
            jax.ShapeDtypeStruct((rows, width), f32),
            jax.ShapeDtypeStruct((rows, width), f32),
        ],
        scratch_shapes=[
            pltpu.VMEM((rows, tile), bf16),
            pltpu.VMEM((rows, tile), bf16),
            pltpu.VMEM((width, rows), bf16),
        ],
        compiler_params=pltpu.CompilerParams(vmem_limit_bytes=56 * 2**20),
        cost_estimate=cost,
        name="feed_forward",
    )(h2, dy, w_up, w_down, up_bias, out_in, dh_in)


def normalise(values):
    mean = jnp.mean(values, axis=-1, keepdims=True)
    centered = values - mean
    var = jnp.mean(centered * centered, axis=-1, keepdims=True)
    rstd = lax.rsqrt(var + NORM_EPS)
    return centered * rstd, rstd


def norm_back(grad, normed, rstd, gain):
    e = grad * gain
    return (
        e
        - jnp.mean(e, axis=-1, keepdims=True)
        - normed * jnp.mean(e * normed, axis=-1, keepdims=True)
    ) * rstd


def in_order(first, mine, other):
    return jnp.stack([jnp.where(first, mine, other), jnp.where(first, other, mine)])


def body(
    dp,
    blk,
    inputs,
    clip_ids,
    ln1_gain,
    ln1_bias,
    w_qkv,
    qv_bias,
    w_out,
    out_bias,
    ln2_gain,
    ln2_bias,
    w_up,
    up_bias,
    w_down,
    down_bias,
    out_grad,
):
    grid = Grid(dp, blk)
    core = grid.me["c"]
    first = core == 0
    chips = grid.z * grid.x * grid.q
    width = inputs.shape[2]
    half = width // 2
    local = inputs.shape[1]
    units = w_up.shape[1] // 2
    swap = lambda v: grid.shift(v, "c", 1)
    pick = lambda v: lax.dynamic_index_in_dim(v, core, 0, keepdims=False)
    unpick = lambda v: lax.dynamic_index_in_dim(v, 1 - core, 0, keepdims=False)

    pad = jnp.zeros((16, width), bf16).at[0, :local].set(clip_ids[0].astype(bf16))
    mine = jnp.concatenate([inputs[0], pad], axis=0)
    rows_of = [mine] + [grid.shift(mine, "q", k) for k in range(1, grid.q)]
    both = [in_order(first, r, swap(r)) for r in rows_of]
    token_rows = jnp.concatenate([b[:, :local].reshape(2 * local, width) for b in both])
    clips = jnp.concatenate([b[:, local, :local].reshape(2 * local) for b in both])
    chip_rows = 2 * local

    small = jnp.concatenate(
        [ln1_gain, ln1_bias, out_bias, ln2_gain, ln2_bias, down_bias, qv_bias, up_bias]
    )
    shard = w_qkv.shape[0]
    split = w_qkv.reshape(shard, 3, 2, half)
    my_qkv = lax.dynamic_index_in_dim(split, core, 2, keepdims=False).reshape(shard, 3 * half)
    to_qkv = lax.dynamic_index_in_dim(split, 1 - core, 2, keepdims=False).reshape(shard, 3 * half)
    small_row = jnp.zeros((8, 3 * half), bf16).at[0, : small.shape[0]].set(small)
    got = swap(jnp.concatenate([to_qkv, small_row]))
    pair = in_order(first, jnp.concatenate([my_qkv, small_row]), got)
    n_small = small.shape[0]
    small_pair = jnp.concatenate([pair[0, shard:, :n_small], pair[1, shard:, :n_small]], axis=1)
    qkv_chip = jnp.concatenate(
        [
            pair[:, :shard].reshape(2 * shard, 3 * half),
            jnp.pad(small_pair, ((0, 0), (0, 3 * half - 2 * n_small))),
        ]
    )
    qkv_all = gather_chips(grid, qkv_chip, ("z", "x", "q")).reshape(chips, 2 * shard + 8, 3 * half)
    full_qkv = qkv_all[:, : 2 * shard].reshape(width, 3 * half)
    small_all = qkv_all[:, 2 * shard, : 2 * n_small].reshape(chips, 2, n_small).astype(f32)
    vec = lambda at, n: small_all[:, :, at : at + n].reshape(chips * 2 * n)
    n_vec = ln1_gain.shape[0]
    gain_one, shift_one, bias_out, gain_two, shift_two, bias_down = (
        vec(n_vec * i, n_vec) for i in range(6)
    )
    bias_qv = vec(n_vec * 6, 2 * n_vec).reshape(2, 2, half)
    bias_q, bias_v = (
        lax.dynamic_index_in_dim(bias_qv[i], core, 0, keepdims=False) for i in range(2)
    )
    bias_up = lax.dynamic_index_in_dim(
        small_all[:, :, 8 * n_vec :], core, 1, keepdims=False
    ).reshape(1, units)

    out_all = gather_chips(grid, w_out, ("z", "x", "q")).reshape(chips, shard, width)
    full_out = jnp.transpose(in_order(first, out_all, swap(out_all)), (1, 0, 2, 3)).reshape(
        width, width
    )

    up_split = jnp.transpose(w_up.reshape(shard, chips, 2, units // chips), (2, 0, 1, 3)).reshape(
        2, shard, units
    )
    up_chip = in_order(first, pick(up_split), swap(unpick(up_split))).reshape(2 * shard, units)
    full_up = gather_chips(grid, up_chip, ("z", "q", "x")).reshape(width, units)
    full_down = gather_chips(grid, w_down, ("z", "x", "q")).reshape(units, width)

    x_all = token_rows.astype(f32)
    n1, rstd1 = normalise(x_all)
    h1 = (n1 * gain_one + shift_one).astype(bf16)
    w_q, w_kv = full_qkv[:, :half], full_qkv[:, half:]
    scale = LOG2E * HEAD_DIM**-0.5
    queries = ((mm(h1[:chip_rows], w_q) + bias_q) * scale).astype(bf16)
    kv = mm(h1, w_kv)
    keys = kv[:, :half].astype(bf16)
    values = (kv[:, half:] + bias_v).astype(bf16)

    lane = lax.broadcasted_iota(jnp.int32, (1, 128), 1) % HEAD_DIM
    same = clips[:, None].astype(jnp.int32) == lane
    hot = same[:chip_rows].astype(bf16)
    pen = jnp.where(same | (lane >= 8), 0.0, -1e30).astype(bf16)
    attended, lse = attn_fwd(queries, keys, values, hot, pen)

    att_mine = attended.astype(bf16)
    att_full = jnp.concatenate(list(in_order(first, att_mine, swap(att_mine))), axis=1)
    after = x_all[:chip_rows] + mm(att_full, full_out) + bias_out
    n2, rstd2 = normalise(after)
    h2 = (n2 * gain_two + shift_two).astype(bf16)

    dy_mine = out_grad[0]
    dy = in_order(first, dy_mine, swap(dy_mine)).reshape(chip_rows, width)
    nil = jnp.zeros((chip_rows, width), f32)
    gdown, gup, gbias, ff_out, d_h2 = feed_forward(
        h2, dy, full_up, full_down, bias_up, nil, nil
    )
    by_core = lambda v: v.reshape(2, local, width)
    out_got = swap(unpick(by_core(ff_out)).astype(bf16)).astype(f32)
    output = (pick(by_core(ff_out)) + out_got + pick(by_core(after)) + bias_down).astype(bf16)[None]

    d_h2 = d_h2 + swap(d_h2.astype(bf16)).astype(f32)
    dy_f = dy.astype(f32)
    gain_two_g = jnp.sum(d_h2 * n2, axis=0)
    shift_two_g = jnp.sum(d_h2, axis=0)
    d_after = dy_f + norm_back(d_h2, n2, rstd2, gain_two)
    d_branch = d_after.astype(bf16)
    out_bias_g = jnp.sum(d_branch.astype(f32), axis=0)
    down_bias_g = jnp.sum(dy_f, axis=0)
    d_cols = lax.dynamic_slice_in_dim(d_branch, core * half, half, 1)
    g_out = mm(att_full, d_cols, ((0,), (0,))).astype(bf16)
    my_out = lax.dynamic_slice_in_dim(full_out, core * half, half, 0)
    d_att = mm(d_branch, my_out, ((1,), (1,))).astype(bf16)

    dq, dk, dv = attn_bwd(queries, keys, values, hot, pen, attended, d_att, lse)
    dkv = jnp.concatenate([dk, dv], axis=1)
    g_qkv = jnp.concatenate(
        [mm(h1[:chip_rows], dq, ((0,), (0,))), mm(h1, dkv, ((0,), (0,)))], axis=1
    ).astype(bf16)
    bias_g = jnp.stack(
        [jnp.sum(dq.astype(f32), axis=0), jnp.sum(dv.astype(f32), axis=0)]
    )

    d_h1 = mm(dkv, w_kv, ((1,), (1,)))
    d_own = d_h1[:chip_rows] + mm(dq, w_q, ((1,), (1,)))
    d_blocks = [d_own] + [
        d_h1[chip_rows * k : chip_rows * (k + 1)] for k in range(1, grid.q)
    ]
    summed = []
    for block in d_blocks:
        block = by_core(block)
        summed.append(pick(block) + swap(unpick(block).astype(bf16)).astype(f32))
    d_mine = summed[0]
    for k in range(1, grid.q):
        d_mine = d_mine + grid.shift(summed[k].astype(bf16), "q", grid.q - k).astype(f32)
    n1_mine = pick(by_core(n1[:chip_rows]))
    rstd1_mine = pick(rstd1[:chip_rows].reshape(2, local, 1))
    gain_one_g = jnp.sum(d_mine * n1_mine, axis=0)
    shift_one_g = jnp.sum(d_mine, axis=0)
    input_grad = (
        pick(by_core(d_after)) + norm_back(d_mine, n1_mine, rstd1_mine, gain_one)
    )[None]

    spread = lambda v: v.reshape((grid.z, grid.x, grid.q, v.shape[0] // chips) + v.shape[1:])
    w_down_g = scatter_chips(grid, spread(gdown), ("q", "x", "z"))
    up_chip_g = scatter_chips(grid, spread(gup), ("x", "q", "z")).reshape(2, shard, units)
    up_other = swap(unpick(up_chip_g).astype(bf16)).astype(f32)
    up_pair = in_order(first, pick(up_chip_g), up_other).reshape(2, shard, chips, units // chips)
    w_up_g = jnp.transpose(up_pair, (1, 2, 0, 3)).reshape(shard, 2 * units)
    out_chip_g = scatter_chips(grid, spread(g_out), ("q", "x", "z")).reshape(2, shard, half)
    out_other = swap(unpick(out_chip_g).astype(bf16)).astype(f32)
    w_out_g = jnp.concatenate(list(in_order(first, pick(out_chip_g), out_other)), axis=1)
    qkv_chip_g = scatter_chips(grid, spread(g_qkv), ("q", "x", "z")).reshape(2, shard, 3 * half)
    qkv_other = swap(unpick(qkv_chip_g).astype(bf16)).astype(f32)
    qkv_pair = in_order(first, pick(qkv_chip_g), qkv_other).reshape(2, shard, 3, half)
    w_qkv_g = jnp.transpose(qkv_pair, (1, 2, 0, 3)).reshape(shard, 6 * half)

    per = lambda v: v.reshape(chips, 2, n_vec)
    bias_pair = in_order(first, bias_g, swap(bias_g))
    qv_sum = jnp.transpose(bias_pair, (1, 0, 2)).reshape(chips, 2, 2 * n_vec)
    one_g = jnp.stack([gain_one_g, shift_one_g])
    one_g = one_g + swap(one_g)
    vectors = jnp.concatenate(
        [
            per(one_g[0]),
            per(one_g[1]),
            per(out_bias_g),
            per(gain_two_g),
            per(shift_two_g),
            per(down_bias_g),
            qv_sum,
        ],
        axis=2,
    )
    vectors = lax.dynamic_index_in_dim(vectors, core, 1, keepdims=False)
    vectors = jnp.concatenate([vectors, gbias.reshape(chips, units // chips)], axis=1)
    vectors = scatter_chips(grid, spread(vectors)[..., 0, :], ("q", "x", "z"))
    cut = lambda at, n: vectors[at : at + n]
    return (
        output,
        input_grad,
        cut(0, n_vec),
        cut(n_vec, n_vec),
        w_qkv_g,
        cut(6 * n_vec, 2 * n_vec),
        w_out_g,
        cut(2 * n_vec, n_vec),
        cut(3 * n_vec, n_vec),
        cut(4 * n_vec, n_vec),
        w_up_g,
        cut(8 * n_vec, units // chips),
        w_down_g,
        cut(5 * n_vec, n_vec),
    )


def solution(mesh):
    both = P(("dp", "blk"))
    rows = P(("dp", "blk"), None)
    tokens = P("dp", "blk", None)
    return jax.shard_map(
        functools.partial(body, mesh.shape["dp"], mesh.shape["blk"]),
        mesh=mesh,
        in_specs=(
            tokens,
            P("dp", "blk"),
            both,
            both,
            rows,
            both,
            rows,
            both,
            both,
            both,
            rows,
            both,
            rows,
            both,
            tokens,
        ),
        out_specs=(
            tokens,
            tokens,
            both,
            both,
            rows,
            both,
            rows,
            both,
            both,
            both,
            rows,
            both,
            rows,
            both,
        ),
        check_vma=False,
    )
```

```python
import functools
import itertools
import math

import jax
import jax.numpy as jnp
from jax import lax
from jax.experimental import pallas as pl
from jax.experimental.pallas import tpu as pltpu
from jax.sharding import PartitionSpec as P

HEAD_DIM = 64
NORM_EPS = 1e-06
LOG2E = math.log2(math.e)
f32 = jnp.float32
bf16 = jnp.bfloat16
AXES = ("dp", "blk")


def mm(a, b, dims=((1,), (0,))):
    return lax.dot_general(a, b, (dims, ((), ())), preferred_element_type=f32)


SMALL = pl.CostEstimate(flops=1000, bytes_accessed=1000, transcendentals=0)


class Grid:
    def __init__(self, dp, blk):
        self.size = {"z": dp // 2, "x": 2, "q": blk // 2, "c": 2}
        self.z, self.x, self.q = dp // 2, 2, blk // 2
        self.chips = self.z * 2 * self.q
        me_dp, me_blk = lax.axis_index("dp"), lax.axis_index("blk")
        self.me = {"z": me_dp // 2, "x": me_dp % 2, "q": me_blk // 2, "c": me_blk % 2}
        self.place = jnp.stack([self.me[a] for a in ("z", "x", "q", "c")]).astype(jnp.int32)

    def flat(self, at):
        return ((at["z"] * self.x + at["x"]) * self.q + at["q"]) * 2 + at["c"]

    def shift(self, value, axis, step):
        pairs = []
        for z in range(self.z):
            for x in range(self.x):
                for q in range(self.q):
                    for c in range(2):
                        at = {"z": z, "x": x, "q": q, "c": c}
                        to = dict(at)
                        to[axis] = (at[axis] + step) % self.size[axis]
                        pairs.append((self.flat(at), self.flat(to)))
        return lax.ppermute(value, AXES, pairs)

    def chip(self, place, dz, dx, dq):
        z = -1 - dz if dz < 0 else lax.rem(place[0] + (self.z - dz), self.z)
        x = lax.rem(place[1] + (self.x - dx), self.x)
        q = lax.rem(place[2] + (self.q - dq), self.q)
        return (z * self.x + x) * self.q + q

    def relative(self, place, chip, near=False):
        z, x, q = chip // (self.x * self.q), chip // self.q % self.x, chip % self.q
        dx = lax.rem(x + self.x - place[1], self.x)
        dq = lax.rem(q + self.q - place[2], self.q)
        if near:
            z = lax.rem(z + self.z - place[0], self.z)
        return dx * self.q + dq, z

    def along(self, value, axis):
        return [self.shift(value, axis, k) for k in range(1, self.size[axis])]

    def line(self, value, others):
        return jnp.stack([value] + others)

    def corner_pieces(self, over, sides):
        half = self.z // 2
        return [
            (self.shift(over[:half], "q", k), self.shift(side[half:], "x", 1))
            for k, side in enumerate(sides, 1)
        ]

    def found(self, line, over, sides, corners, plain=False):
        half = self.z // 2
        zs = [-1 - z if plain else z for z in range(self.z)]
        out = [(line, [(z, 0, 0) for z in zs]), (over, [(z, 1, 0) for z in zs])]
        for k, (side, (a, b)) in enumerate(zip(sides, corners), 1):
            out.append((side, [(z, 0, k) for z in zs]))
            out.append((a, [(z, 1, k) for z in zs[:half]]))
            out.append((b, [(z, 1, k) for z in zs[half:]]))
        return out

    def found_last(self, plane, others):
        at = [(x, q) for x in range(2) for q in range(self.q)]
        return [(p, [(z, x, q) for x, q in at]) for z, p in enumerate([plane] + others)]


    def corners(self, value, first=()):
        half = self.z // 2
        over = value[self.q]
        late, sides = [], []
        for k in range(1, self.q):
            corner = value[self.q + k]
            got = behind(self.shift(corner[:half], "x", 1), first)
            late.append(behind(self.shift(corner[half:], "q", k), first))
            side = value[k]
            sides.append(jnp.concatenate([total_of(side[:half], got).astype(bf16), side[half:]]))
        over = jnp.concatenate([over[:half], total_of(over[half:], *late).astype(bf16)])
        return over, sides

    def edges(self, value, over, sides, first=()):
        parts = [self.shift(over, "x", 1)]
        parts += [self.shift(s, "q", k) for k, s in enumerate(sides, 1)]
        parts = behind(parts, first)
        return total_of(value[0], *parts).astype(bf16)

    def column(self, own):
        return total_of(*self.exchange(own))

    def column_near(self, own):
        return total_of(own[0], *(self.shift(own[k], "z", k) for k in range(1, self.z)))

    def groups(self, axes):
        names = ("z", "x", "q", "c")
        rest = [n for n in names if n not in axes]
        out = []
        for fixed in itertools.product(*(range(self.size[n]) for n in rest)):
            at = dict(zip(rest, fixed))
            out.append(
                [
                    self.flat({**at, **dict(zip(axes, v))})
                    for v in itertools.product(*(range(self.size[n]) for n in axes))
                ]
            )
        return out

    def exchange(self, blocks):
        return lax.all_to_all(
            blocks, AXES, 0, 0, axis_index_groups=self.groups(("z",)), tiled=True
        )

    def gather_chips(self, value):
        return lax.all_gather(
            value, AXES, axis=0, axis_index_groups=self.groups(("z", "x", "q")), tiled=True
        )


def total_of(*values):
    return sum(v.astype(f32) for v in values)


def lock(*values):
    return lax.optimization_barrier(values)


def behind(value, *others):
    return lax.optimization_barrier((value, others))[0]


def call(kernel, place, operands, **kw):
    spec = pltpu.PrefetchScalarGridSpec(
        num_scalar_prefetch=1,
        grid=kw.pop("grid"),
        in_specs=kw.pop("in_specs"),
        out_specs=kw.pop("out_specs"),
        scratch_shapes=kw.pop("scratch_shapes", []),
    )
    return pl.pallas_call(
        kernel,
        grid_spec=spec,
        compiler_params=pltpu.CompilerParams(vmem_limit_bytes=kw.pop("mib") * 2**20),
        **kw,
    )(place, *operands)


class Pieces:
    def __init__(self, grid, found):
        self.grid = grid
        self.found = found
        self.arrays = [f[0] for f in found]
        self.count = sum(f[0].shape[0] for f in found)

    def copies(self, place, refs, sem, moves):
        out = []
        for ref, (piece, at_chips) in zip(refs, self.found):
            for i, distance in enumerate(at_chips):
                chip = self.grid.chip(place, *distance)
                for at, rows, col, cols, to in moves:
                    source = ref.at[i, pl.ds(at, rows), pl.ds(col, cols)]
                    out.append(pltpu.make_async_copy(source, to(chip), sem.at[len(out)]))
        return out


class Whole:
    def __init__(self, arrays):
        self.arrays = arrays
        self.count = 1


def pick(grid, found, first, lanes):
    arrays = [f[0][:, first:, :lanes] for f in found]
    rows = arrays[0].shape[1]

    def kernel(place, *refs):
        for ref, (piece, at_chips) in zip(refs[:-1], found):
            for i, distance in enumerate(at_chips):
                refs[-1][grid.chip(place, *distance)] = ref[i]

    return call(
        kernel,
        grid.place,
        arrays,
        grid=(1,),
        in_specs=[pl.BlockSpec(a.shape, lambda i, s: (0, 0, 0)) for a in arrays],
        out_specs=pl.BlockSpec((grid.chips, rows, lanes), lambda i, s: (0, 0, 0)),
        out_shape=jax.ShapeDtypeStruct((grid.chips, rows, lanes), bf16),
        cost_estimate=SMALL,
        mib=8,
        name="pick",
    )


def vectors_kernel(place, small_ref, out_ref):
    rows, width = small_ref.shape[0], out_ref.shape[1]
    chips = rows // 16
    m = lax.broadcasted_iota(jnp.int32, (128, width), 0)
    j = lax.broadcasted_iota(jnp.int32, (128, width), 1)
    small = small_ref[...]
    narrow, wide = width // chips, 2 * width // chips
    spread = lambda n: mm(small, ((j % n) == m).astype(bf16)).reshape(chips, 16, width)
    one = lax.broadcasted_iota(jnp.int32, (chips, 16, width), 2)
    chip = lax.broadcasted_iota(jnp.int32, (chips, 16, width), 0)
    a, b = spread(narrow), spread(wide)
    plain = jnp.sum(jnp.where(one // narrow == chip, a, 0.0), axis=0)
    low = jnp.sum(jnp.where(one // wide == chip, b, 0.0), axis=0)
    high = jnp.sum(jnp.where(one // wide + chips // 2 == chip, b, 0.0), axis=0)
    out_ref[...] = jnp.concatenate(
        [plain[0:6], low[6:7], high[6:7], low[7:8], high[7:8], plain[0:6]], axis=0
    )


def vectors_of(grid, small, width):
    rows = small.shape[0]
    return call(
        vectors_kernel,
        grid.place,
        [small],
        grid=(1,),
        in_specs=[pl.BlockSpec((rows, 128), lambda i, s: (0, 0))],
        out_specs=pl.BlockSpec((16, width), lambda i, s: (0, 0)),
        out_shape=jax.ShapeDtypeStruct((16, width), f32),
        cost_estimate=SMALL,
        mib=8,
        name="vectors",
    )


def first_lanes(head):
    lane = lax.broadcasted_iota(jnp.int32, (1, 2 * HEAD_DIM), 1)
    return lane < HEAD_DIM if head == 0 else lane >= HEAD_DIM


def chunk_of(rows):
    return 1536 if rows % 1536 == 0 else rows


def attn_fwd_kernel(q_ref, k_ref, v_ref, hot_ref, pen_ref, o_ref, ob_ref, lse_ref):
    total_keys = k_ref.shape[0]
    chunk = chunk_of(total_keys)
    steps = total_keys // chunk
    query_rows = q_ref.shape[0]
    query, hot = q_ref[...], hot_ref[...]
    outs = []
    for head in range(2):
        sel = first_lanes(head)
        q_aug = jnp.where(sel, query, hot)

        def scores(rows):
            k_aug = jnp.where(sel, k_ref[rows, :], pen_ref[rows, :])
            return mm(k_aug, q_aug, ((1,), (1,)))

        def weigh(rows, s, top):
            p = jnp.exp2(s - top)
            added = mm(v_ref[rows, :], p.astype(bf16), ((0,), (0,)))
            return jnp.sum(p, axis=0, keepdims=True), added

        if steps == 1:
            s = scores(slice(0, chunk))
            top = jnp.max(s, axis=0, keepdims=True)
            total, acc = weigh(slice(0, chunk), s, top)
        else:

            def step(i, carry):
                top, total, acc = carry
                rows = pl.ds(pl.multiple_of(i * chunk, chunk), chunk)
                s = scores(rows)
                new_top = jnp.maximum(top, jnp.max(s, axis=0, keepdims=True))
                more, added = weigh(rows, s, new_top)
                fade = jnp.exp2(top - new_top)
                return new_top, total * fade + more, acc * fade + added

            top, total, acc = lax.fori_loop(
                0,
                steps,
                step,
                (
                    jnp.full((1, query_rows), -1e30, f32),
                    jnp.zeros((1, query_rows), f32),
                    jnp.zeros((2 * HEAD_DIM, query_rows), f32),
                ),
            )
        outs.append((acc / total)[head * HEAD_DIM : (head + 1) * HEAD_DIM])
        lse_ref[0, head : head + 1, :] = top + jnp.log2(total)
    out = jnp.concatenate(outs, axis=0).T
    o_ref[...] = out
    ob_ref[...] = out.astype(bf16)


def attn_fwd(queries, keys, values, hot, pen, start, pairs):
    rows, width = queries.shape[0], pairs * 128
    total_keys = keys.shape[0]
    pairs = width // 128
    block = 256 if rows % 256 == 0 else rows
    cost = SMALL
    return pl.pallas_call(
        attn_fwd_kernel,
        grid=(pairs, rows // block),
        in_specs=[
            pl.BlockSpec((block, 128), lambda p, i: (i, p + start)),
            pl.BlockSpec((total_keys, 128), lambda p, i: (0, p + start)),
            pl.BlockSpec((total_keys, 128), lambda p, i: (0, p + start)),
            pl.BlockSpec((block, 128), lambda p, i: (i, 0)),
            pl.BlockSpec((total_keys, 128), lambda p, i: (0, 0)),
        ],
        out_specs=[
            pl.BlockSpec((block, 128), lambda p, i: (i, p)),
            pl.BlockSpec((block, 128), lambda p, i: (i, p)),
            pl.BlockSpec((1, 2, block), lambda p, i: (p, 0, i)),
        ],
        out_shape=[
            jax.ShapeDtypeStruct((rows, width), f32),
            jax.ShapeDtypeStruct((rows, width), bf16),
            jax.ShapeDtypeStruct((pairs, 2, rows), f32),
        ],
        compiler_params=pltpu.CompilerParams(vmem_limit_bytes=16 * 2**20),
        cost_estimate=cost,
        name="attn_fwd",
    )(queries, keys, values, hot, pen)


def attn_bwd_kernel(
    q_ref, k_ref, v_ref, hot_ref, pen_ref, o_ref, do_ref, lse_ref, dq_ref, dk_ref, dv_ref, dk_acc, dv_acc
):
    total_keys = k_ref.shape[0]
    chunk = chunk_of(total_keys)
    steps = total_keys // chunk
    at, last = pl.program_id(1), pl.num_programs(1) - 1
    query, hot, grad = q_ref[...], hot_ref[...], do_ref[...]

    @pl.when(at == 0)
    def _():
        dk_acc[...] = jnp.zeros_like(dk_acc)
        dv_acc[...] = jnp.zeros_like(dv_acc)

    flipped = (grad.astype(f32) * o_ref[...]).T
    zero = jnp.zeros_like(query)

    def step(rows):
        keys, values, pen = k_ref[rows, :], v_ref[rows, :], pen_ref[rows, :]
        dq = None
        dk = dk_acc[rows, :]
        dv = dv_acc[rows, :]
        for head in range(2):
            sel = first_lanes(head)
            delta = jnp.sum(
                flipped[head * HEAD_DIM : (head + 1) * HEAD_DIM], axis=0, keepdims=True
            )
            k_aug = jnp.where(sel, keys, pen)
            s = mm(k_aug, jnp.where(sel, query, hot), ((1,), (1,)))
            p = jnp.exp2(s - lse_ref[0, head : head + 1, :])
            grad_h = jnp.where(sel, grad, zero)
            dp = mm(values, grad_h, ((1,), (1,)))
            ds = (p * (dp - delta)).astype(bf16)
            dv = dv + mm(p.astype(bf16), grad_h)
            dk = dk + mm(ds, jnp.where(sel, query, zero))
            part = mm(keys, ds, ((0,), (0,)))
            part = part[head * HEAD_DIM : (head + 1) * HEAD_DIM]
            dq = part if dq is None else jnp.concatenate([dq, part], axis=0)
        dk_acc[rows, :] = dk
        dv_acc[rows, :] = dv
        return dq

    if steps == 1:
        dq = step(slice(0, chunk))
    else:
        dq = lax.fori_loop(
            0,
            steps,
            lambda i, total: total + step(pl.ds(pl.multiple_of(i * chunk, chunk), chunk)),
            jnp.zeros((2 * HEAD_DIM, query.shape[0]), f32),
        )
    dq_ref[...] = (dq.T * HEAD_DIM**-0.5).astype(bf16)

    @pl.when(at == last)
    def _():
        dk_ref[...] = (dk_acc[...] * (1.0 / LOG2E)).astype(bf16)
        dv_ref[...] = dv_acc[...].astype(bf16)


def attn_bwd(queries, keys, values, hot, pen, attended, d_attended, lse, start, pairs):
    rows = queries.shape[0]
    total_keys = keys.shape[0]
    block = 256 if rows % 256 == 0 else rows
    by_query = pl.BlockSpec((block, 128), lambda p, i: (i, p + start))
    own = pl.BlockSpec((block, 128), lambda p, i: (i, p))
    by_key = pl.BlockSpec((total_keys, 128), lambda p, i: (0, p + start))
    to_query = pl.BlockSpec((block, 128), lambda p, i: (i, p))
    to_key = pl.BlockSpec((total_keys, 128), lambda p, i: (0, p))
    width = pairs * 128
    cost = SMALL
    return pl.pallas_call(
        attn_bwd_kernel,
        grid=(pairs, rows // block),
        in_specs=[
            by_query,
            by_key,
            by_key,
            pl.BlockSpec((block, 128), lambda p, i: (i, 0)),
            pl.BlockSpec((total_keys, 128), lambda p, i: (0, 0)),
            own,
            by_query,
            pl.BlockSpec((1, 2, block), lambda p, i: (p, 0, i)),
        ],
        out_specs=[to_query, to_key, to_key],
        out_shape=[
            jax.ShapeDtypeStruct((rows, width), bf16),
            jax.ShapeDtypeStruct((total_keys, width), bf16),
            jax.ShapeDtypeStruct((total_keys, width), bf16),
        ],
        scratch_shapes=[pltpu.VMEM((total_keys, 128), f32), pltpu.VMEM((total_keys, 128), f32)],
        compiler_params=pltpu.CompilerParams(vmem_limit_bytes=24 * 2**20),
        cost_estimate=cost,
        name="attn_bwd",
    )(queries, keys, values, hot, pen, attended, d_attended, lse)


def halves(place, mine, other):
    first = place[3] == 0
    return jnp.where(first, mine, other), jnp.where(first, other, mine)


def load_all(copies):
    for c in copies:
        c.start()
    for c in copies:
        c.wait()


def qkv_kernel(weights, moves, place, n1_ref, vec_ref, *refs):
    pieces, (q_ref, k_ref, v_ref, h1t_ref, w_out, w_s, sem) = refs[:-7], refs[-7:]
    half = q_ref.shape[1]
    width = n1_ref.shape[1]
    step = pl.program_id(0)

    @pl.when(step == 0)
    def _():
        if isinstance(weights, Pieces):
            load_all(weights.copies(place, pieces, sem, moves(w_s)))
        else:
            load_all([pltpu.make_async_copy(pieces[0], w_s.at[0], sem.at[0])])
        w_out[...] = w_s[...]

    h1 = (n1_ref[...] * vec_ref[0:1, :] + vec_ref[1:2, :]).astype(bf16)
    low, high = vec_ref[6:8, :half], vec_ref[6:8, half:]
    bias = jnp.where(place[3] == 0, low, high)
    w = w_s[...].reshape(width, 3 * half)

    @pl.when(step < 2)
    def _():
        q = mm(h1, w[:, :half]) + bias[0:1]
        q_ref[...] = (q * (LOG2E * HEAD_DIM**-0.5)).astype(bf16)

    kv = mm(h1, w[:, half:])
    k_ref[...] = kv[:, :half].astype(bf16)
    v_ref[...] = (kv[:, half:] + bias[1:2]).astype(bf16)
    h1t_ref[...] = h1.T


def project_qkv(grid, n1, vec, weights, local):
    rows, width = n1.shape
    half = width // 2
    if isinstance(weights, Pieces):
        r = width // grid.chips
        moves = lambda w: [(0, r, 0, 3 * half, lambda chip: w.at[chip])]
        shape = (grid.chips, r, 3 * half)
    else:
        moves = None
        shape = (1, width, 3 * half)
    q, k, v, h1t, w = call(
        functools.partial(qkv_kernel, weights, moves),
        grid.place,
        [n1, vec] + weights.arrays,
        grid=(rows // local,),
        in_specs=[
            pl.BlockSpec((local, width), lambda i, s: (i, 0)),
            pl.BlockSpec(vec.shape, lambda i, s: (0, 0)),
        ]
        + [pl.BlockSpec(memory_space=pl.ANY)] * len(weights.arrays),
        out_specs=[
            pl.BlockSpec((local, half), lambda i, s: (jnp.minimum(i, 1), 0)),
            pl.BlockSpec((local, half), lambda i, s: (i, 0)),
            pl.BlockSpec((local, half), lambda i, s: (i, 0)),
            pl.BlockSpec((width, local), lambda i, s: (0, i)),
            pl.BlockSpec(shape, lambda i, s: (0, 0, 0)),
        ],
        out_shape=[
            jax.ShapeDtypeStruct((2 * local, half), bf16),
            jax.ShapeDtypeStruct((rows, half), bf16),
            jax.ShapeDtypeStruct((rows, half), bf16),
            jax.ShapeDtypeStruct((width, rows), bf16),
            jax.ShapeDtypeStruct(shape, bf16),
        ],
        scratch_shapes=[pltpu.VMEM(shape, bf16), pltpu.SemaphoreType.DMA((weights.count,))],
        cost_estimate=SMALL,
        mib=20,
        name="qkv",
    )
    return q, k, v, h1t, w.reshape(width, 3 * half)


def mean_of(v):
    return jnp.mean(v, axis=-1, keepdims=True)


def join(refs):
    return jnp.concatenate([r[...] for r in refs], axis=1)


def out_kernel(n, place, x_ref, w_ref, vec_ref, *refs):
    (after_ref, h2_ref, n2_ref, rstd_ref) = refs[2 * n :]
    a, b = halves(place, join(refs[:n]), join(refs[n : 2 * n]))
    after = x_ref[...].astype(f32) + mm(a, w_ref[0]) + mm(b, w_ref[1]) + vec_ref[2:3, :]
    after_ref[...] = after
    centered = after - mean_of(after)
    rstd = lax.rsqrt(mean_of(centered * centered) + NORM_EPS)
    n2 = centered * rstd
    n2_ref[...] = n2
    rstd_ref[...] = jnp.broadcast_to(rstd, rstd_ref.shape)
    h2_ref[...] = (n2 * vec_ref[3:4, :] + vec_ref[4:5, :]).astype(bf16)


def project_out(grid, x, mine, other, w, vec):
    rows, width = mine[0].shape[0], x.shape[1]
    block = 256 if rows % 256 == 0 else rows
    line = lambda n: pl.BlockSpec((block, n), lambda i, s: (i, 0))
    return call(
        functools.partial(out_kernel, len(mine)),
        grid.place,
        [x, w, vec] + mine + other,
        grid=(rows // block,),
        in_specs=[
            line(width),
            pl.BlockSpec(w.shape, lambda i, s: (0, 0, 0)),
            pl.BlockSpec(vec.shape, lambda i, s: (0, 0)),
        ]
        + [line(v.shape[1]) for v in mine + other],
        out_specs=[line(width), line(width), line(width), line(128)],
        out_shape=[
            jax.ShapeDtypeStruct((rows, width), f32),
            jax.ShapeDtypeStruct((rows, width), bf16),
            jax.ShapeDtypeStruct((rows, width), f32),
            jax.ShapeDtypeStruct((rows, 128), f32),
        ],
        cost_estimate=SMALL,
        mib=16,
        name="out_proj",
    )


def norm_back(grad, normed, rstd, gain):
    e = grad * gain
    return (e - mean_of(e) - normed * mean_of(e * normed)) * rstd


def sum_rows(v):
    return jnp.sum(v, axis=0, keepdims=True)


def out_back_kernel(
    place, mine_ref, got_ref, dy_ref, n2_ref, rstd_ref, vec_ref, w_ref, after_ref, branch_ref, datt_ref, sums_ref
):
    d_h2 = mine_ref[...] + got_ref[...].astype(f32)
    dy = dy_ref[...].astype(f32)
    n2 = n2_ref[...]
    d_after = dy + norm_back(d_h2, n2, rstd_ref[:, 0:1], vec_ref[3:4, :])
    after_ref[...] = d_after
    branch = d_after.astype(bf16)
    branch_ref[...] = branch
    datt_ref[...] = mm(branch, w_ref[0], ((1,), (1,))).astype(bf16)
    rows = [sum_rows(branch.astype(f32)), sum_rows(d_h2 * n2), sum_rows(d_h2), sum_rows(dy)]
    sums = jnp.concatenate(rows + [jnp.zeros((4, dy.shape[1]), f32)], axis=0) * 0.5

    @pl.when(pl.program_id(0) == 0)
    def _():
        sums_ref[...] = jnp.zeros_like(sums_ref)

    sums_ref[...] += sums


def out_back(grid, mine, got, dy, n2, rstd, vec, w):
    rows, width = mine.shape
    block = 256 if rows % 256 == 0 else rows
    line = lambda n: pl.BlockSpec((block, n), lambda i, s: (i, 0))
    return call(
        out_back_kernel,
        grid.place,
        [mine, got, dy, n2, rstd, vec, w],
        grid=(rows // block,),
        in_specs=[
            line(width),
            line(width),
            line(width),
            line(width),
            line(128),
            pl.BlockSpec(vec.shape, lambda i, s: (0, 0)),
            pl.BlockSpec((1,) + w.shape[1:], lambda i, s: (s[3], 0, 0)),
        ],
        out_specs=[
            line(width),
            line(width),
            line(width // 2),
            pl.BlockSpec((8, width), lambda i, s: (0, 0)),
        ],
        out_shape=[
            jax.ShapeDtypeStruct((rows, width), f32),
            jax.ShapeDtypeStruct((rows, width), bf16),
            jax.ShapeDtypeStruct((rows, width // 2), bf16),
            jax.ShapeDtypeStruct((8, width), f32),
        ],
        cost_estimate=SMALL,
        mib=20,
        name="out_back",
    )


def store_rows(grid, place, ref, value, first, shard, to, tail=()):
    for i in range(value.shape[0] // shard):
        column, z = grid.relative(place, first + i, True)
        at = (column, z) + tail + (pl.ds(to, shard),) + (slice(None),)
        ref[at] = value[i * shard : (i + 1) * shard]


def out_grad_kernel(grid, fast, n, place, d_ref, *refs):
    g_ref = refs[-1]
    parts = halves(place, join(refs[:n]), join(refs[n : 2 * n]))
    for i, part in enumerate(parts):
        g = mm(part, d_ref[...], ((0,), (0,))).astype(bf16)
        if fast:
            shard = 2 * g.shape[0] // grid.chips
            store_rows(grid, place, g_ref, g, i * g.shape[0] // shard, shard, 0)
        else:
            g_ref[i] = g


def out_gradient(grid, fast, mine, other, branch):
    rows, half = branch.shape[0], branch.shape[1] // 2
    shape = (2 * grid.q, grid.z, 2 * half // grid.chips, half) if fast else (2, half, half)
    return call(
        functools.partial(out_grad_kernel, grid, fast, len(mine)),
        grid.place,
        [branch] + mine + other,
        grid=(1,),
        in_specs=[pl.BlockSpec((rows, half), lambda i, s: (0, s[3]))]
        + [pl.BlockSpec(v.shape, lambda i, s: (0, 0)) for v in mine + other],
        out_specs=pl.BlockSpec(shape, lambda i, s: (0,) * len(shape)),
        out_shape=jax.ShapeDtypeStruct(shape, bf16),
        cost_estimate=SMALL,
        mib=8,
        name="w_out_grad",
    )


def vector_rows(chips, sums1, sums2, ups):
    width = sums1.shape[1]
    narrow, wide = width // chips, 2 * width // chips
    plain = jnp.concatenate([sums1[0:2], sums2[0:4], sums1[0:2]], axis=0)

    def fold(value, n, chip):
        lane = lax.broadcasted_iota(jnp.int32, (chips, 8, width), 2)
        value = jnp.where(lane // n == chip, value, 0.0).reshape(chips * 8, width)
        m = lax.broadcasted_iota(jnp.int32, (width, 128), 1)
        j = lax.broadcasted_iota(jnp.int32, (width, 128), 0)
        return mm(value.astype(bf16), (j % n == m).astype(bf16)).reshape(chips, 8, 128)

    chip = lax.broadcasted_iota(jnp.int32, (chips, 8, width), 0)
    a = fold(jnp.broadcast_to(plain[None], (chips, 8, width)), narrow, chip)
    low = jnp.concatenate([sums1[2:3], ups[0:1]] * 4, axis=0)
    high = jnp.concatenate([sums1[3:4], ups[1:2]] * 4, axis=0)
    both = jnp.where(chip < chips // 2, low[None], high[None])
    b = fold(both, wide, chip % (chips // 2))
    row = lax.broadcasted_iota(jnp.int32, (chips, 8, 128), 1)
    return jnp.where(row < 6, a, b).astype(bf16)


def qkv_grad_kernel(grid, fast, pairs, more, place, h1t_ref, dq_ref, dk_ref, dv_ref, *refs):
    g_ref = refs[-1]
    chip_rows = dq_ref.shape[0]
    if more:
        rows = vector_rows(grid.chips, *(r[...] for r in refs[:-1]))
        shard = h1t_ref.shape[0] // grid.chips
        rows = jnp.concatenate([rows, jnp.zeros_like(rows)], axis=1)
        for i in range(grid.chips):
            column, z = grid.relative(place, i, True)
            g_ref[column, z, 0, pl.ds(shard, 16), 0:128] = rows[i]
            g_ref[column, z, 0, pl.ds(shard, 16), 128:384] = jnp.zeros((16, 256), bf16)
    for p in range(pairs):
        cols = slice(p * 128, (p + 1) * 128)
        gq = mm(h1t_ref[:, :chip_rows], dq_ref[:, cols])
        gk = mm(h1t_ref[...], dk_ref[:, cols])
        gv = mm(h1t_ref[...], dv_ref[:, cols])
        g = jnp.concatenate([gq, gk, gv], axis=1).astype(bf16)
        if fast:
            store_rows(grid, place, g_ref, g, 0, g.shape[0] // grid.chips, 0, (p,))
        else:
            g_ref[p] = g


def qkv_gradient(grid, fast, h1t, dq, dk, dv, *more):
    width, rows = h1t.shape
    pairs = dq.shape[1] // 128
    if fast:
        shape = (2 * grid.q, grid.z, pairs, width // grid.chips + (16 if more else 0), 384)
    else:
        shape = (pairs, width, 384)
    whole = lambda v: pl.BlockSpec(v.shape, lambda i, s: (0, 0))
    return call(
        functools.partial(qkv_grad_kernel, grid, fast, pairs, len(more)),
        grid.place,
        [h1t, dq, dk, dv] + list(more),
        grid=(1,),
        in_specs=[whole(v) for v in (h1t, dq, dk, dv) + more],
        out_specs=pl.BlockSpec(shape, lambda i, s: (0,) * len(shape)),
        out_shape=jax.ShapeDtypeStruct(shape, bf16),
        cost_estimate=SMALL,
        mib=16,
        name="w_qkv_grad",
    )


def input_back_kernel(parts, place, *refs):
    grads, (w_ref, n1_ref, mine_ref, other_ref, sums_ref) = refs[: 3 * parts], refs[3 * parts :]
    step = pl.program_id(0)
    dq, dk, dv = (
        jnp.concatenate([grads[3 * p + i][...] for p in range(parts)], axis=1) for i in range(3)
    )
    half = dq.shape[1]
    width = n1_ref.shape[1]
    dq = jnp.where(step < 2, dq, jnp.zeros_like(dq))
    d = mm(jnp.concatenate([dq, dk, dv], axis=1), w_ref[...], ((1,), (1,)))
    block, core = step // 2, step % 2

    @pl.when(core == place[3])
    def _():
        mine_ref[block] = d

    @pl.when(core != place[3])
    def _():
        other_ref[block] = d.astype(bf16)

    none = jnp.zeros((1, half), f32)

    def spread(v):
        v = sum_rows(v.astype(f32))
        first = place[3] == 0
        return jnp.concatenate([jnp.where(first, v, none), jnp.where(first, none, v)], axis=1)

    rows = [sum_rows(d * n1_ref[...]), sum_rows(d), spread(dq), spread(dv)]
    sums = jnp.concatenate(rows + [jnp.zeros((4, width), f32)], axis=0)

    @pl.when(step == 0)
    def _():
        sums_ref[...] = jnp.zeros_like(sums_ref)

    sums_ref[...] += sums


def input_back(grid, grads, w, n1, local):
    rows, width = n1.shape
    flat = [g for part in grads for g in part]
    specs = []
    for dq, dk, dv in grads:
        n = dq.shape[1]
        specs.append(pl.BlockSpec((local, n), lambda i, s: (jnp.minimum(i, 1), 0)))
        specs += [pl.BlockSpec((local, n), lambda i, s: (i, 0))] * 2
    shape = (grid.q, local, width)
    return call(
        functools.partial(input_back_kernel, len(grads)),
        grid.place,
        flat + [w, n1],
        grid=(rows // local,),
        in_specs=specs
        + [
            pl.BlockSpec(w.shape, lambda i, s: (0, 0)),
            pl.BlockSpec((local, width), lambda i, s: (i, 0)),
        ],
        out_specs=[
            pl.BlockSpec(shape, lambda i, s: (0, 0, 0)),
            pl.BlockSpec(shape, lambda i, s: (0, 0, 0)),
            pl.BlockSpec((8, width), lambda i, s: (0, 0)),
        ],
        out_shape=[
            jax.ShapeDtypeStruct(shape, f32),
            jax.ShapeDtypeStruct(shape, bf16),
            jax.ShapeDtypeStruct((8, width), f32),
        ],
        cost_estimate=SMALL,
        mib=24,
        name="input_back",
    )


def finish_kernel(n_got, place, *refs):
    mine_ref, got_ref = refs[:2]
    sides = refs[2 : 2 + n_got]
    n1_ref, rstd_ref, after_ref, vec_ref, out_ref = refs[2 + n_got :]
    d = mine_ref[0] + got_ref[0].astype(f32)
    for s in sides:
        d = d + s[...].astype(f32)
    out_ref[...] = after_ref[...] + norm_back(d, n1_ref[...], rstd_ref[...], vec_ref[0:1, :])


def finish(grid, mine, got, sides, n1, rstd1, d_after, vec):
    _, rows, width = mine.shape
    first = pl.BlockSpec((1, rows, width), lambda i, s: (0, 0, 0))
    own = lambda n: pl.BlockSpec((rows, n), lambda i, s: (s[3], 0))
    return call(
        functools.partial(finish_kernel, len(sides)),
        grid.place,
        [mine, got] + sides + [n1, rstd1, d_after, vec],
        grid=(1,),
        in_specs=[first, first]
        + [pl.BlockSpec((rows, width), lambda i, s: (0, 0))] * len(sides)
        + [own(width), own(1), own(width), pl.BlockSpec(vec.shape, lambda i, s: (0, 0))],
        out_specs=pl.BlockSpec((rows, width), lambda i, s: (0, 0)),
        out_shape=jax.ShapeDtypeStruct((rows, width), f32),
        cost_estimate=SMALL,
        mib=20,
        name="finish",
    )


def ff_kernel(grid, ups, downs, place, h2_ref, dy_ref, vec_ref, *refs):
    fast = isinstance(ups, Pieces)
    n_up, n = len(ups.arrays), len(ups.arrays) + len(downs.arrays)
    pieces, refs = refs[:n], refs[n:]
    if fast:
        g_ref, refs = refs[0], refs[1:]
    else:
        (gdown_ref, gup_ref), refs = refs[:2], refs[2:]
    gbias_ref, out_ref, dh_ref, dhb_ref, act_s, dhid_s, h2t_s, up_s, down_s, sem, down_sem = refs
    step = pl.program_id(0)
    rows, width = h2_ref.shape
    units = act_s.shape[1]
    part = 256 if rows % 256 == 0 else rows

    @pl.when(step == 0)
    def _():
        if fast:
            r = up_s.shape[2]
            copies = ups.copies(
                place,
                pieces[:n_up],
                sem,
                [
                    (0, r, 0, width, lambda chip: up_s.at[0, chip]),
                    (r, r, 0, width, lambda chip: up_s.at[1, chip]),
                ],
            )
        else:
            tile = pl.ds(0, units), pl.ds(units, units)
            copies = [
                pltpu.make_async_copy(pieces[0].at[:, tile[i]], up_s.at[i, 0], sem.at[i])
                for i in range(2)
            ]
        copies.append(pltpu.make_async_copy(pieces[n_up], down_s, down_sem.at[0]))
        for c in copies:
            c.start()
        h2t_s[...] = h2_ref[...].T
        for c in copies:
            c.wait()

    w_up = up_s[step].reshape(width, units)
    d = down_s.shape[0] // 2
    w_down = down_s[pl.ds(step * d, d)]
    bias = jnp.where(step == 0, vec_ref[8:9, :], vec_ref[9:10, :])
    for at in range(0, rows, part):
        here = slice(at, at + part)
        for col in range(0, units, 256):
            cols = slice(col, col + 256)
            hidden = mm(h2_ref[here, :], w_up[:, cols]) + bias[:, cols]
            phi = 0.5 * (1.0 + lax.erf(hidden * (0.5**0.5)))
            dens = jnp.exp(-0.5 * hidden * hidden) * (1.0 / math.sqrt(2.0 * math.pi))
            act_s[here, cols] = (hidden * phi).astype(bf16)
            d_act = mm(dy_ref[here, :], w_down[cols, :], ((1,), (1,)))
            dhid_s[here, cols] = (d_act * (phi + hidden * dens)).astype(bf16)
    act, d_hidden = act_s[...], dhid_s[...]
    gdown = mm(act, dy_ref[...], ((0,), (0,))).astype(bf16)
    gup = mm(h2t_s[...], d_hidden).astype(bf16)
    gbias_ref[0] = sum_rows(d_hidden.astype(f32))
    out = mm(act, w_down)
    dh = mm(d_hidden, w_up, ((1,), (1,)))
    if fast:
        down_shard = 2 * units // grid.chips
        up_shard = width // grid.chips
        half = grid.chips // 2
        for i in range(half):
            column, z = grid.relative(place, step * half + i)
            g_ref[column, z, 0:down_shard, :] = gdown[i * down_shard : (i + 1) * down_shard]
        for i in range(grid.chips):
            column, z = grid.relative(place, i)
            to = pl.multiple_of(down_shard + step * up_shard, 16)
            g_ref[column, z, pl.ds(to, up_shard), :] = gup[i * up_shard : (i + 1) * up_shard]
    else:
        gdown_ref[...] = gdown
        gup_ref[...] = gup

    @pl.when(step == 0)
    def _():
        out_ref[...] = out
        dh_ref[...] = dh

    @pl.when(step == 1)
    def _():
        out_ref[...] += out
        total = dh_ref[...] + dh
        dh_ref[...] = total
        dhb_ref[...] = total.astype(bf16)


def feed_forward(grid, h2, dy, ups, downs, vec, units):
    fast = isinstance(ups, Pieces)
    rows, width = h2.shape
    tile = units // 2
    chips = grid.chips
    whole = pl.BlockSpec((rows, width), lambda j, s: (0, 0))
    cols = pl.BlockSpec((width, tile), lambda j, s: (0, j))
    lines = pl.BlockSpec((tile, width), lambda j, s: (j, 0))
    if fast:
        shape = (2 * grid.q, grid.z, (units + width * 2) // chips, width)
        g_specs = [pl.BlockSpec(shape, lambda j, s: (0, 0, 0, 0))]
        g_shapes = [jax.ShapeDtypeStruct(shape, bf16)]
        up_shape = (2, chips, width // chips, tile)
    else:
        g_specs = [lines, cols]
        g_shapes = [
            jax.ShapeDtypeStruct((units, width), bf16),
            jax.ShapeDtypeStruct((width, units), bf16),
        ]
        up_shape = (2, 1, width, tile)
    return call(
        functools.partial(ff_kernel, grid, ups, downs),
        grid.place,
        [h2, dy, vec] + ups.arrays + downs.arrays,
        grid=(2,),
        in_specs=[whole, whole, pl.BlockSpec(vec.shape, lambda j, s: (0, 0))]
        + [pl.BlockSpec(memory_space=pl.ANY)] * len(ups.arrays + downs.arrays),
        out_specs=g_specs
        + [pl.BlockSpec((1, 1, tile), lambda j, s: (j, 0, 0)), whole, whole, whole],
        out_shape=g_shapes
        + [
            jax.ShapeDtypeStruct((2, 1, tile), f32),
            jax.ShapeDtypeStruct((rows, width), f32),
            jax.ShapeDtypeStruct((rows, width), f32),
            jax.ShapeDtypeStruct((rows, width), bf16),
        ],
        scratch_shapes=[
            pltpu.VMEM((rows, tile), bf16),
            pltpu.VMEM((rows, tile), bf16),
            pltpu.VMEM((width, rows), bf16),
            pltpu.VMEM(up_shape, bf16),
            pltpu.VMEM((units, width), bf16),
            pltpu.SemaphoreType.DMA((2 * ups.count,)),
            pltpu.SemaphoreType.DMA((downs.count,)),
        ],
        cost_estimate=SMALL,
        mib=40,
        name="feed_forward",
    )


def in_order(first, mine, other):
    return jnp.stack([jnp.where(first, mine, other), jnp.where(first, other, mine)])


def body(
    dp,
    blk,
    inputs,
    clip_ids,
    ln1_gain,
    ln1_bias,
    w_qkv,
    qv_bias,
    w_out,
    out_bias,
    ln2_gain,
    ln2_bias,
    w_up,
    up_bias,
    w_down,
    down_bias,
    out_grad,
):
    grid = Grid(dp, blk)
    core = grid.me["c"]
    first = core == 0
    chips = grid.chips
    width = inputs.shape[2]
    half = width // 2
    local = inputs.shape[1]
    chip_rows = 2 * local
    units = w_up.shape[1] // 2
    shard = w_qkv.shape[0]
    per_chip = units // chips
    fast = shard % 8 == 0 and per_chip % 16 == 0
    swap = lambda v: grid.shift(v, "c", 1)
    at_core = lambda v, dim=0: lax.dynamic_index_in_dim(v, core, dim, keepdims=False)
    not_core = lambda v, dim=0: lax.dynamic_index_in_dim(v, 1 - core, dim, keepdims=False)

    pad = jnp.zeros((16, width), bf16).at[0, :local].set(clip_ids[0].astype(bf16))
    mine = jnp.concatenate([inputs[0], pad], axis=0)
    dy_mine = out_grad[0]
    if fast:
        put = lambda v, n: jnp.zeros((128,), bf16).at[:n].set(v)
        place_at = lambda v: jnp.where(first, jnp.pad(v, (0, v.size)), jnp.pad(v, (v.size, 0)))
        vecs = [ln1_gain, ln1_bias, out_bias, ln2_gain, ln2_bias, down_bias, qv_bias]
        rows = jnp.stack([jnp.pad(place_at(v), (0, 128 - 2 * v.size)) for v in vecs])
        up_row = put(up_bias, per_chip)[None]
        blank = jnp.zeros((8, 128), bf16)
        mine_small = jnp.concatenate([rows, up_row, blank])
        their_small = jnp.concatenate([rows, jnp.zeros_like(up_row), blank])
        widen = lambda v: jnp.pad(v, ((0, 0), (0, 3 * half - 128)))
        split = w_qkv.reshape(shard, 3, 2, half)
        my_qkv = at_core(split, 2).reshape(shard, 3 * half)
        to_qkv = not_core(split, 2).reshape(shard, 3 * half)
        up_split = w_up.reshape(shard, chips, 2, per_chip)
        out_split = w_out.reshape(shard, 2, half)
        my_up = at_core(up_split, 2).reshape(shard, units)
        to_up = not_core(up_split, 2).reshape(shard, units)
        my_out, to_out = at_core(out_split, 1), not_core(out_split, 1)
        got = swap(jnp.concatenate([to_qkv, widen(their_small)]))
        pair = in_order(first, my_qkv, got[:shard])
        small_chip = mine_small + got[shard:, :128]
        qkv_piece = jnp.concatenate([pair.reshape(2 * shard, 3 * half), widen(small_chip)])

        full_down = grid.gather_chips(w_down)
        downs = Whole([full_down])
        qkv_piece, x_sent = lock(qkv_piece, mine)
        qkv_z = grid.along(qkv_piece, "z")
        x_far = grid.along(x_sent, "q")
        x_near = swap(x_sent)
        got = swap(jnp.concatenate([to_up, to_out], axis=1))
        up_pair = in_order(first, my_up, got[:, :units]).reshape(2 * shard, units)
        up_piece = jnp.concatenate([up_pair[:, :width], up_pair[:, width:]])
        out_piece = in_order(first, my_out, got[:, units:]).reshape(2 * shard, half)
        cut = 2 * shard * 2 // 3 // 16 * 16
        low = jnp.pad(out_piece[cut:], ((0, 2 * cut - 2 * shard), (0, 0)))
        up_piece = jnp.concatenate([up_piece, jnp.concatenate([out_piece[:cut], low], axis=1)])

        qkv_z, x_far, x_near, up_piece = lock(qkv_z, x_far, x_near, up_piece)
        qkv_line = grid.line(qkv_piece, qkv_z)
        qkv_over, qkv_sides = grid.shift(qkv_line, "x", 1), grid.along(qkv_line, "q")
        up_line = grid.exchange(jnp.broadcast_to(up_piece, (grid.z,) + up_piece.shape))
        x_both = [(mine, x_near)] + [(v, swap(v)) for v in x_far]
        dy_near = swap(dy_mine)

        qkv_over, qkv_sides, x_both, dy_near = lock(qkv_over, qkv_sides, x_both, dy_near)
        found = grid.found(
            qkv_line, qkv_over, qkv_sides, grid.corner_pieces(qkv_over, qkv_sides)
        )
        qkv_weights = Pieces(grid, found)
        small_all = pick(grid, found, 2 * shard, 128)
        vec = vectors_of(grid, small_all.reshape(chips * 16, 128), width)
    else:
        whole = lambda v: lax.all_gather(v, AXES, axis=0, tiled=True)
        full_qkv = at_core(whole(w_qkv).reshape(width, 3, 2, half), 2).reshape(width, 3 * half)
        qkv_weights = Whole([full_qkv])
        full_out = whole(w_out)
        full_up = at_core(whole(w_up).reshape(width, chips, 2, per_chip), 2).reshape(width, units)
        full_down = at_core(whole(w_down).reshape(chips, 2, per_chip, width), 1).reshape(
            units, width
        )
        ups, downs = Whole([full_up]), Whole([full_down])
        up_all = at_core(whole(up_bias).reshape(chips, 2, per_chip), 1).reshape(2, width)
        singles = [ln1_gain, ln1_bias, out_bias, ln2_gain, ln2_bias, down_bias]
        vec = jnp.concatenate(
            [whole(v)[None] for v in singles]
            + [whole(qv_bias).reshape(2, width), up_all, jnp.zeros((6, width), bf16)]
        ).astype(f32)
        x_both = [(v, swap(v)) for v in [mine] + grid.along(mine, "q")]
        dy_near = swap(dy_mine)

    both = [in_order(first, *v) for v in x_both]
    token_rows = jnp.concatenate([b[:, :local].reshape(chip_rows, width) for b in both])
    clips = jnp.concatenate([b[:, local, :local].reshape(chip_rows) for b in both])
    x_all = token_rows.astype(f32)
    centered = x_all - mean_of(x_all)
    rstd1 = lax.rsqrt(mean_of(centered * centered) + NORM_EPS)
    n1 = centered * rstd1
    lane = lax.broadcasted_iota(jnp.int32, (1, 128), 1) % HEAD_DIM
    same = clips[:, None].astype(jnp.int32) == lane
    hot = same[:chip_rows].astype(bf16)
    pen = jnp.where(same | (lane >= 8), 0.0, -1e30).astype(bf16)
    dy = in_order(first, dy_mine, dy_near).reshape(chip_rows, width)

    queries, keys, values, h1t, full_qkv = project_qkv(grid, n1, vec, qkv_weights, local)
    pairs = half // 128
    forward = lambda q, a, n: attn_fwd(q, keys, values, hot, pen, a, n)
    if fast:
        queries, up_line = lock(queries, up_line)
        up_over, up_sides = grid.shift(up_line, "x", 1), grid.along(up_line, "q")
    parts = [forward(queries, 0, pairs - 1)]
    if fast:
        up_over, up_sides = behind((up_over, up_sides), parts[0])
        queries = behind(queries, up_over, up_sides)
        corners = grid.corner_pieces(up_over, up_sides)
        found = grid.found(up_line, up_over, up_sides, corners, True)
        ups = Pieces(grid, found)
        out_all = pick(grid, found, 4 * shard, width)
        low = out_all[:, : 2 * shard - cut, half:]
        out_cols = jnp.concatenate([out_all[:, :, :half], low], axis=1).reshape(width, half)
        full_out = jnp.concatenate(list(in_order(first, out_cols, swap(out_cols))), axis=1)
    parts.append(forward(queries, pairs - 1, 1))
    att_mine = [p[1] for p in parts]
    att_other = [swap(v) for v in att_mine]
    out_rows = full_out.reshape(2, half, width)
    after, h2, n2, rstd2 = project_out(grid, token_rows, att_mine, att_other, out_rows, vec)

    *g_ff, gbias, ff_out, dh, dh_b = feed_forward(grid, h2, dy, ups, downs, vec, units)
    d_after, d_branch, d_att, sums2 = out_back(grid, dh, swap(dh_b), dy, n2, rstd2, vec, out_rows)
    g_out = out_gradient(grid, fast, att_mine, att_other, d_branch)

    def back(d, i):
        att, _, lse = parts[i]
        start = i * (pairs - 1)
        return attn_bwd(queries, keys, values, hot, pen, att, d, lse, start, att.shape[1] // 128)

    by_core = lambda v: v.reshape(2, local, width)
    up_sums = gbias.reshape(2, width)
    if fast:
        ff_over, ff_sides = grid.corners(g_ff[0], (d_att, g_out))
        d_att = behind(d_att, ff_over, ff_sides)
    grads = [back(d_att, 0)]
    g_first = qkv_gradient(grid, fast, h1t, *grads[0])
    if fast:
        g_first = jnp.concatenate([g_first, g_out[:, :, None]], axis=2)
    d_att, g_first = lock(d_att, g_first)
    grads.append(back(d_att, 1))
    if fast:
        first_over, first_sides = grid.corners(g_first, grads[1])
        ff_own = grid.edges(g_ff[0], ff_over, ff_sides, grads[1])
        grads, ff_own, first_over, first_sides = lock(grads, ff_own, first_over, first_sides)
    d_mine, d_other, sums1 = input_back(grid, grads, full_qkv, n1, local)
    d_got = swap(d_other)
    if fast:
        g_last = qkv_gradient(grid, fast, h1t, *grads[1], sums1, sums2, up_sums)
        ff = grid.column(ff_own)
    else:
        g_last = qkv_gradient(grid, fast, h1t, *grads[1])
    sent = [
        (d_mine[k] + d_got[k].astype(f32)).astype(bf16) for k in range(1, grid.q)
    ]
    if fast:
        first_own = grid.edges(g_first, first_over, first_sides, g_last)
        sent, g_last, first_own = lock(sent, g_last, first_own)
    got = [grid.shift(s, "q", grid.q - k) for k, s in enumerate(sent, 1)]
    ff_out = behind(ff_out, sent)
    out_got = swap(not_core(by_core(ff_out)).astype(bf16)).astype(f32)
    result = at_core(by_core(ff_out)) + out_got + at_core(by_core(after)) + vec[5:6]
    output = result.astype(bf16)[None]
    input_grad = finish(grid, d_mine, d_got, got, n1, rstd1, d_after, vec)[None]

    if fast:
        last_over, last_sides = grid.corners(g_last)
        last_own = grid.edges(g_last, last_over, last_sides, ff)
        g_first, g_last = grid.column_near(first_own), grid.column_near(last_own)
        mine, g_last = g_last[:, 2 * shard :, :128], g_last[:, : 2 * shard]
        w_down_g = ff[:per_chip]
        up_chip = ff[per_chip:].reshape(2, 2, shard, width)
        up_other = swap(not_core(up_chip, 1).astype(bf16)).astype(f32)
        up_both = in_order(first, at_core(up_chip, 1), up_other)
        w_up_g = jnp.transpose(
            up_both.reshape(2, 2, shard, chips // 2, per_chip), (2, 1, 3, 0, 4)
        ).reshape(shard, 2 * units)

        def across(v):
            v = v.reshape(v.shape[0], 2, shard, half)
            other = swap(not_core(v, 1).astype(bf16)).astype(f32)
            return in_order(first, at_core(v, 1), other)

        g_first, g_last = across(g_first), across(g_last)
        early = pairs - 1
        w_out_g = jnp.concatenate([g_first[0, early], g_first[1, early]], axis=1)
        per_pair = jnp.concatenate([g_first[:, :early], g_last], axis=1)
        per_pair = per_pair.reshape(2, pairs, shard, 3, 128)
        w_qkv_g = jnp.transpose(per_pair, (2, 3, 0, 1, 4)).reshape(shard, 6 * half)
        mine = mine[0, :8]
        summed = mine + swap(mine.astype(bf16)).astype(f32)
        cut = lambda n: jnp.where(first, summed[:, :n], summed[:, n : 2 * n])
        six, qv_g, up_g = cut(shard)[:6], cut(2 * shard)[6], mine[7, :per_chip]
    else:
        reduce = lambda v: lax.psum_scatter(v, AXES, scatter_dimension=0, tiled=True)

        def spread(v, dim):
            v = v.astype(f32)
            zero = jnp.zeros_like(v)
            return jnp.stack([jnp.where(first, v, zero), jnp.where(first, zero, v)], axis=dim)

        gdown, gup = g_ff
        w_down_g = reduce(
            spread(gdown.reshape(chips, per_chip, width), 1).reshape(2 * units, width)
        )
        w_up_g = reduce(spread(gup.reshape(width, chips, per_chip), 2).reshape(width, 2 * units))
        w_out_g = reduce(spread(g_out.reshape(width, half), 1).reshape(width, width))
        per_pair = jnp.concatenate([g_first, g_last]).reshape(pairs, width, 3, 128)
        per_pair = jnp.transpose(per_pair, (1, 2, 0, 3)).reshape(width, 3, half)
        w_qkv_g = reduce(spread(per_pair, 2).reshape(width, 6 * half))
        nothing = jnp.zeros_like(up_sums)
        sums = jnp.concatenate(
            [
                sums1[0:2],
                sums2[0:4],
                sums1[2:4],
                jnp.where(first, up_sums, nothing),
                jnp.where(first, nothing, up_sums),
            ]
        )
        sums = lax.psum(sums, AXES)
        me = (lax.axis_index("dp") * blk) + lax.axis_index("blk")
        six = lax.dynamic_slice(sums, (0, me * shard), (6, shard))
        qv_g = lax.dynamic_slice(sums[6:8].reshape(2 * width), (me * 2 * shard,), (2 * shard,))
        up_g = at_core(sums[8:12].reshape(2, units))
        up_g = lax.dynamic_slice(up_g, (me // 2 * per_chip,), (per_chip,))

    return (
        output,
        input_grad,
        six[0],
        six[1],
        w_qkv_g,
        qv_g,
        w_out_g,
        six[2],
        six[3],
        six[4],
        w_up_g,
        up_g,
        w_down_g,
        six[5],
    )


def solution(mesh):
    both = P(("dp", "blk"))
    rows = P(("dp", "blk"), None)
    tokens = P("dp", "blk", None)
    return jax.shard_map(
        functools.partial(body, mesh.shape["dp"], mesh.shape["blk"]),
        mesh=mesh,
        in_specs=(
            tokens,
            P("dp", "blk"),
            both,
            both,
            rows,
            both,
            rows,
            both,
            both,
            both,
            rows,
            both,
            rows,
            both,
            tokens,
        ),
        out_specs=(
            tokens,
            tokens,
            both,
            both,
            rows,
            both,
            rows,
            both,
            both,
            both,
            rows,
            both,
            rows,
            both,
        ),
        check_vma=False,
    )
```

```python
import functools
import itertools
import math

import jax
import jax.numpy as jnp
from jax import lax
from jax.experimental import pallas as pl
from jax.experimental.pallas import tpu as pltpu
from jax.sharding import PartitionSpec as P

HEAD_DIM = 64
NORM_EPS = 1e-06
LOG2E = math.log2(math.e)
f32 = jnp.float32
bf16 = jnp.bfloat16
AXES = ("dp", "blk")


def mm(a, b, dims=((1,), (0,))):
    return lax.dot_general(a, b, (dims, ((), ())), preferred_element_type=f32)


SMALL = pl.CostEstimate(flops=1000, bytes_accessed=1000, transcendentals=0)


class Grid:
    def __init__(self, dp, blk):
        self.size = {"z": dp // 2, "x": 2, "q": blk // 2, "c": 2}
        self.z, self.x, self.q = dp // 2, 2, blk // 2
        self.chips = self.z * 2 * self.q
        me_dp, me_blk = lax.axis_index("dp"), lax.axis_index("blk")
        self.me = {"z": me_dp // 2, "x": me_dp % 2, "q": me_blk // 2, "c": me_blk % 2}
        self.place = jnp.stack([self.me[a] for a in ("z", "x", "q", "c")]).astype(jnp.int32)

    def flat(self, at):
        return ((at["z"] * self.x + at["x"]) * self.q + at["q"]) * 2 + at["c"]

    def shift(self, value, axis, step):
        pairs = []
        for z in range(self.z):
            for x in range(self.x):
                for q in range(self.q):
                    for c in range(2):
                        at = {"z": z, "x": x, "q": q, "c": c}
                        to = dict(at)
                        to[axis] = (at[axis] + step) % self.size[axis]
                        pairs.append((self.flat(at), self.flat(to)))
        return lax.ppermute(value, AXES, pairs)

    def chip(self, place, dz, dx, dq):
        z = -1 - dz if dz < 0 else lax.rem(place[0] + (self.z - dz), self.z)
        x = lax.rem(place[1] + (self.x - dx), self.x)
        q = lax.rem(place[2] + (self.q - dq), self.q)
        return (z * self.x + x) * self.q + q

    def relative(self, place, chip, near=False):
        z, x, q = chip // (self.x * self.q), chip // self.q % self.x, chip % self.q
        dx = lax.rem(x + self.x - place[1], self.x)
        dq = lax.rem(q + self.q - place[2], self.q)
        if near:
            z = lax.rem(z + self.z - place[0], self.z)
        return dx * self.q + dq, z

    def along(self, value, axis):
        return [self.shift(value, axis, k) for k in range(1, self.size[axis])]

    def line(self, value, others):
        return jnp.stack([value] + others)

    def corner_pieces(self, over, sides):
        half = self.z // 2
        return [
            (self.shift(over[:half], "q", k), self.shift(side[half:], "x", 1))
            for k, side in enumerate(sides, 1)
        ]

    def found(self, line, over, sides, corners, plain=False):
        half = self.z // 2
        zs = [-1 - z if plain else z for z in range(self.z)]
        out = [(line, [(z, 0, 0) for z in zs]), (over, [(z, 1, 0) for z in zs])]
        for k, (side, (a, b)) in enumerate(zip(sides, corners), 1):
            out.append((side, [(z, 0, k) for z in zs]))
            out.append((a, [(z, 1, k) for z in zs[:half]]))
            out.append((b, [(z, 1, k) for z in zs[half:]]))
        return out

    def found_last(self, plane, others):
        at = [(x, q) for x in range(2) for q in range(self.q)]
        return [(p, [(z, x, q) for x, q in at]) for z, p in enumerate([plane] + others)]


    def corners(self, value, first=()):
        half = self.z // 2
        over = value[self.q]
        late, sides = [], []
        for k in range(1, self.q):
            corner = value[self.q + k]
            got = behind(self.shift(corner[:half], "x", 1), first)
            late.append(behind(self.shift(corner[half:], "q", k), first))
            side = value[k]
            sides.append(jnp.concatenate([total_of(side[:half], got).astype(bf16), side[half:]]))
        over = jnp.concatenate([over[:half], total_of(over[half:], *late).astype(bf16)])
        return over, sides

    def edges(self, value, over, sides, first=()):
        parts = [self.shift(over, "x", 1)]
        parts += [self.shift(s, "q", k) for k, s in enumerate(sides, 1)]
        parts = behind(parts, first)
        return total_of(value[0], *parts).astype(bf16)

    def column(self, own):
        return total_of(*self.exchange(own))

    def column_near(self, own):
        return total_of(own[0], *(self.shift(own[k], "z", k) for k in range(1, self.z)))

    def groups(self, axes):
        names = ("z", "x", "q", "c")
        rest = [n for n in names if n not in axes]
        out = []
        for fixed in itertools.product(*(range(self.size[n]) for n in rest)):
            at = dict(zip(rest, fixed))
            out.append(
                [
                    self.flat({**at, **dict(zip(axes, v))})
                    for v in itertools.product(*(range(self.size[n]) for n in axes))
                ]
            )
        return out

    def exchange(self, blocks):
        return lax.all_to_all(
            blocks, AXES, 0, 0, axis_index_groups=self.groups(("z",)), tiled=True
        )

    def gather_chips(self, value):
        return lax.all_gather(
            value, AXES, axis=0, axis_index_groups=self.groups(("z", "x", "q")), tiled=True
        )


def total_of(*values):
    return sum(v.astype(f32) for v in values)


def lock(*values):
    return lax.optimization_barrier(values)


def behind(value, *others):
    return lax.optimization_barrier((value, others))[0]


def hbm(value):
    return pltpu.with_memory_space_constraint(value, pltpu.HBM)


def call(kernel, place, operands, **kw):
    spec = pltpu.PrefetchScalarGridSpec(
        num_scalar_prefetch=1,
        grid=kw.pop("grid"),
        in_specs=kw.pop("in_specs"),
        out_specs=kw.pop("out_specs"),
        scratch_shapes=kw.pop("scratch_shapes", []),
    )
    return pl.pallas_call(
        kernel,
        grid_spec=spec,
        compiler_params=pltpu.CompilerParams(vmem_limit_bytes=kw.pop("mib") * 2**20),
        **kw,
    )(place, *operands)


class Pieces:
    def __init__(self, grid, found):
        self.grid = grid
        self.found = found
        self.arrays = [f[0] for f in found]
        self.count = sum(f[0].shape[0] for f in found)

    def copies(self, place, refs, sem, moves):
        out = []
        for ref, (piece, at_chips) in zip(refs, self.found):
            for i, distance in enumerate(at_chips):
                chip = self.grid.chip(place, *distance)
                for at, rows, col, cols, to in moves:
                    source = ref.at[i, pl.ds(at, rows), pl.ds(col, cols)]
                    out.append(pltpu.make_async_copy(source, to(chip), sem.at[len(out)]))
        return out


class Whole:
    def __init__(self, arrays):
        self.arrays = arrays
        self.count = 1


def pick(grid, found, first, lanes):
    arrays = [f[0][:, first:, :lanes] for f in found]
    rows = arrays[0].shape[1]

    def kernel(place, *refs):
        for ref, (piece, at_chips) in zip(refs[:-1], found):
            for i, distance in enumerate(at_chips):
                refs[-1][grid.chip(place, *distance)] = ref[i]

    return call(
        kernel,
        grid.place,
        arrays,
        grid=(1,),
        in_specs=[pl.BlockSpec(a.shape, lambda i, s: (0, 0, 0)) for a in arrays],
        out_specs=pl.BlockSpec((grid.chips, rows, lanes), lambda i, s: (0, 0, 0)),
        out_shape=jax.ShapeDtypeStruct((grid.chips, rows, lanes), bf16),
        cost_estimate=SMALL,
        mib=8,
        name="pick",
    )


def vectors_kernel(place, small_ref, out_ref):
    rows, width = small_ref.shape[0], out_ref.shape[1]
    chips = rows // 16
    m = lax.broadcasted_iota(jnp.int32, (128, width), 0)
    j = lax.broadcasted_iota(jnp.int32, (128, width), 1)
    small = small_ref[...]
    narrow, wide = width // chips, 2 * width // chips
    spread = lambda n: mm(small, ((j % n) == m).astype(bf16)).reshape(chips, 16, width)
    one = lax.broadcasted_iota(jnp.int32, (chips, 16, width), 2)
    chip = lax.broadcasted_iota(jnp.int32, (chips, 16, width), 0)
    a, b = spread(narrow), spread(wide)
    plain = jnp.sum(jnp.where(one // narrow == chip, a, 0.0), axis=0)
    low = jnp.sum(jnp.where(one // wide == chip, b, 0.0), axis=0)
    high = jnp.sum(jnp.where(one // wide + chips // 2 == chip, b, 0.0), axis=0)
    out_ref[...] = jnp.concatenate(
        [plain[0:6], low[6:7], high[6:7], low[7:8], high[7:8], plain[0:6]], axis=0
    )


def vectors_of(grid, small, width):
    rows = small.shape[0]
    return call(
        vectors_kernel,
        grid.place,
        [small],
        grid=(1,),
        in_specs=[pl.BlockSpec((rows, 128), lambda i, s: (0, 0))],
        out_specs=pl.BlockSpec((16, width), lambda i, s: (0, 0)),
        out_shape=jax.ShapeDtypeStruct((16, width), f32),
        cost_estimate=SMALL,
        mib=8,
        name="vectors",
    )


def first_lanes(head):
    lane = lax.broadcasted_iota(jnp.int32, (1, 2 * HEAD_DIM), 1)
    return lane < HEAD_DIM if head == 0 else lane >= HEAD_DIM


def chunk_of(rows):
    return 1536 if rows % 1536 == 0 else rows


def attn_fwd_kernel(q_ref, k_ref, v_ref, hot_ref, pen_ref, o_ref, ob_ref, lse_ref):
    total_keys = k_ref.shape[0]
    chunk = chunk_of(total_keys)
    steps = total_keys // chunk
    query_rows = q_ref.shape[0]
    query, hot = q_ref[...], hot_ref[...]
    outs = []
    for head in range(2):
        sel = first_lanes(head)
        q_aug = jnp.where(sel, query, hot)

        def scores(rows):
            k_aug = jnp.where(sel, k_ref[rows, :], pen_ref[rows, :])
            return mm(k_aug, q_aug, ((1,), (1,)))

        def weigh(rows, s, top):
            p = jnp.exp2(s - top)
            added = mm(v_ref[rows, :], p.astype(bf16), ((0,), (0,)))
            return jnp.sum(p, axis=0, keepdims=True), added

        if steps == 1:
            s = scores(slice(0, chunk))
            top = jnp.max(s, axis=0, keepdims=True)
            total, acc = weigh(slice(0, chunk), s, top)
        else:

            def step(i, carry):
                top, total, acc = carry
                rows = pl.ds(pl.multiple_of(i * chunk, chunk), chunk)
                s = scores(rows)
                new_top = jnp.maximum(top, jnp.max(s, axis=0, keepdims=True))
                more, added = weigh(rows, s, new_top)
                fade = jnp.exp2(top - new_top)
                return new_top, total * fade + more, acc * fade + added

            top, total, acc = lax.fori_loop(
                0,
                steps,
                step,
                (
                    jnp.full((1, query_rows), -1e30, f32),
                    jnp.zeros((1, query_rows), f32),
                    jnp.zeros((2 * HEAD_DIM, query_rows), f32),
                ),
            )
        outs.append((acc / total)[head * HEAD_DIM : (head + 1) * HEAD_DIM])
        lse_ref[0, head : head + 1, :] = top + jnp.log2(total)
    out = jnp.concatenate(outs, axis=0).T
    o_ref[...] = out
    ob_ref[...] = out.astype(bf16)


def attn_fwd(queries, keys, values, hot, pen, start, pairs):
    rows, width = queries.shape[0], pairs * 128
    total_keys = keys.shape[0]
    pairs = width // 128
    block = 256 if rows % 256 == 0 else rows
    cost = SMALL
    return pl.pallas_call(
        attn_fwd_kernel,
        grid=(pairs, rows // block),
        in_specs=[
            pl.BlockSpec((block, 128), lambda p, i: (i, p + start)),
            pl.BlockSpec((total_keys, 128), lambda p, i: (0, p + start)),
            pl.BlockSpec((total_keys, 128), lambda p, i: (0, p + start)),
            pl.BlockSpec((block, 128), lambda p, i: (i, 0)),
            pl.BlockSpec((total_keys, 128), lambda p, i: (0, 0)),
        ],
        out_specs=[
            pl.BlockSpec((block, 128), lambda p, i: (i, p)),
            pl.BlockSpec((block, 128), lambda p, i: (i, p)),
            pl.BlockSpec((1, 2, block), lambda p, i: (p, 0, i)),
        ],
        out_shape=[
            jax.ShapeDtypeStruct((rows, width), f32),
            jax.ShapeDtypeStruct((rows, width), bf16),
            jax.ShapeDtypeStruct((pairs, 2, rows), f32),
        ],
        compiler_params=pltpu.CompilerParams(vmem_limit_bytes=16 * 2**20),
        cost_estimate=cost,
        name="attn_fwd",
    )(queries, keys, values, hot, pen)


def attn_bwd_kernel(
    q_ref, k_ref, v_ref, hot_ref, pen_ref, o_ref, do_ref, lse_ref, dq_ref, dk_ref, dv_ref, dk_acc, dv_acc
):
    total_keys = k_ref.shape[0]
    chunk = chunk_of(total_keys)
    steps = total_keys // chunk
    at, last = pl.program_id(1), pl.num_programs(1) - 1
    query, hot, grad = q_ref[...], hot_ref[...], do_ref[...]

    @pl.when(at == 0)
    def _():
        dk_acc[...] = jnp.zeros_like(dk_acc)
        dv_acc[...] = jnp.zeros_like(dv_acc)

    flipped = (grad.astype(f32) * o_ref[...]).T
    zero = jnp.zeros_like(query)

    def step(rows):
        keys, values, pen = k_ref[rows, :], v_ref[rows, :], pen_ref[rows, :]
        dq = None
        dk = dk_acc[rows, :]
        dv = dv_acc[rows, :]
        for head in range(2):
            sel = first_lanes(head)
            delta = jnp.sum(
                flipped[head * HEAD_DIM : (head + 1) * HEAD_DIM], axis=0, keepdims=True
            )
            k_aug = jnp.where(sel, keys, pen)
            s = mm(k_aug, jnp.where(sel, query, hot), ((1,), (1,)))
            p = jnp.exp2(s - lse_ref[0, head : head + 1, :])
            grad_h = jnp.where(sel, grad, zero)
            dp = mm(values, grad_h, ((1,), (1,)))
            ds = (p * (dp - delta)).astype(bf16)
            dv = dv + mm(p.astype(bf16), grad_h)
            dk = dk + mm(ds, jnp.where(sel, query, zero))
            part = mm(keys, ds, ((0,), (0,)))
            part = part[head * HEAD_DIM : (head + 1) * HEAD_DIM]
            dq = part if dq is None else jnp.concatenate([dq, part], axis=0)
        dk_acc[rows, :] = dk
        dv_acc[rows, :] = dv
        return dq

    if steps == 1:
        dq = step(slice(0, chunk))
    else:
        dq = lax.fori_loop(
            0,
            steps,
            lambda i, total: total + step(pl.ds(pl.multiple_of(i * chunk, chunk), chunk)),
            jnp.zeros((2 * HEAD_DIM, query.shape[0]), f32),
        )
    dq_ref[...] = (dq.T * HEAD_DIM**-0.5).astype(bf16)

    @pl.when(at == last)
    def _():
        dk_ref[...] = (dk_acc[...] * (1.0 / LOG2E)).astype(bf16)
        dv_ref[...] = dv_acc[...].astype(bf16)


def attn_bwd(queries, keys, values, hot, pen, attended, d_attended, lse, start, pairs):
    rows = queries.shape[0]
    total_keys = keys.shape[0]
    block = 256 if rows % 256 == 0 else rows
    by_query = pl.BlockSpec((block, 128), lambda p, i: (i, p + start))
    own = pl.BlockSpec((block, 128), lambda p, i: (i, p))
    by_key = pl.BlockSpec((total_keys, 128), lambda p, i: (0, p + start))
    to_query = pl.BlockSpec((block, 128), lambda p, i: (i, p))
    to_key = pl.BlockSpec((total_keys, 128), lambda p, i: (0, p))
    width = pairs * 128
    cost = SMALL
    return pl.pallas_call(
        attn_bwd_kernel,
        grid=(pairs, rows // block),
        in_specs=[
            by_query,
            by_key,
            by_key,
            pl.BlockSpec((block, 128), lambda p, i: (i, 0)),
            pl.BlockSpec((total_keys, 128), lambda p, i: (0, 0)),
            own,
            by_query,
            pl.BlockSpec((1, 2, block), lambda p, i: (p, 0, i)),
        ],
        out_specs=[to_query, to_key, to_key],
        out_shape=[
            jax.ShapeDtypeStruct((rows, width), bf16),
            jax.ShapeDtypeStruct((total_keys, width), bf16),
            jax.ShapeDtypeStruct((total_keys, width), bf16),
        ],
        scratch_shapes=[pltpu.VMEM((total_keys, 128), f32), pltpu.VMEM((total_keys, 128), f32)],
        compiler_params=pltpu.CompilerParams(vmem_limit_bytes=24 * 2**20),
        cost_estimate=cost,
        name="attn_bwd",
    )(queries, keys, values, hot, pen, attended, d_attended, lse)


def halves(place, mine, other):
    first = place[3] == 0
    return jnp.where(first, mine, other), jnp.where(first, other, mine)


def load_all(copies):
    for c in copies:
        c.start()
    for c in copies:
        c.wait()


def qkv_kernel(weights, moves, place, x_ref, vec_ref, *refs):
    pieces, refs = refs[:-9], refs[-9:]
    q_ref, k_ref, v_ref, h1t_ref, n1_ref, rstd_ref, w_out, w_s, sem = refs
    half = q_ref.shape[1]
    width = x_ref.shape[1]
    step = pl.program_id(0)

    @pl.when(step == 0)
    def _():
        if isinstance(weights, Pieces):
            load_all(weights.copies(place, pieces, sem, moves(w_s)))
        else:
            load_all([pltpu.make_async_copy(pieces[0], w_s.at[0], sem.at[0])])
        w_out[...] = w_s[...]

    x = x_ref[...].astype(f32)
    centered = x - mean_of(x)
    rstd = lax.rsqrt(mean_of(centered * centered) + NORM_EPS)
    n1 = centered * rstd
    n1_ref[...] = n1.astype(bf16)
    rstd_ref[...] = rstd
    h1 = (n1 * vec_ref[0:1, :] + vec_ref[1:2, :]).astype(bf16)
    low, high = vec_ref[6:8, :half], vec_ref[6:8, half:]
    bias = jnp.where(place[3] == 0, low, high)
    w = w_s[...].reshape(width, 3 * half)

    @pl.when(step < 2)
    def _():
        q = mm(h1, w[:, :half]) + bias[0:1]
        q_ref[...] = (q * (LOG2E * HEAD_DIM**-0.5)).astype(bf16)

    kv = mm(h1, w[:, half:])
    k_ref[...] = kv[:, :half].astype(bf16)
    v_ref[...] = (kv[:, half:] + bias[1:2]).astype(bf16)
    h1t_ref[...] = h1.T


def project_qkv(grid, x, vec, weights, local):
    rows, width = x.shape
    half = width // 2
    if isinstance(weights, Pieces):
        r = width // grid.chips
        moves = lambda w: [(0, r, 0, 3 * half, lambda chip: w.at[chip])]
        shape = (grid.chips, r, 3 * half)
    else:
        moves = None
        shape = (1, width, 3 * half)
    *found, w = call(
        functools.partial(qkv_kernel, weights, moves),
        grid.place,
        [x, vec] + [hbm(w) for w in weights.arrays],
        grid=(rows // local,),
        in_specs=[
            pl.BlockSpec((local, width), lambda i, s: (i, 0)),
            pl.BlockSpec(vec.shape, lambda i, s: (0, 0)),
        ]
        + [pl.BlockSpec(memory_space=pl.ANY)] * len(weights.arrays),
        out_specs=[
            pl.BlockSpec((local, half), lambda i, s: (jnp.minimum(i, 1), 0)),
            pl.BlockSpec((local, half), lambda i, s: (i, 0)),
            pl.BlockSpec((local, half), lambda i, s: (i, 0)),
            pl.BlockSpec((width, local), lambda i, s: (0, i)),
            pl.BlockSpec((local, width), lambda i, s: (i, 0)),
            pl.BlockSpec((local, 1), lambda i, s: (i, 0)),
            pl.BlockSpec(shape, lambda i, s: (0, 0, 0)),
        ],
        out_shape=[
            jax.ShapeDtypeStruct((2 * local, half), bf16),
            jax.ShapeDtypeStruct((rows, half), bf16),
            jax.ShapeDtypeStruct((rows, half), bf16),
            pltpu.HBM((width, rows), bf16),
            pltpu.HBM((rows, width), bf16),
            pltpu.HBM((rows, 1), f32),
            pltpu.HBM(shape, bf16),
        ],
        scratch_shapes=[pltpu.VMEM(shape, bf16), pltpu.SemaphoreType.DMA((weights.count,))],
        cost_estimate=SMALL,
        mib=20,
        name="qkv",
    )
    return found + [w.reshape(width, 3 * half)]


def mean_of(v):
    return jnp.mean(v, axis=-1, keepdims=True)


def join(refs):
    return jnp.concatenate([r[...] for r in refs], axis=1)


def out_kernel(n, place, x_ref, w_ref, vec_ref, *refs):
    (after_ref, h2_ref, n2_ref, rstd_ref) = refs[2 * n :]
    a, b = halves(place, join(refs[:n]), join(refs[n : 2 * n]))
    after = x_ref[...].astype(f32) + mm(a, w_ref[0]) + mm(b, w_ref[1]) + vec_ref[2:3, :]
    after_ref[...] = after
    centered = after - mean_of(after)
    rstd = lax.rsqrt(mean_of(centered * centered) + NORM_EPS)
    n2 = centered * rstd
    n2_ref[...] = n2.astype(bf16)
    rstd_ref[...] = jnp.broadcast_to(rstd, rstd_ref.shape)
    h2_ref[...] = (n2 * vec_ref[3:4, :] + vec_ref[4:5, :]).astype(bf16)


def project_out(grid, x, mine, other, w, vec):
    rows, width = mine[0].shape[0], x.shape[1]
    block = 256 if rows % 256 == 0 else rows
    line = lambda n: pl.BlockSpec((block, n), lambda i, s: (i, 0))
    return call(
        functools.partial(out_kernel, len(mine)),
        grid.place,
        [x, w, vec] + mine + other,
        grid=(rows // block,),
        in_specs=[
            line(width),
            pl.BlockSpec(w.shape, lambda i, s: (0, 0, 0)),
            pl.BlockSpec(vec.shape, lambda i, s: (0, 0)),
        ]
        + [line(v.shape[1]) for v in mine + other],
        out_specs=[line(width), line(width), line(width), line(128)],
        out_shape=[
            pltpu.HBM((rows, width), f32),
            pltpu.HBM((rows, width), bf16),
            pltpu.HBM((rows, width), bf16),
            pltpu.HBM((rows, 128), f32),
        ],
        cost_estimate=SMALL,
        mib=16,
        name="out_proj",
    )


def norm_back(grad, normed, rstd, gain):
    e = grad * gain
    return (e - mean_of(e) - normed * mean_of(e * normed)) * rstd


def sum_rows(v):
    return jnp.sum(v, axis=0, keepdims=True)


def out_back_kernel(
    place, mine_ref, got_ref, dy_ref, n2_ref, rstd_ref, vec_ref, w_ref, after_ref, branch_ref, datt_ref, sums_ref
):
    d_h2 = mine_ref[...] + got_ref[...].astype(f32)
    dy = dy_ref[...].astype(f32)
    n2 = n2_ref[...].astype(f32)
    d_after = dy + norm_back(d_h2, n2, rstd_ref[:, 0:1], vec_ref[3:4, :])
    after_ref[...] = d_after
    branch = d_after.astype(bf16)
    branch_ref[...] = branch
    datt_ref[...] = mm(branch, w_ref[0], ((1,), (1,))).astype(bf16)
    rows = [sum_rows(branch.astype(f32)), sum_rows(d_h2 * n2), sum_rows(d_h2), sum_rows(dy)]
    sums = jnp.concatenate(rows + [jnp.zeros((4, dy.shape[1]), f32)], axis=0) * 0.5

    @pl.when(pl.program_id(0) == 0)
    def _():
        sums_ref[...] = jnp.zeros_like(sums_ref)

    sums_ref[...] += sums


def out_back(grid, mine, got, dy, n2, rstd, vec, w):
    rows, width = mine.shape
    block = 256 if rows % 256 == 0 else rows
    line = lambda n: pl.BlockSpec((block, n), lambda i, s: (i, 0))
    return call(
        out_back_kernel,
        grid.place,
        [mine, got, hbm(dy), hbm(n2), hbm(rstd), vec, hbm(w)],
        grid=(rows // block,),
        in_specs=[
            line(width),
            line(width),
            line(width),
            line(width),
            line(128),
            pl.BlockSpec(vec.shape, lambda i, s: (0, 0)),
            pl.BlockSpec((1,) + w.shape[1:], lambda i, s: (s[3], 0, 0)),
        ],
        out_specs=[
            line(width),
            line(width),
            line(width // 2),
            pl.BlockSpec((8, width), lambda i, s: (0, 0)),
        ],
        out_shape=[
            pltpu.HBM((rows, width), f32),
            jax.ShapeDtypeStruct((rows, width), bf16),
            jax.ShapeDtypeStruct((rows, width // 2), bf16),
            jax.ShapeDtypeStruct((8, width), f32),
        ],
        cost_estimate=SMALL,
        mib=20,
        name="out_back",
    )


def store_rows(grid, place, ref, value, shard, slot):
    for i in range(grid.chips):
        column, z = grid.relative(place, i, True)
        ref[column, z, slot, 0:shard, :] = value[i * shard : (i + 1) * shard]


def vector_rows(chips, sums1, sums2, ups):
    width = sums1.shape[1]
    narrow, wide = width // chips, 2 * width // chips
    plain = jnp.concatenate([sums1[0:2], sums2[0:4], sums1[0:2]], axis=0)

    def fold(value, n, chip):
        lane = lax.broadcasted_iota(jnp.int32, (chips, 8, width), 2)
        value = jnp.where(lane // n == chip, value, 0.0).reshape(chips * 8, width)
        m = lax.broadcasted_iota(jnp.int32, (width, 128), 1)
        j = lax.broadcasted_iota(jnp.int32, (width, 128), 0)
        return mm(value.astype(bf16), (j % n == m).astype(bf16)).reshape(chips, 8, 128)

    chip = lax.broadcasted_iota(jnp.int32, (chips, 8, width), 0)
    a = fold(jnp.broadcast_to(plain[None], (chips, 8, width)), narrow, chip)
    low = jnp.concatenate([sums1[2:3], ups[0:1]] * 4, axis=0)
    high = jnp.concatenate([sums1[3:4], ups[1:2]] * 4, axis=0)
    both = jnp.where(chip < chips // 2, low[None], high[None])
    b = fold(both, wide, chip % (chips // 2))
    row = lax.broadcasted_iota(jnp.int32, (chips, 8, 128), 1)
    return jnp.where(row < 6, a, b).astype(bf16)


def matrix_grads_kernel(grid, fast, n, place, h1t_ref, d_ref, *refs):
    g_ref = refs[-1]
    mine, other, flat, more = refs[:n], refs[n : 2 * n], refs[2 * n : 5 * n], refs[5 * n : -1]
    shard = h1t_ref.shape[0] // grid.chips
    slot = 0
    for part in range(n):
        dq_ref, dk_ref, dv_ref = flat[3 * part : 3 * part + 3]
        chip_rows = dq_ref.shape[0]
        for p in range(dq_ref.shape[1] // 128):
            cols = slice(p * 128, (p + 1) * 128)
            gq = mm(h1t_ref[:, :chip_rows], dq_ref[:, cols])
            gkv = mm(h1t_ref[...], jnp.concatenate([dk_ref[:, cols], dv_ref[:, cols]], axis=1))
            g = jnp.concatenate([gq, gkv], axis=1).astype(bf16)
            if fast:
                store_rows(grid, place, g_ref, g, shard, slot)
            else:
                g_ref[slot] = g
            slot += 1
    a, b = halves(place, join(mine), join(other))
    g = mm(jnp.concatenate([a, b], axis=1), d_ref[...], ((0,), (0,))).astype(bf16)
    if fast:
        store_rows(grid, place, g_ref, g, shard, slot)
        rows = vector_rows(grid.chips, *(r[...] for r in more))
        rows = jnp.concatenate([rows, jnp.zeros_like(rows)], axis=1)
        for i in range(grid.chips):
            column, z = grid.relative(place, i, True)
            g_ref[column, z, 0, pl.ds(shard, 16), 0:128] = rows[i]
    else:
        g_ref[slot] = g


def matrix_gradients(grid, fast, h1t, branch, mine, other, grads, more):
    width = h1t.shape[0]
    rows, half = branch.shape[0], branch.shape[1] // 2
    slots = half // 128 + 1
    if fast:
        shape = (2 * grid.q, grid.z, slots, width // grid.chips + 16, half)
    else:
        shape = (slots, width, half)
    flat = [v for part in grads for v in part]
    whole = lambda v: pl.BlockSpec(v.shape, lambda i, s: (0, 0))
    return call(
        functools.partial(matrix_grads_kernel, grid, fast, len(mine)),
        grid.place,
        [hbm(h1t), branch] + mine + other + flat + more,
        grid=(1,),
        in_specs=[whole(h1t), pl.BlockSpec((rows, half), lambda i, s: (0, s[3]))]
        + [whole(v) for v in mine + other + flat + more],
        out_specs=pl.BlockSpec(shape, lambda i, s: (0,) * len(shape)),
        out_shape=pltpu.HBM(shape, bf16),
        cost_estimate=SMALL,
        mib=30,
        name="matrix_grads",
    )


def input_back_kernel(parts, place, *refs):
    grads, (w_ref, n1_ref, mine_ref, other_ref, sums_ref) = refs[: 3 * parts], refs[3 * parts :]
    step = pl.program_id(0)
    dq, dk, dv = (
        jnp.concatenate([grads[3 * p + i][...] for p in range(parts)], axis=1) for i in range(3)
    )
    half = dq.shape[1]
    width = n1_ref.shape[1]
    dq = jnp.where(step < 2, dq, jnp.zeros_like(dq))
    d = mm(jnp.concatenate([dq, dk, dv], axis=1), w_ref[...], ((1,), (1,)))
    block, core = step // 2, step % 2

    @pl.when(core == place[3])
    def _():
        mine_ref[block] = d

    @pl.when(core != place[3])
    def _():
        other_ref[block] = d.astype(bf16)

    none = jnp.zeros((1, half), f32)

    def spread(v):
        v = sum_rows(v.astype(f32))
        first = place[3] == 0
        return jnp.concatenate([jnp.where(first, v, none), jnp.where(first, none, v)], axis=1)

    rows = [sum_rows(d * n1_ref[...].astype(f32)), sum_rows(d), spread(dq), spread(dv)]
    sums = jnp.concatenate(rows + [jnp.zeros((4, width), f32)], axis=0)

    @pl.when(step == 0)
    def _():
        sums_ref[...] = jnp.zeros_like(sums_ref)

    sums_ref[...] += sums


def input_back(grid, grads, w, n1, local):
    rows, width = n1.shape
    flat = [g for part in grads for g in part]
    specs = []
    for dq, dk, dv in grads:
        n = dq.shape[1]
        specs.append(pl.BlockSpec((local, n), lambda i, s: (jnp.minimum(i, 1), 0)))
        specs += [pl.BlockSpec((local, n), lambda i, s: (i, 0))] * 2
    shape = (grid.q, local, width)
    return call(
        functools.partial(input_back_kernel, len(grads)),
        grid.place,
        flat + [hbm(w), hbm(n1)],
        grid=(rows // local,),
        in_specs=specs
        + [
            pl.BlockSpec(w.shape, lambda i, s: (0, 0)),
            pl.BlockSpec((local, width), lambda i, s: (i, 0)),
        ],
        out_specs=[
            pl.BlockSpec(shape, lambda i, s: (0, 0, 0)),
            pl.BlockSpec(shape, lambda i, s: (0, 0, 0)),
            pl.BlockSpec((8, width), lambda i, s: (0, 0)),
        ],
        out_shape=[
            pltpu.HBM(shape, f32),
            jax.ShapeDtypeStruct(shape, bf16),
            jax.ShapeDtypeStruct((8, width), f32),
        ],
        cost_estimate=SMALL,
        mib=24,
        name="input_back",
    )


def finish_kernel(n_got, place, *refs):
    mine_ref, got_ref = refs[:2]
    sides = refs[2 : 2 + n_got]
    n1_ref, rstd_ref, after_ref, vec_ref, out_ref = refs[2 + n_got :]
    d = mine_ref[0] + got_ref[0].astype(f32)
    for s in sides:
        d = d + s[...].astype(f32)
    out_ref[...] = after_ref[...] + norm_back(
        d, n1_ref[...].astype(f32), rstd_ref[...], vec_ref[0:1, :]
    )


def finish(grid, mine, got, sides, n1, rstd1, d_after, vec):
    _, rows, width = mine.shape
    first = pl.BlockSpec((1, rows, width), lambda i, s: (0, 0, 0))
    own = lambda n: pl.BlockSpec((rows, n), lambda i, s: (s[3], 0))
    return call(
        functools.partial(finish_kernel, len(sides)),
        grid.place,
        [hbm(mine), got] + sides + [hbm(n1), rstd1, hbm(d_after), vec],
        grid=(1,),
        in_specs=[first, first]
        + [pl.BlockSpec((rows, width), lambda i, s: (0, 0))] * len(sides)
        + [own(width), own(1), own(width), pl.BlockSpec(vec.shape, lambda i, s: (0, 0))],
        out_specs=pl.BlockSpec((rows, width), lambda i, s: (0, 0)),
        out_shape=jax.ShapeDtypeStruct((rows, width), f32),
        cost_estimate=SMALL,
        mib=20,
        name="finish",
    )


def ff_kernel(grid, ups, downs, place, h2_ref, dy_ref, vec_ref, *refs):
    fast = isinstance(ups, Pieces)
    n_up, n = len(ups.arrays), len(ups.arrays) + len(downs.arrays)
    pieces, refs = refs[:n], refs[n:]
    if fast:
        g_ref, refs = refs[0], refs[1:]
    else:
        (gdown_ref, gup_ref), refs = refs[:2], refs[2:]
    gbias_ref, out_ref, dh_ref, dhb_ref, act_s, dhid_s, h2t_s, up_s, down_s, sem, down_sem = refs
    step = pl.program_id(0)
    rows, width = h2_ref.shape
    units = act_s.shape[1]
    part = 256 if rows % 256 == 0 else rows

    @pl.when(step == 0)
    def _():
        if fast:
            r = up_s.shape[2]
            copies = ups.copies(
                place,
                pieces[:n_up],
                sem,
                [
                    (0, r, 0, width, lambda chip: up_s.at[0, chip]),
                    (r, r, 0, width, lambda chip: up_s.at[1, chip]),
                ],
            )
        else:
            tile = pl.ds(0, units), pl.ds(units, units)
            copies = [
                pltpu.make_async_copy(pieces[0].at[:, tile[i]], up_s.at[i, 0], sem.at[i])
                for i in range(2)
            ]
        copies.append(pltpu.make_async_copy(pieces[n_up].at[:, place[3], pl.ds(0, down_s.shape[1])], down_s, down_sem.at[0]))
        for c in copies:
            c.start()
        h2t_s[...] = h2_ref[...].T
        for c in copies:
            c.wait()

    w_up = up_s[step].reshape(width, units)
    d = down_s.shape[0] // 2
    w_down = down_s[pl.ds(step * d, d)].reshape(units, width)
    bias = jnp.where(step == 0, vec_ref[8:9, :], vec_ref[9:10, :])
    for at in range(0, rows, part):
        here = slice(at, at + part)
        for col in range(0, units, 256):
            cols = slice(col, col + 256)
            hidden = mm(h2_ref[here, :], w_up[:, cols]) + bias[:, cols]
            phi = 0.5 * (1.0 + lax.erf(hidden * (0.5**0.5)))
            dens = jnp.exp(-0.5 * hidden * hidden) * (1.0 / math.sqrt(2.0 * math.pi))
            act_s[here, cols] = (hidden * phi).astype(bf16)
            d_act = mm(dy_ref[here, :], w_down[cols, :], ((1,), (1,)))
            dhid_s[here, cols] = (d_act * (phi + hidden * dens)).astype(bf16)
    act, d_hidden = act_s[...], dhid_s[...]
    gdown = mm(act, dy_ref[...], ((0,), (0,))).astype(bf16)
    gup = mm(h2t_s[...], d_hidden).astype(bf16)
    gbias_ref[0] = sum_rows(d_hidden.astype(f32))
    out = mm(act, w_down)
    dh = mm(d_hidden, w_up, ((1,), (1,)))
    if fast:
        down_shard = 2 * units // grid.chips
        up_shard = width // grid.chips
        half = grid.chips // 2
        for i in range(half):
            column, z = grid.relative(place, step * half + i)
            g_ref[column, z, 0:down_shard, :] = gdown[i * down_shard : (i + 1) * down_shard]
        for i in range(grid.chips):
            column, z = grid.relative(place, i)
            to = pl.multiple_of(down_shard + step * up_shard, 16)
            g_ref[column, z, pl.ds(to, up_shard), :] = gup[i * up_shard : (i + 1) * up_shard]
    else:
        gdown_ref[...] = gdown
        gup_ref[...] = gup

    @pl.when(step == 0)
    def _():
        out_ref[...] = out
        dh_ref[...] = dh

    @pl.when(step == 1)
    def _():
        out_ref[...] += out
        total = dh_ref[...] + dh
        dh_ref[...] = total
        dhb_ref[...] = total.astype(bf16)


def feed_forward(grid, h2, dy, ups, downs, vec, units):
    fast = isinstance(ups, Pieces)
    rows, width = h2.shape
    tile = units // 2
    chips = grid.chips
    whole = pl.BlockSpec((rows, width), lambda j, s: (0, 0))
    cols = pl.BlockSpec((width, tile), lambda j, s: (0, j))
    lines = pl.BlockSpec((tile, width), lambda j, s: (j, 0))
    if fast:
        shape = (2 * grid.q, grid.z, (units + width * 2) // chips, width)
        g_specs = [pl.BlockSpec(shape, lambda j, s: (0, 0, 0, 0))]
        g_shapes = [pltpu.HBM(shape, bf16)]
        up_shape = (2, chips, width // chips, tile)
    else:
        g_specs = [lines, cols]
        g_shapes = [
            jax.ShapeDtypeStruct((units, width), bf16),
            jax.ShapeDtypeStruct((width, units), bf16),
        ]
        up_shape = (2, 1, width, tile)
    return call(
        functools.partial(ff_kernel, grid, ups, downs),
        grid.place,
        [hbm(h2), hbm(dy), vec] + [hbm(w) for w in ups.arrays + downs.arrays],
        grid=(2,),
        in_specs=[whole, whole, pl.BlockSpec(vec.shape, lambda j, s: (0, 0))]
        + [pl.BlockSpec(memory_space=pl.ANY)] * len(ups.arrays + downs.arrays),
        out_specs=g_specs
        + [pl.BlockSpec((1, 1, tile), lambda j, s: (j, 0, 0)), whole, whole, whole],
        out_shape=g_shapes
        + [
            jax.ShapeDtypeStruct((2, 1, tile), f32),
            pltpu.HBM((rows, width), f32),
            jax.ShapeDtypeStruct((rows, width), f32),
            jax.ShapeDtypeStruct((rows, width), bf16),
        ],
        scratch_shapes=[
            pltpu.VMEM((rows, tile), bf16),
            pltpu.VMEM((rows, tile), bf16),
            pltpu.VMEM((width, rows), bf16),
            pltpu.VMEM(up_shape, bf16),
            pltpu.VMEM((chips, units // chips, width), bf16),
            pltpu.SemaphoreType.DMA((2 * ups.count,)),
            pltpu.SemaphoreType.DMA((downs.count,)),
        ],
        cost_estimate=SMALL,
        mib=40,
        name="feed_forward",
    )


def mine_and_other(place, mine_ref, other_ref, slot, first, shard):
    at = pl.ds(pl.multiple_of(first + shard * place[3], 8), shard)
    return halves(place, mine_ref[slot, at, :], other_ref[slot, at, :].astype(f32))


def last_ff_kernel(grid, shard, place, ff_ref, other_ref, up_ref, down_ref):
    width = ff_ref.shape[1]
    per_chip = down_ref.shape[0]
    down_ref[...] = ff_ref[:per_chip, :]
    half = grid.chips // 2
    for h in range(2):
        first = 2 * shard * h
        at = lambda n: pl.ds(pl.multiple_of(n + first + shard * place[3], 8), shard)
        a, b = halves(place, ff_ref[at(per_chip), :], other_ref[at(0), :].astype(f32))
        for i in range(half):
            to = (h * half + i) * 2 * per_chip
            cols = slice(i * per_chip, (i + 1) * per_chip)
            up_ref[:, to : to + 2 * per_chip] = jnp.concatenate([a[:, cols], b[:, cols]], axis=1)


def last_ff(grid, ff, other, shard):
    rows, width = ff.shape
    whole = lambda shape: pl.BlockSpec(shape, lambda i, s: (0, 0))
    up, down = (shard, 4 * width * 2 // 2), (rows - 4 * shard, width)
    return call(
        functools.partial(last_ff_kernel, grid, shard),
        grid.place,
        [ff, other],
        grid=(1,),
        in_specs=[whole(ff.shape), whole(other.shape)],
        out_specs=[whole(up), whole(down)],
        out_shape=[jax.ShapeDtypeStruct(up, f32), jax.ShapeDtypeStruct(down, f32)],
        cost_estimate=SMALL,
        mib=8,
        name="last_ff",
    )


def last_rest_kernel(shard, place, own_ref, other_ref, qkv_ref, out_ref, six_ref, qv_ref, up_ref):
    pairs, half = own_ref.shape[0] - 1, own_ref.shape[2]
    for p in range(pairs + 1):
        both = mine_and_other(place, own_ref, other_ref, p, 0, shard)
        for core, value in enumerate(both):
            if p == pairs:
                out_ref[:, core * half : (core + 1) * half] = value
                continue
            for t in range(3):
                to = 2 * half * t + half * core + 128 * p
                qkv_ref[:, to : to + 128] = value[:, 128 * t : 128 * (t + 1)]
    mine = own_ref[0, 2 * shard : 2 * shard + 8, 0:128]
    total = mine + other_ref[0, 2 * shard : 2 * shard + 8, 0:128].astype(f32)
    first = place[3] == 0
    six_ref[...] = jnp.where(first, total[:, :shard], total[:, shard : 2 * shard])
    n = 2 * shard
    qv_ref[...] = jnp.where(first, total[6:7, :n], total[6:7, n : 2 * n])
    up_ref[...] = mine[7:8, : up_ref.shape[1]]


def last_rest(grid, own, other, shard, per_chip):
    half = own.shape[2]
    whole = lambda shape: pl.BlockSpec(shape, lambda i, s: (0,) * len(shape))
    shapes = [(shard, 6 * half), (shard, 2 * half), (8, shard), (1, 2 * shard), (1, per_chip)]
    return call(
        functools.partial(last_rest_kernel, shard),
        grid.place,
        [own, other],
        grid=(1,),
        in_specs=[whole(own.shape), whole(other.shape)],
        out_specs=[whole(s) for s in shapes],
        out_shape=[jax.ShapeDtypeStruct(s, f32) for s in shapes],
        cost_estimate=SMALL,
        mib=8,
        name="last_rest",
    )


def in_order(first, mine, other):
    return jnp.stack([jnp.where(first, mine, other), jnp.where(first, other, mine)])


def body(
    dp,
    blk,
    inputs,
    clip_ids,
    ln1_gain,
    ln1_bias,
    w_qkv,
    qv_bias,
    w_out,
    out_bias,
    ln2_gain,
    ln2_bias,
    w_up,
    up_bias,
    w_down,
    down_bias,
    out_grad,
):
    grid = Grid(dp, blk)
    core = grid.me["c"]
    first = core == 0
    chips = grid.chips
    width = inputs.shape[2]
    half = width // 2
    local = inputs.shape[1]
    chip_rows = 2 * local
    units = w_up.shape[1] // 2
    shard = w_qkv.shape[0]
    per_chip = units // chips
    fast = shard % 8 == 0 and per_chip % 16 == 0
    swap = lambda v: grid.shift(v, "c", 1)
    at_core = lambda v, dim=0: lax.dynamic_index_in_dim(v, core, dim, keepdims=False)
    not_core = lambda v, dim=0: lax.dynamic_index_in_dim(v, 1 - core, dim, keepdims=False)

    pad = jnp.zeros((16, width), bf16).at[0, :local].set(clip_ids[0].astype(bf16))
    mine = jnp.concatenate([inputs[0], pad], axis=0)
    dy_mine = out_grad[0]
    if fast:
        put = lambda v, n: jnp.zeros((128,), bf16).at[:n].set(v)
        place_at = lambda v: jnp.where(first, jnp.pad(v, (0, v.size)), jnp.pad(v, (v.size, 0)))
        vecs = [ln1_gain, ln1_bias, out_bias, ln2_gain, ln2_bias, down_bias, qv_bias]
        rows = jnp.stack([jnp.pad(place_at(v), (0, 128 - 2 * v.size)) for v in vecs])
        up_row = put(up_bias, per_chip)[None]
        blank = jnp.zeros((8, 128), bf16)
        mine_small = jnp.concatenate([rows, up_row, blank])
        their_small = jnp.concatenate([rows, jnp.zeros_like(up_row), blank])
        widen = lambda v: jnp.pad(v, ((0, 0), (0, 3 * half - 128)))
        split = w_qkv.reshape(shard, 3, 2, half)
        my_qkv = at_core(split, 2).reshape(shard, 3 * half)
        to_qkv = not_core(split, 2).reshape(shard, 3 * half)
        up_split = w_up.reshape(shard, chips, 2, per_chip)
        my_up = at_core(up_split, 2).reshape(shard, units)
        to_up = not_core(up_split, 2).reshape(shard, units)
        got = swap(jnp.concatenate([to_qkv, widen(their_small)]))
        pair = in_order(first, my_qkv, got[:shard])
        small_chip = mine_small + got[shard:, :128]
        qkv_piece = jnp.concatenate([pair.reshape(2 * shard, 3 * half), widen(small_chip)])

        lines = lax.all_gather(jnp.concatenate([w_down, w_out]), AXES, axis=0, tiled=False)
        full_out = lines[:, per_chip:].reshape(width, width)
        downs = Whole([lines.reshape(chips, 2, per_chip + shard, width)])
        qkv_piece, x_sent = lock(qkv_piece, mine)
        qkv_z = grid.along(qkv_piece, "z")
        x_far = grid.along(x_sent, "q")
        x_near = swap(x_sent)
        up_pair = in_order(first, my_up, swap(to_up)).reshape(2 * shard, units)
        up_piece = jnp.concatenate([up_pair[:, :width], up_pair[:, width:]])

        qkv_z, x_far, x_near, up_piece = lock(qkv_z, x_far, x_near, up_piece)
        qkv_line = grid.line(qkv_piece, qkv_z)
        qkv_over, qkv_sides = grid.shift(qkv_line, "x", 1), grid.along(qkv_line, "q")
        up_line = grid.exchange(jnp.broadcast_to(up_piece, (grid.z,) + up_piece.shape))
        x_both = [(mine, x_near)] + [(v, swap(v)) for v in x_far]
        dy_near = swap(dy_mine)

        qkv_over, qkv_sides, x_both, dy_near = lock(qkv_over, qkv_sides, x_both, dy_near)
        found = grid.found(
            qkv_line, qkv_over, qkv_sides, grid.corner_pieces(qkv_over, qkv_sides)
        )
        qkv_weights = Pieces(grid, found)
        small_all = pick(grid, found, 2 * shard, 128)
        vec = vectors_of(grid, small_all.reshape(chips * 16, 128), width)
    else:
        whole = lambda v: lax.all_gather(v, AXES, axis=0, tiled=True)
        full_qkv = at_core(whole(w_qkv).reshape(width, 3, 2, half), 2).reshape(width, 3 * half)
        qkv_weights = Whole([full_qkv])
        full_out = whole(w_out)
        full_up = at_core(whole(w_up).reshape(width, chips, 2, per_chip), 2).reshape(width, units)
        full_down = whole(w_down).reshape(chips, 2, per_chip, width)
        ups, downs = Whole([full_up]), Whole([full_down])
        up_all = at_core(whole(up_bias).reshape(chips, 2, per_chip), 1).reshape(2, width)
        singles = [ln1_gain, ln1_bias, out_bias, ln2_gain, ln2_bias, down_bias]
        vec = jnp.concatenate(
            [whole(v)[None] for v in singles]
            + [whole(qv_bias).reshape(2, width), up_all, jnp.zeros((6, width), bf16)]
        ).astype(f32)
        x_both = [(v, swap(v)) for v in [mine] + grid.along(mine, "q")]
        dy_near = swap(dy_mine)

    both = [in_order(first, *v) for v in x_both]
    token_rows = jnp.concatenate([b[:, :local].reshape(chip_rows, width) for b in both])
    clips = jnp.concatenate([b[:, local, :local].reshape(chip_rows) for b in both])
    lane = lax.broadcasted_iota(jnp.int32, (1, 128), 1) % HEAD_DIM
    same = clips[:, None].astype(jnp.int32) == lane
    hot = same[:chip_rows].astype(bf16)
    pen = jnp.where(same | (lane >= 8), 0.0, -1e30).astype(bf16)
    dy = in_order(first, dy_mine, dy_near).reshape(chip_rows, width)

    queries, keys, values, h1t, n1, rstd1, full_qkv = project_qkv(
        grid, token_rows, vec, qkv_weights, local
    )
    pairs = half // 128
    forward = lambda q, a, n: attn_fwd(q, keys, values, hot, pen, a, n)
    if fast:
        up_line = behind(up_line, [f[0] for f in found])
        up_over, up_sides = grid.shift(up_line, "x", 1), grid.along(up_line, "q")
    parts = [forward(queries, 0, 1)]
    if fast:
        up_over, up_sides = behind((up_over, up_sides), parts[0])
        queries = behind(queries, up_over, up_sides)
        corners = grid.corner_pieces(up_over, up_sides)
        found = grid.found(up_line, up_over, up_sides, corners, True)
        ups = Pieces(grid, found)
    parts.append(forward(queries, 1, pairs - 1))
    att_mine = [p[1] for p in parts]
    if fast:
        att_mine[1] = behind(att_mine[1], corners)
    att_other = [swap(v) for v in att_mine]
    out_rows = full_out.reshape(2, half, width)
    after, h2, n2, rstd2 = project_out(grid, token_rows, att_mine, att_other, out_rows, vec)

    *g_ff, gbias, ff_out, dh, dh_b = feed_forward(grid, h2, dy, ups, downs, vec, units)
    d_after, d_branch, d_att, sums2 = out_back(grid, dh, swap(dh_b), dy, n2, rstd2, vec, out_rows)

    def back(d, i):
        att, _, lse = parts[i]
        start = i
        return attn_bwd(queries, keys, values, hot, pen, att, d, lse, start, att.shape[1] // 128)

    by_core = lambda v: v.reshape(2, local, width)
    up_sums = gbias.reshape(2, width)
    grads = [back(d_att, 0)]
    if fast:
        ff_over, ff_sides = grid.corners(g_ff[0], grads[0])
        d_att = behind(d_att, ff_over, ff_sides)
    grads.append(back(d_att, 1))
    d_mine, d_other, sums1 = input_back(grid, grads, full_qkv, n1, local)
    more = [sums1, sums2, up_sums] if fast else []
    g_all = matrix_gradients(grid, fast, h1t, d_branch, att_mine, att_other, grads, more)
    if fast:
        ff_own = grid.edges(g_ff[0], ff_over, ff_sides, g_all)
        g_all, ff_own, d_other = lock(g_all, ff_own, d_other)
        ff = grid.column(ff_own)
    d_got = swap(d_other)
    sent = [
        (d_mine[k] + d_got[k].astype(f32)).astype(bf16) for k in range(1, grid.q)
    ]
    got = [grid.shift(s, "q", grid.q - k) for k, s in enumerate(sent, 1)]
    ff_out = behind(ff_out, sent)
    out_got = swap(not_core(by_core(ff_out)).astype(bf16)).astype(f32)
    result = at_core(by_core(ff_out)) + out_got + at_core(by_core(after)) + vec[5:6]
    output = result.astype(bf16)[None]
    input_grad = finish(grid, d_mine, d_got, got, n1, rstd1, d_after, vec)[None]

    if fast:
        over, sides = grid.corners(g_all, got)
        own = grid.column_near(grid.edges(g_all, over, sides))
        ff = behind(ff, sides)
        w_up_g, w_down_g = last_ff(grid, ff, swap(ff[per_chip:].astype(bf16)), shard)
        w_qkv_g, w_out_g, six, qv_g, up_g = last_rest(
            grid, own, swap(own.astype(bf16)), shard, per_chip
        )
        qv_g, up_g = qv_g[0], up_g[0]
    else:
        reduce = lambda v: lax.psum_scatter(v, AXES, scatter_dimension=0, tiled=True)

        def spread(v, dim):
            v = v.astype(f32)
            zero = jnp.zeros_like(v)
            return jnp.stack([jnp.where(first, v, zero), jnp.where(first, zero, v)], axis=dim)

        gdown, gup = g_ff
        w_down_g = reduce(
            spread(gdown.reshape(chips, per_chip, width), 1).reshape(2 * units, width)
        )
        w_up_g = reduce(spread(gup.reshape(width, chips, per_chip), 2).reshape(width, 2 * units))
        w_out_g = reduce(spread(g_all[pairs], 1).reshape(width, width))
        per_pair = g_all[:pairs].reshape(pairs, width, 3, 128)
        per_pair = jnp.transpose(per_pair, (1, 2, 0, 3)).reshape(width, 3, half)
        w_qkv_g = reduce(spread(per_pair, 2).reshape(width, 6 * half))
        nothing = jnp.zeros_like(up_sums)
        sums = jnp.concatenate(
            [
                sums1[0:2],
                sums2[0:4],
                sums1[2:4],
                jnp.where(first, up_sums, nothing),
                jnp.where(first, nothing, up_sums),
            ]
        )
        sums = lax.psum(sums, AXES)
        me = (lax.axis_index("dp") * blk) + lax.axis_index("blk")
        six = lax.dynamic_slice(sums, (0, me * shard), (6, shard))
        qv_g = lax.dynamic_slice(sums[6:8].reshape(2 * width), (me * 2 * shard,), (2 * shard,))
        up_g = at_core(sums[8:12].reshape(2, units))
        up_g = lax.dynamic_slice(up_g, (me // 2 * per_chip,), (per_chip,))

    return (
        output,
        input_grad,
        six[0],
        six[1],
        w_qkv_g,
        qv_g,
        w_out_g,
        six[2],
        six[3],
        six[4],
        w_up_g,
        up_g,
        w_down_g,
        six[5],
    )


def solution(mesh):
    both = P(("dp", "blk"))
    rows = P(("dp", "blk"), None)
    tokens = P("dp", "blk", None)
    return jax.shard_map(
        functools.partial(body, mesh.shape["dp"], mesh.shape["blk"]),
        mesh=mesh,
        in_specs=(
            tokens,
            P("dp", "blk"),
            both,
            both,
            rows,
            both,
            rows,
            both,
            both,
            both,
            rows,
            both,
            rows,
            both,
            tokens,
        ),
        out_specs=(
            tokens,
            tokens,
            both,
            both,
            rows,
            both,
            rows,
            both,
            both,
            both,
            rows,
            both,
            rows,
            both,
        ),
        check_vma=False,
    )
```

```python
import functools
import itertools
import math

import jax
import jax.numpy as jnp
from jax import lax
from jax.experimental import pallas as pl
from jax.experimental.pallas import tpu as pltpu
from jax.sharding import PartitionSpec as P

HEAD_DIM = 64
NORM_EPS = 1e-06
LOG2E = math.log2(math.e)
f32 = jnp.float32
bf16 = jnp.bfloat16
AXES = ("dp", "blk")


def mm(a, b, dims=((1,), (0,))):
    return lax.dot_general(a, b, (dims, ((), ())), preferred_element_type=f32)


SMALL = pl.CostEstimate(flops=1000, bytes_accessed=1000, transcendentals=0)


class Grid:
    def __init__(self, dp, blk):
        self.size = {"z": dp // 2, "x": 2, "q": blk // 2, "c": 2}
        self.z, self.x, self.q = dp // 2, 2, blk // 2
        self.chips = self.z * 2 * self.q
        me_dp, me_blk = lax.axis_index("dp"), lax.axis_index("blk")
        self.me = {"z": me_dp // 2, "x": me_dp % 2, "q": me_blk // 2, "c": me_blk % 2}
        self.place = jnp.stack([self.me[a] for a in ("z", "x", "q", "c")]).astype(jnp.int32)

    def flat(self, at):
        return ((at["z"] * self.x + at["x"]) * self.q + at["q"]) * 2 + at["c"]

    def shift(self, value, axis, step):
        pairs = []
        for z in range(self.z):
            for x in range(self.x):
                for q in range(self.q):
                    for c in range(2):
                        at = {"z": z, "x": x, "q": q, "c": c}
                        to = dict(at)
                        to[axis] = (at[axis] + step) % self.size[axis]
                        pairs.append((self.flat(at), self.flat(to)))
        return lax.ppermute(value, AXES, pairs)

    def chip(self, place, dz, dx, dq):
        z = -1 - dz if dz < 0 else lax.rem(place[0] + (self.z - dz), self.z)
        x = lax.rem(place[1] + (self.x - dx), self.x)
        q = lax.rem(place[2] + (self.q - dq), self.q)
        return (z * self.x + x) * self.q + q

    def relative(self, place, chip, near=False):
        z, x, q = chip // (self.x * self.q), chip // self.q % self.x, chip % self.q
        dx = lax.rem(x + self.x - place[1], self.x)
        dq = lax.rem(q + self.q - place[2], self.q)
        if near:
            z = lax.rem(z + self.z - place[0], self.z)
        return dx * self.q + dq, z

    def along(self, value, axis):
        return [self.shift(value, axis, k) for k in range(1, self.size[axis])]

    def line(self, value, others):
        return jnp.stack([value] + others)

    def corner_pieces(self, over, sides):
        half = self.z // 2
        return [
            (self.shift(over[:half], "q", k), self.shift(side[half:], "x", 1))
            for k, side in enumerate(sides, 1)
        ]

    def found(self, line, over, sides, corners, plain=False):
        half = self.z // 2
        zs = [-1 - z if plain else z for z in range(self.z)]
        out = [(line, [(z, 0, 0) for z in zs]), (over, [(z, 1, 0) for z in zs])]
        for k, (side, (a, b)) in enumerate(zip(sides, corners), 1):
            out.append((side, [(z, 0, k) for z in zs]))
            out.append((a, [(z, 1, k) for z in zs[:half]]))
            out.append((b, [(z, 1, k) for z in zs[half:]]))
        return out

    def found_last(self, plane, others):
        at = [(x, q) for x in range(2) for q in range(self.q)]
        return [(p, [(z, x, q) for x, q in at]) for z, p in enumerate([plane] + others)]


    def corners(self, value, first=()):
        half = self.z // 2
        over = value[self.q]
        late, sides = [], []
        for k in range(1, self.q):
            corner = value[self.q + k]
            got = behind(self.shift(corner[:half], "x", 1), first)
            late.append(behind(self.shift(corner[half:], "q", k), first))
            side = value[k]
            sides.append(jnp.concatenate([total_of(side[:half], got).astype(bf16), side[half:]]))
        over = jnp.concatenate([over[:half], total_of(over[half:], *late).astype(bf16)])
        return over, sides

    def edges(self, value, over, sides, first=()):
        parts = [self.shift(over, "x", 1)]
        parts += [self.shift(s, "q", k) for k, s in enumerate(sides, 1)]
        parts = behind(parts, first)
        return total_of(value[0], *parts).astype(bf16)

    def column(self, own):
        return total_of(*self.exchange(own))

    def column_near(self, own, vectors, first=()):
        size = own.shape[1] * own.shape[2]
        rows = jnp.concatenate([own.reshape(self.z, size, own.shape[3])] + [vectors], axis=1)
        got = behind([self.shift(rows[k], "z", k) for k in range(1, self.z)], first)
        total = total_of(own[0], *(v[:size].reshape(own.shape[1:]) for v in got))
        return total, total_of(vectors[0], *(v[size:] for v in got))

    def groups(self, axes):
        names = ("z", "x", "q", "c")
        rest = [n for n in names if n not in axes]
        out = []
        for fixed in itertools.product(*(range(self.size[n]) for n in rest)):
            at = dict(zip(rest, fixed))
            out.append(
                [
                    self.flat({**at, **dict(zip(axes, v))})
                    for v in itertools.product(*(range(self.size[n]) for n in axes))
                ]
            )
        return out

    def exchange(self, blocks):
        return lax.all_to_all(
            blocks, AXES, 0, 0, axis_index_groups=self.groups(("z",)), tiled=True
        )

    def gather_chips(self, value):
        return lax.all_gather(
            value, AXES, axis=0, axis_index_groups=self.groups(("z", "x", "q")), tiled=True
        )


def total_of(*values):
    return sum(v.astype(f32) for v in values)


def lock(*values):
    return lax.optimization_barrier(values)


def behind(value, *others):
    return lax.optimization_barrier((value, others))[0]


def hbm(value):
    return pltpu.with_memory_space_constraint(value, pltpu.HBM)


def call(kernel, place, operands, **kw):
    spec = pltpu.PrefetchScalarGridSpec(
        num_scalar_prefetch=1,
        grid=kw.pop("grid"),
        in_specs=kw.pop("in_specs"),
        out_specs=kw.pop("out_specs"),
        scratch_shapes=kw.pop("scratch_shapes", []),
    )
    return pl.pallas_call(
        kernel,
        grid_spec=spec,
        compiler_params=pltpu.CompilerParams(vmem_limit_bytes=kw.pop("mib") * 2**20),
        **kw,
    )(place, *operands)


class Pieces:
    def __init__(self, grid, found):
        self.grid = grid
        self.found = found
        self.arrays = [f[0] for f in found]
        self.count = sum(f[0].shape[0] for f in found)

    def copies(self, place, refs, sem, moves):
        out = []
        for ref, (piece, at_chips) in zip(refs, self.found):
            for i, distance in enumerate(at_chips):
                chip = self.grid.chip(place, *distance)
                for at, rows, col, cols, to in moves:
                    source = ref.at[i, pl.ds(at, rows), pl.ds(col, cols)]
                    out.append(pltpu.make_async_copy(source, to(chip), sem.at[len(out)]))
        return out


class Whole:
    def __init__(self, arrays):
        self.arrays = arrays
        self.count = 1


def pick(grid, found, first, lanes):
    arrays = [f[0][:, first:, :lanes] for f in found]
    rows = arrays[0].shape[1]

    def kernel(place, *refs):
        for ref, (piece, at_chips) in zip(refs[:-1], found):
            for i, distance in enumerate(at_chips):
                refs[-1][grid.chip(place, *distance)] = ref[i]

    return call(
        kernel,
        grid.place,
        arrays,
        grid=(1,),
        in_specs=[pl.BlockSpec(a.shape, lambda i, s: (0, 0, 0)) for a in arrays],
        out_specs=pl.BlockSpec((grid.chips, rows, lanes), lambda i, s: (0, 0, 0)),
        out_shape=jax.ShapeDtypeStruct((grid.chips, rows, lanes), bf16),
        cost_estimate=SMALL,
        mib=8,
        name="pick",
    )


def vectors_kernel(place, small_ref, out_ref):
    rows, width = small_ref.shape[0], out_ref.shape[1]
    chips = rows // 16
    m = lax.broadcasted_iota(jnp.int32, (128, width), 0)
    j = lax.broadcasted_iota(jnp.int32, (128, width), 1)
    small = small_ref[...]
    narrow, wide = width // chips, 2 * width // chips
    spread = lambda n: mm(small, ((j % n) == m).astype(bf16)).reshape(chips, 16, width)
    one = lax.broadcasted_iota(jnp.int32, (chips, 16, width), 2)
    chip = lax.broadcasted_iota(jnp.int32, (chips, 16, width), 0)
    a, b = spread(narrow), spread(wide)
    plain = jnp.sum(jnp.where(one // narrow == chip, a, 0.0), axis=0)
    low = jnp.sum(jnp.where(one // wide == chip, b, 0.0), axis=0)
    high = jnp.sum(jnp.where(one // wide + chips // 2 == chip, b, 0.0), axis=0)
    out_ref[...] = jnp.concatenate(
        [plain[0:6], low[6:7], high[6:7], low[7:8], high[7:8], plain[0:6]], axis=0
    )


def vectors_of(grid, small, width):
    rows = small.shape[0]
    return call(
        vectors_kernel,
        grid.place,
        [small],
        grid=(1,),
        in_specs=[pl.BlockSpec((rows, 128), lambda i, s: (0, 0))],
        out_specs=pl.BlockSpec((16, width), lambda i, s: (0, 0)),
        out_shape=jax.ShapeDtypeStruct((16, width), f32),
        cost_estimate=SMALL,
        mib=8,
        name="vectors",
    )


def first_lanes(head):
    lane = lax.broadcasted_iota(jnp.int32, (1, 2 * HEAD_DIM), 1)
    return lane < HEAD_DIM if head == 0 else lane >= HEAD_DIM


def chunk_of(rows):
    return 1536 if rows % 1536 == 0 else rows


def attn_fwd_kernel(q_ref, k_ref, v_ref, hot_ref, pen_ref, o_ref, ob_ref, lse_ref):
    total_keys = k_ref.shape[0]
    chunk = chunk_of(total_keys)
    steps = total_keys // chunk
    query_rows = q_ref.shape[0]
    query, hot = q_ref[...], hot_ref[...]
    outs = []
    for head in range(2):
        sel = first_lanes(head)
        q_aug = jnp.where(sel, query, hot)

        def scores(rows):
            k_aug = jnp.where(sel, k_ref[rows, :], pen_ref[rows, :])
            return mm(k_aug, q_aug, ((1,), (1,)))

        def weigh(rows, s, top):
            p = jnp.exp2(s - top)
            added = mm(v_ref[rows, :], p.astype(bf16), ((0,), (0,)))
            return jnp.sum(p, axis=0, keepdims=True), added

        if steps == 1:
            s = scores(slice(0, chunk))
            top = jnp.max(s, axis=0, keepdims=True)
            total, acc = weigh(slice(0, chunk), s, top)
        else:

            def step(i, carry):
                top, total, acc = carry
                rows = pl.ds(pl.multiple_of(i * chunk, chunk), chunk)
                s = scores(rows)
                new_top = jnp.maximum(top, jnp.max(s, axis=0, keepdims=True))
                more, added = weigh(rows, s, new_top)
                fade = jnp.exp2(top - new_top)
                return new_top, total * fade + more, acc * fade + added

            top, total, acc = lax.fori_loop(
                0,
                steps,
                step,
                (
                    jnp.full((1, query_rows), -1e30, f32),
                    jnp.zeros((1, query_rows), f32),
                    jnp.zeros((2 * HEAD_DIM, query_rows), f32),
                ),
            )
        outs.append((acc / total)[head * HEAD_DIM : (head + 1) * HEAD_DIM])
        lse_ref[0, head : head + 1, :] = top + jnp.log2(total)
    out = jnp.concatenate(outs, axis=0).T
    o_ref[...] = out
    ob_ref[...] = out.astype(bf16)


def attn_fwd(queries, keys, values, hot, pen, start, pairs):
    rows, width = queries.shape[0], pairs * 128
    total_keys = keys.shape[0]
    pairs = width // 128
    block = rows
    cost = SMALL
    return pl.pallas_call(
        attn_fwd_kernel,
        grid=(pairs, rows // block),
        in_specs=[
            pl.BlockSpec((block, 128), lambda p, i: (i, p + start)),
            pl.BlockSpec((total_keys, 128), lambda p, i: (0, p + start)),
            pl.BlockSpec((total_keys, 128), lambda p, i: (0, p + start)),
            pl.BlockSpec((block, 128), lambda p, i: (i, 0)),
            pl.BlockSpec((total_keys, 128), lambda p, i: (0, 0)),
        ],
        out_specs=[
            pl.BlockSpec((block, 128), lambda p, i: (i, p)),
            pl.BlockSpec((block, 128), lambda p, i: (i, p)),
            pl.BlockSpec((1, 2, block), lambda p, i: (p, 0, i)),
        ],
        out_shape=[
            jax.ShapeDtypeStruct((rows, width), f32),
            jax.ShapeDtypeStruct((rows, width), bf16),
            jax.ShapeDtypeStruct((pairs, 2, rows), f32),
        ],
        compiler_params=pltpu.CompilerParams(vmem_limit_bytes=32 * 2**20),
        cost_estimate=cost,
        name="attn_fwd",
    )(queries, keys, values, hot, pen)


def attn_bwd_kernel(
    q_ref, k_ref, v_ref, hot_ref, pen_ref, o_ref, do_ref, lse_ref, dq_ref, dk_ref, dv_ref
):
    total_keys = k_ref.shape[0]
    chunk = chunk_of(total_keys)
    steps = total_keys // chunk
    query, hot, grad = q_ref[...], hot_ref[...], do_ref[...]
    flipped = (grad.astype(f32) * o_ref[...]).T
    zero = jnp.zeros_like(query)

    def step(rows):
        keys, values, pen = k_ref[rows, :], v_ref[rows, :], pen_ref[rows, :]
        dq, dk, dv = [], 0.0, 0.0
        for head in range(2):
            sel = first_lanes(head)
            lanes = slice(head * HEAD_DIM, (head + 1) * HEAD_DIM)
            delta = jnp.sum(flipped[lanes], axis=0, keepdims=True)
            k_aug = jnp.where(sel, keys, pen)
            s = mm(k_aug, jnp.where(sel, query, hot), ((1,), (1,)))
            p = jnp.exp2(s - lse_ref[0, head : head + 1, :])
            grad_h = jnp.where(sel, grad, zero)
            dp = mm(values, grad_h, ((1,), (1,)))
            ds = (p * (dp - delta)).astype(bf16)
            dv = dv + mm(p.astype(bf16), grad_h)
            dk = dk + mm(ds, jnp.where(sel, query, zero))
            dq.append(mm(keys, ds, ((0,), (0,)))[lanes])
        dk_ref[rows, :] = (dk * (1.0 / LOG2E)).astype(bf16)
        dv_ref[rows, :] = dv.astype(bf16)
        return jnp.concatenate(dq, axis=0)

    if steps == 1:
        dq = step(slice(0, chunk))
    else:
        dq = lax.fori_loop(
            0,
            steps,
            lambda i, total: total + step(pl.ds(pl.multiple_of(i * chunk, chunk), chunk)),
            jnp.zeros((2 * HEAD_DIM, query.shape[0]), f32),
        )
    dq_ref[...] = (dq.T * HEAD_DIM**-0.5).astype(bf16)


def attn_bwd(queries, keys, values, hot, pen, attended, d_attended, lse, start, pairs):
    rows = queries.shape[0]
    total_keys = keys.shape[0]
    block = rows
    by_query = pl.BlockSpec((block, 128), lambda p, i: (i, p + start))
    by_key = pl.BlockSpec((total_keys, 128), lambda p, i: (0, p + start))
    to_query = pl.BlockSpec((block, 128), lambda p, i: (i, p))
    to_key = pl.BlockSpec((total_keys, 128), lambda p, i: (0, p))
    width = pairs * 128
    cost = SMALL
    return pl.pallas_call(
        attn_bwd_kernel,
        grid=(pairs, rows // block),
        in_specs=[
            by_query,
            by_key,
            by_key,
            pl.BlockSpec((block, 128), lambda p, i: (i, 0)),
            pl.BlockSpec((total_keys, 128), lambda p, i: (0, 0)),
            by_query,
            by_query,
            pl.BlockSpec((1, 2, block), lambda p, i: (p + start, 0, i)),
        ],
        out_specs=[to_query, to_key, to_key],
        out_shape=[
            jax.ShapeDtypeStruct((rows, width), bf16),
            jax.ShapeDtypeStruct((total_keys, width), bf16),
            jax.ShapeDtypeStruct((total_keys, width), bf16),
        ],
        compiler_params=pltpu.CompilerParams(vmem_limit_bytes=40 * 2**20),
        cost_estimate=cost,
        name="attn_bwd",
    )(queries, keys, values, hot, pen, attended, d_attended, lse)


def halves(place, mine, other):
    first = place[3] == 0
    return jnp.where(first, mine, other), jnp.where(first, other, mine)


def load_all(copies):
    for c in copies:
        c.start()
    for c in copies:
        c.wait()


def qkv_kernel(weights, moves, place, x_ref, vec_ref, *refs):
    pieces, refs = refs[:-9], refs[-9:]
    q_ref, k_ref, v_ref, h1t_ref, n1_ref, rstd_ref, w_out, w_s, sem = refs
    half = q_ref.shape[1]
    width = x_ref.shape[1]
    step = pl.program_id(0)

    @pl.when(step == 0)
    def _():
        if isinstance(weights, Pieces):
            load_all(weights.copies(place, pieces, sem, moves(w_s)))
        else:
            load_all([pltpu.make_async_copy(pieces[0], w_s.at[0], sem.at[0])])
        w_out[...] = w_s[...]

    x = x_ref[...].astype(f32)
    centered = x - mean_of(x)
    rstd = lax.rsqrt(mean_of(centered * centered) + NORM_EPS)
    n1 = centered * rstd
    n1_ref[...] = n1.astype(bf16)
    rstd_ref[...] = rstd
    h1 = (n1 * vec_ref[0:1, :] + vec_ref[1:2, :]).astype(bf16)
    low, high = vec_ref[6:8, :half], vec_ref[6:8, half:]
    bias = jnp.where(place[3] == 0, low, high)
    w = w_s[...].reshape(width, 3 * half)

    @pl.when(step < 2)
    def _():
        q = mm(h1, w[:, :half]) + bias[0:1]
        q_ref[...] = (q * (LOG2E * HEAD_DIM**-0.5)).astype(bf16)

    kv = mm(h1, w[:, half:])
    k_ref[...] = kv[:, :half].astype(bf16)
    v_ref[...] = (kv[:, half:] + bias[1:2]).astype(bf16)
    h1t_ref[...] = h1.T


def project_qkv(grid, x, vec, weights, local):
    rows, width = x.shape
    half = width // 2
    if isinstance(weights, Pieces):
        r = width // grid.chips
        moves = lambda w: [(0, r, 0, 3 * half, lambda chip: w.at[chip])]
        shape = (grid.chips, r, 3 * half)
    else:
        moves = None
        shape = (1, width, 3 * half)
    *found, w = call(
        functools.partial(qkv_kernel, weights, moves),
        grid.place,
        [x, vec] + [hbm(w) for w in weights.arrays],
        grid=(rows // local,),
        in_specs=[
            pl.BlockSpec((local, width), lambda i, s: (i, 0)),
            pl.BlockSpec(vec.shape, lambda i, s: (0, 0)),
        ]
        + [pl.BlockSpec(memory_space=pl.ANY)] * len(weights.arrays),
        out_specs=[
            pl.BlockSpec((local, half), lambda i, s: (jnp.minimum(i, 1), 0)),
            pl.BlockSpec((local, half), lambda i, s: (i, 0)),
            pl.BlockSpec((local, half), lambda i, s: (i, 0)),
            pl.BlockSpec((width, local), lambda i, s: (0, i)),
            pl.BlockSpec((local, width), lambda i, s: (i, 0)),
            pl.BlockSpec((local, 1), lambda i, s: (i, 0)),
            pl.BlockSpec(shape, lambda i, s: (0, 0, 0)),
        ],
        out_shape=[
            jax.ShapeDtypeStruct((2 * local, half), bf16),
            jax.ShapeDtypeStruct((rows, half), bf16),
            jax.ShapeDtypeStruct((rows, half), bf16),
            pltpu.HBM((width, rows), bf16),
            pltpu.HBM((rows, width), bf16),
            pltpu.HBM((rows, 1), f32),
            pltpu.HBM(shape, bf16),
        ],
        scratch_shapes=[pltpu.VMEM(shape, bf16), pltpu.SemaphoreType.DMA((weights.count,))],
        cost_estimate=SMALL,
        mib=20,
        name="qkv",
    )
    return found + [w.reshape(width, 3 * half)]


def mean_of(v):
    return jnp.mean(v, axis=-1, keepdims=True)


def join(refs):
    return jnp.concatenate([r[...] for r in refs], axis=1)


def out_kernel(n, place, x_ref, w_ref, vec_ref, *refs):
    (after_ref, h2_ref, n2_ref, rstd_ref) = refs[2 * n :]
    a, b = halves(place, join(refs[:n]), join(refs[n : 2 * n]))
    after = x_ref[...].astype(f32) + mm(a, w_ref[0]) + mm(b, w_ref[1]) + vec_ref[2:3, :]
    after_ref[...] = after
    centered = after - mean_of(after)
    rstd = lax.rsqrt(mean_of(centered * centered) + NORM_EPS)
    n2 = centered * rstd
    n2_ref[...] = n2.astype(bf16)
    rstd_ref[...] = jnp.broadcast_to(rstd, rstd_ref.shape)
    h2_ref[...] = (n2 * vec_ref[3:4, :] + vec_ref[4:5, :]).astype(bf16)


def project_out(grid, x, mine, other, w, vec):
    rows, width = mine[0].shape[0], x.shape[1]
    block = 256 if rows % 256 == 0 else rows
    line = lambda n: pl.BlockSpec((block, n), lambda i, s: (i, 0))
    return call(
        functools.partial(out_kernel, len(mine)),
        grid.place,
        [x, w, vec] + mine + other,
        grid=(rows // block,),
        in_specs=[
            line(width),
            pl.BlockSpec(w.shape, lambda i, s: (0, 0, 0)),
            pl.BlockSpec(vec.shape, lambda i, s: (0, 0)),
        ]
        + [line(v.shape[1]) for v in mine + other],
        out_specs=[line(width), line(width), line(width), line(128)],
        out_shape=[
            pltpu.HBM((rows, width), f32),
            pltpu.HBM((rows, width), bf16),
            pltpu.HBM((rows, width), bf16),
            pltpu.HBM((rows, 128), f32),
        ],
        cost_estimate=SMALL,
        mib=16,
        name="out_proj",
    )


def norm_back(grad, normed, rstd, gain):
    e = grad * gain
    return (e - mean_of(e) - normed * mean_of(e * normed)) * rstd


def sum_rows(v):
    return jnp.sum(v, axis=0, keepdims=True)


def out_back_kernel(
    place, mine_ref, got_ref, dy_ref, n2_ref, rstd_ref, vec_ref, w_ref, after_ref, branch_ref, datt_ref, sums_ref
):
    d_h2 = mine_ref[...] + got_ref[...].astype(f32)
    dy = dy_ref[...].astype(f32)
    n2 = n2_ref[...].astype(f32)
    d_after = dy + norm_back(d_h2, n2, rstd_ref[:, 0:1], vec_ref[3:4, :])
    after_ref[...] = d_after
    branch = d_after.astype(bf16)
    branch_ref[...] = branch
    datt_ref[...] = mm(branch, w_ref[0], ((1,), (1,))).astype(bf16)
    rows = [sum_rows(branch.astype(f32)), sum_rows(d_h2 * n2), sum_rows(d_h2), sum_rows(dy)]
    sums = jnp.concatenate(rows + [jnp.zeros((4, dy.shape[1]), f32)], axis=0) * 0.5

    @pl.when(pl.program_id(0) == 0)
    def _():
        sums_ref[...] = jnp.zeros_like(sums_ref)

    sums_ref[...] += sums


def out_back(grid, mine, got, dy, n2, rstd, vec, w):
    rows, width = mine.shape
    block = 256 if rows % 256 == 0 else rows
    line = lambda n: pl.BlockSpec((block, n), lambda i, s: (i, 0))
    return call(
        out_back_kernel,
        grid.place,
        [mine, got, hbm(dy), hbm(n2), hbm(rstd), vec, hbm(w)],
        grid=(rows // block,),
        in_specs=[
            line(width),
            line(width),
            line(width),
            line(width),
            line(128),
            pl.BlockSpec(vec.shape, lambda i, s: (0, 0)),
            pl.BlockSpec((1,) + w.shape[1:], lambda i, s: (s[3], 0, 0)),
        ],
        out_specs=[
            line(width),
            line(width),
            line(width // 2),
            pl.BlockSpec((8, width), lambda i, s: (0, 0)),
        ],
        out_shape=[
            pltpu.HBM((rows, width), f32),
            jax.ShapeDtypeStruct((rows, width), bf16),
            jax.ShapeDtypeStruct((rows, width // 2), bf16),
            jax.ShapeDtypeStruct((8, width), f32),
        ],
        cost_estimate=SMALL,
        mib=20,
        name="out_back",
    )


def store_rows(grid, place, ref, value, shard, slot):
    for i in range(grid.chips):
        column, z = grid.relative(place, i, True)
        ref[column, z, slot, 0:shard, :] = value[i * shard : (i + 1) * shard]


def matrix_grads_kernel(grid, fast, n, parts, place, h1t_ref, d_ref, *refs):
    g_ref = refs[-1]
    mine, other, refs = refs[:n], refs[n : 2 * n], refs[2 * n : -1]
    flat = refs
    shard = h1t_ref.shape[0] // grid.chips
    slot = 0
    for part in range(parts):
        dq_ref, dk_ref, dv_ref = flat[3 * part : 3 * part + 3]
        chip_rows = dq_ref.shape[0]
        for p in range(dq_ref.shape[1] // 128):
            cols = slice(p * 128, (p + 1) * 128)
            gq = mm(h1t_ref[:, :chip_rows], dq_ref[:, cols])
            gkv = mm(h1t_ref[...], jnp.concatenate([dk_ref[:, cols], dv_ref[:, cols]], axis=1))
            g = jnp.concatenate([gq, gkv], axis=1).astype(bf16)
            if fast:
                store_rows(grid, place, g_ref, g, shard, slot)
            else:
                g_ref[slot] = g
            slot += 1
    a, b = halves(place, join(mine), join(other))
    g = mm(jnp.concatenate([a, b], axis=1), d_ref[...], ((0,), (0,))).astype(bf16)
    if fast:
        store_rows(grid, place, g_ref, g, shard, slot)
    else:
        g_ref[slot] = g


def matrix_gradients(grid, fast, h1t, branch, mine, other, grads):
    width = h1t.shape[0]
    rows, half = branch.shape[0], branch.shape[1] // 2
    slots = half // 128 + 1
    if fast:
        shape = (2 * grid.q, grid.z, slots, width // grid.chips, half)
    else:
        shape = (slots, width, half)
    flat = [v for part in grads for v in part]
    whole = lambda v: pl.BlockSpec(v.shape, lambda i, s: (0, 0))
    return call(
        functools.partial(matrix_grads_kernel, grid, fast, len(mine), len(grads)),
        grid.place,
        [hbm(h1t), branch] + mine + other + flat,
        grid=(1,),
        in_specs=[whole(h1t), pl.BlockSpec((rows, half), lambda i, s: (0, s[3]))]
        + [whole(v) for v in mine + other + flat],
        out_specs=pl.BlockSpec(shape, lambda i, s: (0,) * len(shape)),
        out_shape=pltpu.HBM(shape, bf16),
        cost_estimate=SMALL,
        mib=30,
        name="matrix_grads",
    )


def input_back_kernel(parts, place, *refs):
    grads, (w_ref, n1_ref, sums_ref, up_ref) = refs[: 3 * parts], refs[3 * parts : 3 * parts + 4]
    mine_ref, other_ref, vec_ref = refs[3 * parts + 4 :]
    step, last = pl.program_id(0), pl.num_programs(0) - 1
    dq, dk, dv = (
        jnp.concatenate([grads[3 * p + i][...] for p in range(parts)], axis=1) for i in range(3)
    )
    half = dq.shape[1]
    local, width = n1_ref.shape
    local = local // 2
    dq = jnp.where(step < 1, dq, jnp.zeros_like(dq))
    d = mm(jnp.concatenate([dq, dk, dv], axis=1), w_ref[...], ((1,), (1,)))
    to = pl.ds(pl.multiple_of(step * local, local), local)
    a, b = halves(place, d[:local], d[local:])
    mine_ref[to, :] = a
    other_ref[to, :] = b.astype(bf16)
    none = jnp.zeros((1, half), f32)
    first = place[3] == 0

    def spread(v):
        v = sum_rows(v.astype(f32))
        return jnp.concatenate([jnp.where(first, v, none), jnp.where(first, none, v)], axis=1)

    top = jnp.concatenate([sum_rows(d * n1_ref[...].astype(f32)), sum_rows(d)], axis=0)
    low = jnp.concatenate([spread(dq), spread(dv)], axis=0)

    @pl.when(step == 0)
    def _():
        up, no = up_ref[...], jnp.zeros_like(up_ref[...])
        ups = [jnp.where(first, up, no), jnp.where(first, no, up), jnp.zeros((4, width), f32)]
        vec_ref[...] = jnp.concatenate([top, sums_ref[0:4, :], low] + ups, axis=0)

    @pl.when(step > 0)
    def _():
        vec_ref[0:2, :] += top
        vec_ref[6:8, :] += low

    @pl.when(step == last)
    def _():
        at = other_ref.shape[0] - 16
        other_ref[at:, :] = vec_ref[...].astype(bf16)


def input_back(grid, grads, w, n1, sums, ups, local):
    rows, width = n1.shape
    flat = [g for part in grads for g in part]
    specs = []
    for dq, dk, dv in grads:
        n = dq.shape[1]
        specs.append(pl.BlockSpec((2 * local, n), lambda i, s: (0, 0)))
        specs += [pl.BlockSpec((2 * local, n), lambda i, s: (i, 0))] * 2
    whole = lambda shape: pl.BlockSpec(shape, lambda i, s: (0, 0))
    mine, other, vec = (grid.q * local, width), (grid.q * local + 16, width), (16, width)
    return call(
        functools.partial(input_back_kernel, len(grads)),
        grid.place,
        flat + [hbm(w), hbm(n1), sums, ups],
        grid=(grid.q,),
        in_specs=specs
        + [whole(w.shape), pl.BlockSpec((2 * local, width), lambda i, s: (i, 0))]
        + [whole(sums.shape), whole(ups.shape)],
        out_specs=[whole(mine), whole(other), whole(vec)],
        out_shape=[
            pltpu.HBM(mine, f32),
            jax.ShapeDtypeStruct(other, bf16),
            jax.ShapeDtypeStruct(vec, f32),
        ],
        cost_estimate=SMALL,
        mib=30,
        name="input_back",
    )


def finish_kernel(n_got, place, *refs):
    mine_ref, got_ref = refs[:2]
    sides = refs[2 : 2 + n_got]
    n1_ref, rstd_ref, after_ref, vec_ref, out_ref = refs[2 + n_got :]
    d = mine_ref[...] + got_ref[...].astype(f32)
    for s in sides:
        d = d + s[...].astype(f32)
    out_ref[...] = after_ref[...] + norm_back(
        d, n1_ref[...].astype(f32), rstd_ref[...], vec_ref[0:1, :]
    )


def finish(grid, mine, got, sides, n1, rstd1, d_after, vec):
    rows, width = n1.shape[0] // 2 // grid.q, n1.shape[1]
    first = pl.BlockSpec((rows, width), lambda i, s: (0, 0))
    own = lambda n: pl.BlockSpec((rows, n), lambda i, s: (s[3], 0))
    return call(
        functools.partial(finish_kernel, len(sides)),
        grid.place,
        [hbm(mine), got] + sides + [hbm(n1), rstd1, hbm(d_after), vec],
        grid=(1,),
        in_specs=[first, first]
        + [pl.BlockSpec((rows, width), lambda i, s: (0, 0))] * len(sides)
        + [own(width), own(1), own(width), pl.BlockSpec(vec.shape, lambda i, s: (0, 0))],
        out_specs=pl.BlockSpec((rows, width), lambda i, s: (0, 0)),
        out_shape=jax.ShapeDtypeStruct((rows, width), f32),
        cost_estimate=SMALL,
        mib=20,
        name="finish",
    )


def ff_kernel(grid, ups, downs, place, h2_ref, dy_ref, vec_ref, *refs):
    fast = isinstance(ups, Pieces)
    n_up, n = len(ups.arrays), len(ups.arrays) + len(downs.arrays)
    pieces, refs = refs[:n], refs[n:]
    if fast:
        g_ref, refs = refs[0], refs[1:]
    else:
        (gdown_ref, gup_ref), refs = refs[:2], refs[2:]
    gbias_ref, out_ref, dh_ref, dhb_ref, act_s, dhid_s, h2t_s, up_s, down_s, sem, down_sem = refs
    step = pl.program_id(0)
    rows, width = h2_ref.shape
    units = act_s.shape[1]
    part = 256 if rows % 256 == 0 else rows

    @pl.when(step == 0)
    def _():
        if fast:
            r = up_s.shape[2]
            copies = ups.copies(
                place,
                pieces[:n_up],
                sem,
                [
                    (0, r, 0, width, lambda chip: up_s.at[0, chip]),
                    (r, r, 0, width, lambda chip: up_s.at[1, chip]),
                ],
            )
        else:
            tile = pl.ds(0, units), pl.ds(units, units)
            copies = [
                pltpu.make_async_copy(pieces[0].at[:, tile[i]], up_s.at[i, 0], sem.at[i])
                for i in range(2)
            ]
        copies.append(pltpu.make_async_copy(pieces[n_up].at[:, place[3], pl.ds(0, down_s.shape[1])], down_s, down_sem.at[0]))
        for c in copies:
            c.start()
        h2t_s[...] = h2_ref[...].T
        for c in copies:
            c.wait()

    w_up = up_s[step].reshape(width, units)
    d = down_s.shape[0] // 2
    w_down = down_s[pl.ds(step * d, d)].reshape(units, width)
    bias = jnp.where(step == 0, vec_ref[8:9, :], vec_ref[9:10, :])
    for at in range(0, rows, part):
        here = slice(at, at + part)
        for col in range(0, units, 256):
            cols = slice(col, col + 256)
            hidden = mm(h2_ref[here, :], w_up[:, cols]) + bias[:, cols]
            phi = 0.5 * (1.0 + lax.erf(hidden * (0.5**0.5)))
            dens = jnp.exp(-0.5 * hidden * hidden) * (1.0 / math.sqrt(2.0 * math.pi))
            act_s[here, cols] = (hidden * phi).astype(bf16)
            d_act = mm(dy_ref[here, :], w_down[cols, :], ((1,), (1,)))
            dhid_s[here, cols] = (d_act * (phi + hidden * dens)).astype(bf16)
    act, d_hidden = act_s[...], dhid_s[...]
    gdown = mm(act, dy_ref[...], ((0,), (0,))).astype(bf16)
    gup = mm(h2t_s[...], d_hidden).astype(bf16)
    gbias_ref[0] = sum_rows(d_hidden.astype(f32))
    out = mm(act, w_down)
    dh = mm(d_hidden, w_up, ((1,), (1,)))
    if fast:
        down_shard = 2 * units // grid.chips
        up_shard = width // grid.chips
        half = grid.chips // 2
        for i in range(half):
            column, z = grid.relative(place, step * half + i, True)
            g_ref[column, z, 0:down_shard, :] = gdown[i * down_shard : (i + 1) * down_shard]
        for i in range(grid.chips):
            column, z = grid.relative(place, i, True)
            to = pl.multiple_of(down_shard + step * up_shard, 16)
            g_ref[column, z, pl.ds(to, up_shard), :] = gup[i * up_shard : (i + 1) * up_shard]
    else:
        gdown_ref[...] = gdown
        gup_ref[...] = gup

    @pl.when(step == 0)
    def _():
        out_ref[...] = out
        dh_ref[...] = dh

    @pl.when(step == 1)
    def _():
        out_ref[...] += out
        total = dh_ref[...] + dh
        dh_ref[...] = total
        dhb_ref[...] = total.astype(bf16)


def feed_forward(grid, h2, dy, ups, downs, vec, units):
    fast = isinstance(ups, Pieces)
    rows, width = h2.shape
    tile = units // 2
    chips = grid.chips
    whole = pl.BlockSpec((rows, width), lambda j, s: (0, 0))
    cols = pl.BlockSpec((width, tile), lambda j, s: (0, j))
    lines = pl.BlockSpec((tile, width), lambda j, s: (j, 0))
    if fast:
        shape = (2 * grid.q, grid.z, (units + width * 2) // chips, width)
        g_specs = [pl.BlockSpec(shape, lambda j, s: (0, 0, 0, 0))]
        g_shapes = [pltpu.HBM(shape, bf16)]
        up_shape = (2, chips, width // chips, tile)
    else:
        g_specs = [lines, cols]
        g_shapes = [
            jax.ShapeDtypeStruct((units, width), bf16),
            jax.ShapeDtypeStruct((width, units), bf16),
        ]
        up_shape = (2, 1, width, tile)
    return call(
        functools.partial(ff_kernel, grid, ups, downs),
        grid.place,
        [hbm(h2), hbm(dy), vec] + [hbm(w) for w in ups.arrays + downs.arrays],
        grid=(2,),
        in_specs=[whole, whole, pl.BlockSpec(vec.shape, lambda j, s: (0, 0))]
        + [pl.BlockSpec(memory_space=pl.ANY)] * len(ups.arrays + downs.arrays),
        out_specs=g_specs
        + [pl.BlockSpec((1, 1, tile), lambda j, s: (j, 0, 0)), whole, whole, whole],
        out_shape=g_shapes
        + [
            jax.ShapeDtypeStruct((2, 1, tile), f32),
            pltpu.HBM((rows, width), f32),
            jax.ShapeDtypeStruct((rows, width), f32),
            jax.ShapeDtypeStruct((rows, width), bf16),
        ],
        scratch_shapes=[
            pltpu.VMEM((rows, tile), bf16),
            pltpu.VMEM((rows, tile), bf16),
            pltpu.VMEM((width, rows), bf16),
            pltpu.VMEM(up_shape, bf16),
            pltpu.VMEM((chips, units // chips, width), bf16),
            pltpu.SemaphoreType.DMA((2 * ups.count,)),
            pltpu.SemaphoreType.DMA((downs.count,)),
        ],
        cost_estimate=SMALL,
        mib=40,
        name="feed_forward",
    )


def mine_and_other(place, mine_ref, other_ref, slot, first, shard):
    at = pl.ds(pl.multiple_of(first + shard * place[3], 8), shard)
    return halves(place, mine_ref[slot, at, :], other_ref[slot, at, :].astype(f32))


def last_ff_kernel(grid, shard, place, ff_ref, other_ref, up_ref, down_ref):
    width = ff_ref.shape[1]
    per_chip = down_ref.shape[0]
    down_ref[...] = ff_ref[:per_chip, :]
    half = grid.chips // 2
    for h in range(2):
        first = 2 * shard * h
        at = lambda n: pl.ds(pl.multiple_of(n + first + shard * place[3], 8), shard)
        a, b = halves(place, ff_ref[at(per_chip), :], other_ref[at(0), :].astype(f32))
        for i in range(half):
            to = (h * half + i) * 2 * per_chip
            cols = slice(i * per_chip, (i + 1) * per_chip)
            up_ref[:, to : to + 2 * per_chip] = jnp.concatenate([a[:, cols], b[:, cols]], axis=1)


def last_ff(grid, ff, other, shard):
    rows, width = ff.shape
    whole = lambda shape: pl.BlockSpec(shape, lambda i, s: (0, 0))
    up, down = (shard, 4 * width * 2 // 2), (rows - 4 * shard, width)
    return call(
        functools.partial(last_ff_kernel, grid, shard),
        grid.place,
        [ff, other],
        grid=(1,),
        in_specs=[whole(ff.shape), whole(other.shape)],
        out_specs=[whole(up), whole(down)],
        out_shape=[jax.ShapeDtypeStruct(up, f32), jax.ShapeDtypeStruct(down, f32)],
        cost_estimate=SMALL,
        mib=8,
        name="last_ff",
    )


def last_rest_kernel(
    grid, shard, place, own_ref, other_ref, vec_ref, qkv_ref, out_ref, six_ref, qv_ref, up_ref
):
    pairs, half = own_ref.shape[0] - 1, own_ref.shape[2]
    for p in range(pairs + 1):
        both = mine_and_other(place, own_ref, other_ref, p, 0, shard)
        for core, value in enumerate(both):
            if p == pairs:
                out_ref[:, core * half : (core + 1) * half] = value
                continue
            for t in range(3):
                to = 2 * half * t + half * core + 128 * p
                qkv_ref[:, to : to + 128] = value[:, 128 * t : 128 * (t + 1)]
    width = 2 * half
    vec = jnp.concatenate([vec_ref[0:16, :], vec_ref[16:32, :]], axis=1)
    chip = (place[0] * grid.x + place[1]) * grid.q + place[2]

    def cut(rows, start):
        lane = lax.broadcasted_iota(jnp.int32, (width, 128), 0)
        to = lax.broadcasted_iota(jnp.int32, (width, 128), 1)
        take = (lane == to + start).astype(f32)
        return lax.dot_general(
            rows,
            take,
            (((1,), (0,)), ((), ())),
            precision=lax.Precision.HIGHEST,
            preferred_element_type=f32,
        )

    me = chip * 2 + place[3]
    six_ref[...] = cut(vec[0:8], me * shard)[:, :shard]

    def long(low, high, start, ref):
        n = ref.shape[1]
        rows = jnp.where(start >= width, high, low)
        start = jnp.where(start >= width, start - width, start)
        ref[...] = cut(jnp.broadcast_to(rows, (8, width)), start)[0:1, :n]

    long(vec[6:7], vec[7:8], me * 2 * shard, qv_ref)
    first = place[3] == 0
    low, high = jnp.where(first, vec[8:9], vec[10:11]), jnp.where(first, vec[9:10], vec[11:12])
    long(low, high, chip * up_ref.shape[1], up_ref)


def last_rest(grid, own, other, vec, shard, per_chip):
    half = own.shape[2]
    whole = lambda shape: pl.BlockSpec(shape, lambda i, s: (0,) * len(shape))
    shapes = [(shard, 6 * half), (shard, 2 * half), (8, shard), (1, 2 * shard), (1, per_chip)]
    return call(
        functools.partial(last_rest_kernel, grid, shard),
        grid.place,
        [own, other, vec],
        grid=(1,),
        in_specs=[whole(own.shape), whole(other.shape), whole(vec.shape)],
        out_specs=[whole(s) for s in shapes],
        out_shape=[jax.ShapeDtypeStruct(s, f32) for s in shapes],
        cost_estimate=SMALL,
        mib=8,
        name="last_rest",
    )


def in_order(first, mine, other):
    return jnp.stack([jnp.where(first, mine, other), jnp.where(first, other, mine)])


def body(
    dp,
    blk,
    inputs,
    clip_ids,
    ln1_gain,
    ln1_bias,
    w_qkv,
    qv_bias,
    w_out,
    out_bias,
    ln2_gain,
    ln2_bias,
    w_up,
    up_bias,
    w_down,
    down_bias,
    out_grad,
):
    grid = Grid(dp, blk)
    core = grid.me["c"]
    first = core == 0
    chips = grid.chips
    width = inputs.shape[2]
    half = width // 2
    local = inputs.shape[1]
    chip_rows = 2 * local
    units = w_up.shape[1] // 2
    shard = w_qkv.shape[0]
    per_chip = units // chips
    fast = shard % 8 == 0 and per_chip % 16 == 0
    swap = lambda v: grid.shift(v, "c", 1)
    at_core = lambda v, dim=0: lax.dynamic_index_in_dim(v, core, dim, keepdims=False)
    not_core = lambda v, dim=0: lax.dynamic_index_in_dim(v, 1 - core, dim, keepdims=False)

    pad = jnp.zeros((16, width), bf16).at[0, :local].set(clip_ids[0].astype(bf16))
    mine = jnp.concatenate([inputs[0], pad], axis=0)
    dy_mine = out_grad[0]
    if fast:
        put = lambda v, n: jnp.zeros((128,), bf16).at[:n].set(v)
        place_at = lambda v: jnp.where(first, jnp.pad(v, (0, v.size)), jnp.pad(v, (v.size, 0)))
        vecs = [ln1_gain, ln1_bias, out_bias, ln2_gain, ln2_bias, down_bias, qv_bias]
        rows = jnp.stack([jnp.pad(place_at(v), (0, 128 - 2 * v.size)) for v in vecs])
        up_row = put(up_bias, per_chip)[None]
        blank = jnp.zeros((8, 128), bf16)
        mine_small = jnp.concatenate([rows, up_row, blank])
        their_small = jnp.concatenate([rows, jnp.zeros_like(up_row), blank])
        widen = lambda v: jnp.pad(v, ((0, 0), (0, 3 * half - 128)))
        split = w_qkv.reshape(shard, 3, 2, half)
        my_qkv = at_core(split, 2).reshape(shard, 3 * half)
        to_qkv = not_core(split, 2).reshape(shard, 3 * half)
        up_split = w_up.reshape(shard, chips, 2, per_chip)
        my_up = at_core(up_split, 2).reshape(shard, units)
        to_up = not_core(up_split, 2).reshape(shard, units)
        got = swap(jnp.concatenate([to_qkv, widen(their_small)]))
        pair = in_order(first, my_qkv, got[:shard])
        small_chip = mine_small + got[shard:, :128]
        qkv_piece = jnp.concatenate([pair.reshape(2 * shard, 3 * half), widen(small_chip)])

        lines = lax.all_gather(jnp.concatenate([w_down, w_out]), AXES, axis=0, tiled=False)
        full_out = lines[:, per_chip:].reshape(width, width)
        downs = Whole([lines.reshape(chips, 2, per_chip + shard, width)])
        qkv_piece, x_sent = lock(qkv_piece, mine)
        qkv_z = grid.along(qkv_piece, "z")
        x_far = grid.along(x_sent, "q")
        x_near = swap(x_sent)
        up_pair = in_order(first, my_up, swap(to_up)).reshape(2 * shard, units)
        up_piece = jnp.concatenate([up_pair[:, :width], up_pair[:, width:]])

        qkv_z, x_far, x_near, up_piece = lock(qkv_z, x_far, x_near, up_piece)
        qkv_line = grid.line(qkv_piece, qkv_z)
        qkv_over, qkv_sides = grid.shift(qkv_line, "x", 1), grid.along(qkv_line, "q")
        up_line = grid.exchange(jnp.broadcast_to(up_piece, (grid.z,) + up_piece.shape))
        x_both = [(mine, x_near)] + [(v, swap(v)) for v in x_far]
        dy_near = swap(dy_mine)

        qkv_over, qkv_sides, x_both, dy_near = lock(qkv_over, qkv_sides, x_both, dy_near)
        found = grid.found(
            qkv_line, qkv_over, qkv_sides, grid.corner_pieces(qkv_over, qkv_sides)
        )
        qkv_weights = Pieces(grid, found)
        small_all = pick(grid, found, 2 * shard, 128)
        vec = vectors_of(grid, small_all.reshape(chips * 16, 128), width)
    else:
        whole = lambda v: lax.all_gather(v, AXES, axis=0, tiled=True)
        full_qkv = at_core(whole(w_qkv).reshape(width, 3, 2, half), 2).reshape(width, 3 * half)
        qkv_weights = Whole([full_qkv])
        full_out = whole(w_out)
        full_up = at_core(whole(w_up).reshape(width, chips, 2, per_chip), 2).reshape(width, units)
        full_down = whole(w_down).reshape(chips, 2, per_chip, width)
        ups, downs = Whole([full_up]), Whole([full_down])
        up_all = at_core(whole(up_bias).reshape(chips, 2, per_chip), 1).reshape(2, width)
        singles = [ln1_gain, ln1_bias, out_bias, ln2_gain, ln2_bias, down_bias]
        vec = jnp.concatenate(
            [whole(v)[None] for v in singles]
            + [whole(qv_bias).reshape(2, width), up_all, jnp.zeros((6, width), bf16)]
        ).astype(f32)
        x_both = [(v, swap(v)) for v in [mine] + grid.along(mine, "q")]
        dy_near = swap(dy_mine)

    both = [in_order(first, *v) for v in x_both]
    token_rows = jnp.concatenate([b[:, :local].reshape(chip_rows, width) for b in both])
    clips = jnp.concatenate([b[:, local, :local].reshape(chip_rows) for b in both])
    lane = lax.broadcasted_iota(jnp.int32, (1, 128), 1) % HEAD_DIM
    same = clips[:, None].astype(jnp.int32) == lane
    hot = same[:chip_rows].astype(bf16)
    pen = jnp.where(same | (lane >= 8), 0.0, -1e30).astype(bf16)
    dy = in_order(first, dy_mine, dy_near).reshape(chip_rows, width)

    queries, keys, values, h1t, n1, rstd1, full_qkv = project_qkv(
        grid, token_rows, vec, qkv_weights, local
    )
    pairs = half // 128
    if fast:
        queries, up_line = lock(queries, up_line)
        up_over, up_sides = grid.shift(up_line, "x", 1), grid.along(up_line, "q")
    attended, att, lse = attn_fwd(queries, keys, values, hot, pen, 0, pairs)
    if fast:
        up_over, up_sides = behind((up_over, up_sides), att)
        corners = grid.corner_pieces(up_over, up_sides)
        ups = Pieces(grid, grid.found(up_line, up_over, up_sides, corners, True))
    att_mine, att_other = [att], [swap(att)]
    out_rows = full_out.reshape(2, half, width)
    after, h2, n2, rstd2 = project_out(grid, token_rows, att_mine, att_other, out_rows, vec)

    *g_ff, gbias, ff_out, dh, dh_b = feed_forward(grid, h2, dy, ups, downs, vec, units)
    d_after, d_branch, d_att, sums2 = out_back(grid, dh, swap(dh_b), dy, n2, rstd2, vec, out_rows)

    def back(d, a, n):
        return attn_bwd(queries, keys, values, hot, pen, attended, d, lse, a, n)

    by_core = lambda v: v.reshape(2, local, width)
    up_sums = gbias.reshape(2, width)
    grads = [back(d_att, 0, 1)]
    if fast:
        ff_over, ff_sides = grid.corners(g_ff[0], grads[0])
        d_att = behind(d_att, ff_over, ff_sides)
    grads.append(back(d_att, 1, pairs - 1))
    g_all = matrix_gradients(grid, fast, h1t, d_branch, att_mine, att_other, grads)
    if fast:
        ff_own = grid.edges(g_ff[0], ff_over, ff_sides, g_all)
        grads, g_all, ff_own = lock(grads, g_all, ff_own)
        ff_z = [grid.shift(ff_own[k], "z", k) for k in range(1, grid.z)]
    else:
        grads, g_all = lock(grads, g_all)
    d_mine, d_other, sums = input_back(grid, grads, full_qkv, n1, sums2, up_sums, local)
    if fast:
        over, sides = grid.corners(g_all, d_other)
        middle = grid.z // 2 - 1
        ends = ff_z[:middle] + ff_z[middle + 1 :]
        d_other, over, sides, ends = lock(d_other, over, sides, ends)
    d_got = swap(d_other)
    sent = [
        total_of(*(v[k * local : (k + 1) * local] for v in (d_mine, d_got))).astype(bf16)
        for k in range(1, grid.q)
    ]
    got = [grid.shift(s, "q", grid.q - k) for k, s in enumerate(sent, 1)]
    if fast:
        vectors = sums + d_got[grid.q * local :].astype(f32)
    ff_out = behind(ff_out, sent)
    out_got = swap(not_core(by_core(ff_out)).astype(bf16)).astype(f32)
    result = at_core(by_core(ff_out)) + out_got + at_core(by_core(after)) + vec[5:6]
    output = result.astype(bf16)[None]
    input_grad = finish(grid, d_mine, d_got, got, n1, rstd1, d_after, vec)[None]

    if fast:
        own = grid.edges(g_all, over, sides, (vectors, sent))
        ff = total_of(ff_own[0], behind(ff_z[middle], own), *ends)
        vectors = jnp.concatenate([vectors[:, :half], vectors[:, half:]]).astype(bf16)
        own, vectors = lock(own, vectors)
        vectors = jnp.broadcast_to(vectors, (grid.z,) + vectors.shape)
        w_up_g, w_down_g = last_ff(grid, ff, swap(ff[per_chip:].astype(bf16)), shard)
        own, vectors = grid.column_near(own, vectors, (output, w_up_g))
        vectors = vectors + behind(grid.shift(vectors, "x", 1), input_grad)
        vectors = vectors + sum(grid.along(vectors, "q"))
        w_qkv_g, w_out_g, six, qv_g, up_g = last_rest(
            grid, own, swap(own.astype(bf16)), vectors, shard, per_chip
        )
        qv_g, up_g = qv_g[0], up_g[0]
    else:
        reduce = lambda v: lax.psum_scatter(v, AXES, scatter_dimension=0, tiled=True)

        def spread(v, dim):
            v = v.astype(f32)
            zero = jnp.zeros_like(v)
            return jnp.stack([jnp.where(first, v, zero), jnp.where(first, zero, v)], axis=dim)

        gdown, gup = g_ff
        w_down_g = reduce(
            spread(gdown.reshape(chips, per_chip, width), 1).reshape(2 * units, width)
        )
        w_up_g = reduce(spread(gup.reshape(width, chips, per_chip), 2).reshape(width, 2 * units))
        w_out_g = reduce(spread(g_all[pairs], 1).reshape(width, width))
        per_pair = g_all[:pairs].reshape(pairs, width, 3, 128)
        per_pair = jnp.transpose(per_pair, (1, 2, 0, 3)).reshape(width, 3, half)
        w_qkv_g = reduce(spread(per_pair, 2).reshape(width, 6 * half))
        sums = lax.psum(sums, AXES)
        me = (lax.axis_index("dp") * blk) + lax.axis_index("blk")
        six = lax.dynamic_slice(sums, (0, me * shard), (6, shard))
        qv_g = lax.dynamic_slice(sums[6:8].reshape(2 * width), (me * 2 * shard,), (2 * shard,))
        up_g = at_core(sums[8:12].reshape(2, units))
        up_g = lax.dynamic_slice(up_g, (me // 2 * per_chip,), (per_chip,))

    return (
        output,
        input_grad,
        six[0],
        six[1],
        w_qkv_g,
        qv_g,
        w_out_g,
        six[2],
        six[3],
        six[4],
        w_up_g,
        up_g,
        w_down_g,
        six[5],
    )


def solution(mesh):
    both = P(("dp", "blk"))
    rows = P(("dp", "blk"), None)
    tokens = P("dp", "blk", None)
    return jax.shard_map(
        functools.partial(body, mesh.shape["dp"], mesh.shape["blk"]),
        mesh=mesh,
        in_specs=(
            tokens,
            P("dp", "blk"),
            both,
            both,
            rows,
            both,
            rows,
            both,
            both,
            both,
            rows,
            both,
            rows,
            both,
            tokens,
        ),
        out_specs=(
            tokens,
            tokens,
            both,
            both,
            rows,
            both,
            rows,
            both,
            both,
            both,
            rows,
            both,
            rows,
            both,
        ),
        check_vma=False,
    )
```

```python
import functools
import itertools
import math

import jax
import jax.numpy as jnp
from jax import lax
from jax.experimental import pallas as pl
from jax.experimental.pallas import tpu as pltpu
from jax.sharding import PartitionSpec as P

HEAD_DIM = 64
NORM_EPS = 1e-06
LOG2E = math.log2(math.e)
f32 = jnp.float32
bf16 = jnp.bfloat16
AXES = ("dp", "blk")


def mm(a, b, dims=((1,), (0,))):
    return lax.dot_general(a, b, (dims, ((), ())), preferred_element_type=f32)


SMALL = pl.CostEstimate(flops=1000, bytes_accessed=1000, transcendentals=0)


class Grid:
    def __init__(self, dp, blk):
        self.size = {"z": dp // 2, "x": 2, "q": blk // 2, "c": 2}
        self.z, self.x, self.q = dp // 2, 2, blk // 2
        self.chips = self.z * 2 * self.q
        me_dp, me_blk = lax.axis_index("dp"), lax.axis_index("blk")
        self.me = {"z": me_dp // 2, "x": me_dp % 2, "q": me_blk // 2, "c": me_blk % 2}
        self.place = jnp.stack([self.me[a] for a in ("z", "x", "q", "c")]).astype(jnp.int32)

    def flat(self, at):
        return ((at["z"] * self.x + at["x"]) * self.q + at["q"]) * 2 + at["c"]

    def shift(self, value, axis, step):
        pairs = []
        for z in range(self.z):
            for x in range(self.x):
                for q in range(self.q):
                    for c in range(2):
                        at = {"z": z, "x": x, "q": q, "c": c}
                        to = dict(at)
                        to[axis] = (at[axis] + step) % self.size[axis]
                        pairs.append((self.flat(at), self.flat(to)))
        return lax.ppermute(value, AXES, pairs)

    def chip(self, place, dz, dx, dq):
        z = -1 - dz if dz < 0 else lax.rem(place[0] + (self.z - dz), self.z)
        x = lax.rem(place[1] + (self.x - dx), self.x)
        q = lax.rem(place[2] + (self.q - dq), self.q)
        return (z * self.x + x) * self.q + q

    def relative(self, place, chip, near=False):
        z, x, q = chip // (self.x * self.q), chip // self.q % self.x, chip % self.q
        dx = lax.rem(x + self.x - place[1], self.x)
        dq = lax.rem(q + self.q - place[2], self.q)
        if near:
            z = lax.rem(z + self.z - place[0], self.z)
        return dx * self.q + dq, z

    def along(self, value, axis):
        return [self.shift(value, axis, k) for k in range(1, self.size[axis])]

    def line(self, value, others):
        return jnp.stack([value] + others)

    def corner_pieces(self, over, sides):
        half = self.z // 2
        return [
            (self.shift(over[:half], "q", k), self.shift(side[half:], "x", 1))
            for k, side in enumerate(sides, 1)
        ]

    def found(self, line, over, sides, corners, plain=False):
        half = self.z // 2
        zs = [-1 - z if plain else z for z in range(self.z)]
        out = [(line, [(z, 0, 0) for z in zs]), (over, [(z, 1, 0) for z in zs])]
        for k, (side, (a, b)) in enumerate(zip(sides, corners), 1):
            out.append((side, [(z, 0, k) for z in zs]))
            out.append((a, [(z, 1, k) for z in zs[:half]]))
            out.append((b, [(z, 1, k) for z in zs[half:]]))
        return out

    def found_last(self, plane, others):
        at = [(x, q) for x in range(2) for q in range(self.q)]
        return [(p, [(z, x, q) for x, q in at]) for z, p in enumerate([plane] + others)]


    def corners(self, value, first=()):
        half = self.z // 2
        over = value[self.q]
        late, sides = [], []
        for k in range(1, self.q):
            corner = value[self.q + k]
            got = behind(self.shift(corner[:half], "x", 1), first)
            late.append(behind(self.shift(corner[half:], "q", k), first))
            side = value[k]
            sides.append(jnp.concatenate([total_of(side[:half], got).astype(bf16), side[half:]]))
        over = jnp.concatenate([over[:half], total_of(over[half:], *late).astype(bf16)])
        return over, sides

    def edges(self, value, over, sides, first=()):
        parts = [self.shift(over, "x", 1)]
        parts += [self.shift(s, "q", k) for k, s in enumerate(sides, 1)]
        parts = behind(parts, first)
        return total_of(value[0], *parts).astype(bf16)

    def column(self, own):
        return total_of(*self.exchange(own))

    def column_near(self, own, vectors, first=()):
        size = own.shape[1] * own.shape[2]
        rows = jnp.concatenate([own.reshape(self.z, size, own.shape[3])] + [vectors], axis=1)
        got = behind([self.shift(rows[k], "z", k) for k in range(1, self.z)], first)
        total = total_of(own[0], *(v[:size].reshape(own.shape[1:]) for v in got))
        return total, total_of(vectors[0], *(v[size:] for v in got))

    def groups(self, axes):
        names = ("z", "x", "q", "c")
        rest = [n for n in names if n not in axes]
        out = []
        for fixed in itertools.product(*(range(self.size[n]) for n in rest)):
            at = dict(zip(rest, fixed))
            out.append(
                [
                    self.flat({**at, **dict(zip(axes, v))})
                    for v in itertools.product(*(range(self.size[n]) for n in axes))
                ]
            )
        return out

    def exchange(self, blocks):
        return lax.all_to_all(
            blocks, AXES, 0, 0, axis_index_groups=self.groups(("z",)), tiled=True
        )

    def gather_chips(self, value):
        return lax.all_gather(
            value, AXES, axis=0, axis_index_groups=self.groups(("z", "x", "q")), tiled=True
        )


def total_of(*values):
    return sum(v.astype(f32) for v in values)


def lock(*values):
    return lax.optimization_barrier(values)


def behind(value, *others):
    return lax.optimization_barrier((value, others))[0]


def hbm(value):
    return pltpu.with_memory_space_constraint(value, pltpu.HBM)


def call(kernel, place, operands, **kw):
    spec = pltpu.PrefetchScalarGridSpec(
        num_scalar_prefetch=1,
        grid=kw.pop("grid"),
        in_specs=kw.pop("in_specs"),
        out_specs=kw.pop("out_specs"),
        scratch_shapes=kw.pop("scratch_shapes", []),
    )
    return pl.pallas_call(
        kernel,
        grid_spec=spec,
        compiler_params=pltpu.CompilerParams(vmem_limit_bytes=kw.pop("mib") * 2**20),
        **kw,
    )(place, *operands)


class Pieces:
    def __init__(self, grid, found):
        self.grid = grid
        self.found = found
        self.arrays = [f[0] for f in found]
        self.count = sum(f[0].shape[0] for f in found)

    def copies(self, place, refs, sem, moves):
        out = []
        for ref, (piece, at_chips) in zip(refs, self.found):
            for i, distance in enumerate(at_chips):
                chip = self.grid.chip(place, *distance)
                for at, rows, col, cols, to in moves:
                    source = ref.at[i, pl.ds(at, rows), pl.ds(col, cols)]
                    out.append(pltpu.make_async_copy(source, to(chip), sem.at[len(out)]))
        return out


class Whole:
    def __init__(self, arrays):
        self.arrays = arrays
        self.count = 1


def pick(grid, found, first, lanes):
    arrays = [f[0][:, first:, :lanes] for f in found]
    rows = arrays[0].shape[1]

    def kernel(place, *refs):
        for ref, (piece, at_chips) in zip(refs[:-1], found):
            for i, distance in enumerate(at_chips):
                refs[-1][grid.chip(place, *distance)] = ref[i]

    return call(
        kernel,
        grid.place,
        arrays,
        grid=(1,),
        in_specs=[pl.BlockSpec(a.shape, lambda i, s: (0, 0, 0)) for a in arrays],
        out_specs=pl.BlockSpec((grid.chips, rows, lanes), lambda i, s: (0, 0, 0)),
        out_shape=jax.ShapeDtypeStruct((grid.chips, rows, lanes), bf16),
        cost_estimate=SMALL,
        mib=8,
        name="pick",
    )


def vectors_kernel(place, small_ref, out_ref):
    rows, width = small_ref.shape[0], out_ref.shape[1]
    chips = rows // 16
    m = lax.broadcasted_iota(jnp.int32, (128, width), 0)
    j = lax.broadcasted_iota(jnp.int32, (128, width), 1)
    small = small_ref[...]
    narrow, wide = width // chips, 2 * width // chips
    spread = lambda n: mm(small, ((j % n) == m).astype(bf16)).reshape(chips, 16, width)
    one = lax.broadcasted_iota(jnp.int32, (chips, 16, width), 2)
    chip = lax.broadcasted_iota(jnp.int32, (chips, 16, width), 0)
    a, b = spread(narrow), spread(wide)
    plain = jnp.sum(jnp.where(one // narrow == chip, a, 0.0), axis=0)
    low = jnp.sum(jnp.where(one // wide == chip, b, 0.0), axis=0)
    high = jnp.sum(jnp.where(one // wide + chips // 2 == chip, b, 0.0), axis=0)
    out_ref[...] = jnp.concatenate(
        [plain[0:6], low[6:7], high[6:7], low[7:8], high[7:8], plain[0:6]], axis=0
    )


def vectors_of(grid, small, width):
    rows = small.shape[0]
    return call(
        vectors_kernel,
        grid.place,
        [small],
        grid=(1,),
        in_specs=[pl.BlockSpec((rows, 128), lambda i, s: (0, 0))],
        out_specs=pl.BlockSpec((16, width), lambda i, s: (0, 0)),
        out_shape=jax.ShapeDtypeStruct((16, width), f32),
        cost_estimate=SMALL,
        mib=8,
        name="vectors",
    )


def first_lanes(head):
    lane = lax.broadcasted_iota(jnp.int32, (1, 2 * HEAD_DIM), 1)
    return lane < HEAD_DIM if head == 0 else lane >= HEAD_DIM


def chunk_of(rows):
    return 1536 if rows % 1536 == 0 else rows


def attn_fwd_kernel(q_ref, k_ref, v_ref, hot_ref, pen_ref, o_ref, ob_ref, lse_ref):
    total_keys = k_ref.shape[0]
    chunk = chunk_of(total_keys)
    steps = total_keys // chunk
    query_rows = q_ref.shape[0]
    query, hot = q_ref[...], hot_ref[...]
    outs = []
    for head in range(2):
        sel = first_lanes(head)
        q_aug = jnp.where(sel, query, hot)

        def scores(rows):
            k_aug = jnp.where(sel, k_ref[rows, :], pen_ref[rows, :])
            return mm(k_aug, q_aug, ((1,), (1,)))

        def weigh(rows, s, top):
            p = jnp.exp2(s - top)
            added = mm(v_ref[rows, :], p.astype(bf16), ((0,), (0,)))
            return jnp.sum(p, axis=0, keepdims=True), added

        if steps == 1:
            s = scores(slice(0, chunk))
            top = jnp.max(s, axis=0, keepdims=True)
            total, acc = weigh(slice(0, chunk), s, top)
        else:

            def step(i, carry):
                top, total, acc = carry
                rows = pl.ds(pl.multiple_of(i * chunk, chunk), chunk)
                s = scores(rows)
                new_top = jnp.maximum(top, jnp.max(s, axis=0, keepdims=True))
                more, added = weigh(rows, s, new_top)
                fade = jnp.exp2(top - new_top)
                return new_top, total * fade + more, acc * fade + added

            top, total, acc = lax.fori_loop(
                0,
                steps,
                step,
                (
                    jnp.full((1, query_rows), -1e30, f32),
                    jnp.zeros((1, query_rows), f32),
                    jnp.zeros((2 * HEAD_DIM, query_rows), f32),
                ),
            )
        outs.append((acc / total)[head * HEAD_DIM : (head + 1) * HEAD_DIM])
        lse_ref[0, head : head + 1, :] = top + jnp.log2(total)
    out = jnp.concatenate(outs, axis=0).T
    o_ref[...] = out
    ob_ref[...] = out.astype(bf16)


def attn_fwd(queries, keys, values, hot, pen, start, pairs):
    rows, width = queries.shape[0], pairs * 128
    total_keys = keys.shape[0]
    pairs = width // 128
    block = rows
    cost = SMALL
    return pl.pallas_call(
        attn_fwd_kernel,
        grid=(pairs, rows // block),
        in_specs=[
            pl.BlockSpec((block, 128), lambda p, i: (i, p + start)),
            pl.BlockSpec((total_keys, 128), lambda p, i: (0, p + start)),
            pl.BlockSpec((total_keys, 128), lambda p, i: (0, p + start)),
            pl.BlockSpec((block, 128), lambda p, i: (i, 0)),
            pl.BlockSpec((total_keys, 128), lambda p, i: (0, 0)),
        ],
        out_specs=[
            pl.BlockSpec((block, 128), lambda p, i: (i, p)),
            pl.BlockSpec((block, 128), lambda p, i: (i, p)),
            pl.BlockSpec((1, 2, block), lambda p, i: (p, 0, i)),
        ],
        out_shape=[
            pltpu.HBM((rows, width), f32),
            jax.ShapeDtypeStruct((rows, width), bf16),
            jax.ShapeDtypeStruct((pairs, 2, rows), f32),
        ],
        compiler_params=pltpu.CompilerParams(vmem_limit_bytes=32 * 2**20),
        cost_estimate=cost,
        name="attn_fwd",
    )(queries, keys, values, hot, pen)


def attn_bwd_kernel(
    q_ref, k_ref, v_ref, hot_ref, pen_ref, o_ref, do_ref, lse_ref, dq_ref, dk_ref, dv_ref
):
    total_keys = k_ref.shape[0]
    chunk = chunk_of(total_keys)
    steps = total_keys // chunk
    query, hot, grad = q_ref[...], hot_ref[...], do_ref[...]
    flipped = (grad.astype(f32) * o_ref[...]).T
    zero = jnp.zeros_like(query)

    def step(rows):
        keys, values, pen = k_ref[rows, :], v_ref[rows, :], pen_ref[rows, :]
        dq, dk, dv = [], 0.0, 0.0
        for head in range(2):
            sel = first_lanes(head)
            lanes = slice(head * HEAD_DIM, (head + 1) * HEAD_DIM)
            delta = jnp.sum(flipped[lanes], axis=0, keepdims=True)
            k_aug = jnp.where(sel, keys, pen)
            s = mm(k_aug, jnp.where(sel, query, hot), ((1,), (1,)))
            p = jnp.exp2(s - lse_ref[0, head : head + 1, :])
            grad_h = jnp.where(sel, grad, zero)
            dp = mm(values, grad_h, ((1,), (1,)))
            ds = (p * (dp - delta)).astype(bf16)
            dv = dv + mm(p.astype(bf16), grad_h)
            dk = dk + mm(ds, jnp.where(sel, query, zero))
            dq.append(mm(keys, ds, ((0,), (0,)))[lanes])
        dk_ref[rows, :] = (dk * (1.0 / LOG2E)).astype(bf16)
        dv_ref[rows, :] = dv.astype(bf16)
        return jnp.concatenate(dq, axis=0)

    if steps == 1:
        dq = step(slice(0, chunk))
    else:
        dq = lax.fori_loop(
            0,
            steps,
            lambda i, total: total + step(pl.ds(pl.multiple_of(i * chunk, chunk), chunk)),
            jnp.zeros((2 * HEAD_DIM, query.shape[0]), f32),
        )
    dq_ref[...] = (dq.T * HEAD_DIM**-0.5).astype(bf16)


def attn_bwd(queries, keys, values, hot, pen, attended, d_attended, lse, start, pairs):
    rows = queries.shape[0]
    total_keys = keys.shape[0]
    block = rows
    by_query = pl.BlockSpec((block, 128), lambda p, i: (i, p + start))
    by_key = pl.BlockSpec((total_keys, 128), lambda p, i: (0, p + start))
    to_query = pl.BlockSpec((block, 128), lambda p, i: (i, p))
    to_key = pl.BlockSpec((total_keys, 128), lambda p, i: (0, p))
    width = pairs * 128
    cost = SMALL
    return pl.pallas_call(
        attn_bwd_kernel,
        grid=(pairs, rows // block),
        in_specs=[
            by_query,
            by_key,
            by_key,
            pl.BlockSpec((block, 128), lambda p, i: (i, 0)),
            pl.BlockSpec((total_keys, 128), lambda p, i: (0, 0)),
            by_query,
            by_query,
            pl.BlockSpec((1, 2, block), lambda p, i: (p + start, 0, i)),
        ],
        out_specs=[to_query, to_key, to_key],
        out_shape=[
            jax.ShapeDtypeStruct((rows, width), bf16),
            jax.ShapeDtypeStruct((total_keys, width), bf16),
            jax.ShapeDtypeStruct((total_keys, width), bf16),
        ],
        compiler_params=pltpu.CompilerParams(vmem_limit_bytes=40 * 2**20),
        cost_estimate=cost,
        name="attn_bwd",
    )(queries, keys, values, hot, pen, attended, d_attended, lse)


def halves(place, mine, other):
    first = place[3] == 0
    return jnp.where(first, mine, other), jnp.where(first, other, mine)


def load_all(copies):
    for c in copies:
        c.start()
    for c in copies:
        c.wait()


def qkv_kernel(weights, moves, place, x_ref, vec_ref, *refs):
    pieces, refs = refs[:-9], refs[-9:]
    q_ref, k_ref, v_ref, h1t_ref, n1_ref, rstd_ref, w_out, w_s, sem = refs
    half = q_ref.shape[1]
    width = x_ref.shape[1]
    step = pl.program_id(0)

    @pl.when(step == 0)
    def _():
        if isinstance(weights, Pieces):
            load_all(weights.copies(place, pieces, sem, moves(w_s)))
        else:
            load_all([pltpu.make_async_copy(pieces[0], w_s.at[0], sem.at[0])])
        w_out[...] = w_s[...]

    x = x_ref[...].astype(f32)
    centered = x - mean_of(x)
    rstd = lax.rsqrt(mean_of(centered * centered) + NORM_EPS)
    n1 = centered * rstd
    n1_ref[...] = n1.astype(bf16)
    rstd_ref[...] = rstd
    h1 = (n1 * vec_ref[0:1, :] + vec_ref[1:2, :]).astype(bf16)
    low, high = vec_ref[6:8, :half], vec_ref[6:8, half:]
    bias = jnp.where(place[3] == 0, low, high)
    w = w_s[...].reshape(width, 3 * half)

    @pl.when(step < 2)
    def _():
        q = mm(h1, w[:, :half]) + bias[0:1]
        q_ref[...] = (q * (LOG2E * HEAD_DIM**-0.5)).astype(bf16)

    kv = mm(h1, w[:, half:])
    k_ref[...] = kv[:, :half].astype(bf16)
    v_ref[...] = (kv[:, half:] + bias[1:2]).astype(bf16)
    h1t_ref[...] = h1.T


def project_qkv(grid, x, vec, weights, local):
    rows, width = x.shape
    half = width // 2
    if isinstance(weights, Pieces):
        r = width // grid.chips
        moves = lambda w: [(0, r, 0, 3 * half, lambda chip: w.at[chip])]
        shape = (grid.chips, r, 3 * half)
    else:
        moves = None
        shape = (1, width, 3 * half)
    *found, w = call(
        functools.partial(qkv_kernel, weights, moves),
        grid.place,
        [x, vec] + [hbm(w) for w in weights.arrays],
        grid=(rows // local,),
        in_specs=[
            pl.BlockSpec((local, width), lambda i, s: (i, 0)),
            pl.BlockSpec(vec.shape, lambda i, s: (0, 0)),
        ]
        + [pl.BlockSpec(memory_space=pl.ANY)] * len(weights.arrays),
        out_specs=[
            pl.BlockSpec((local, half), lambda i, s: (jnp.minimum(i, 1), 0)),
            pl.BlockSpec((local, half), lambda i, s: (i, 0)),
            pl.BlockSpec((local, half), lambda i, s: (i, 0)),
            pl.BlockSpec((width, local), lambda i, s: (0, i)),
            pl.BlockSpec((local, width), lambda i, s: (i, 0)),
            pl.BlockSpec((local, 1), lambda i, s: (i, 0)),
            pl.BlockSpec(shape, lambda i, s: (0, 0, 0)),
        ],
        out_shape=[
            pltpu.HBM((2 * local, half), bf16),
            pltpu.HBM((rows, half), bf16),
            pltpu.HBM((rows, half), bf16),
            pltpu.HBM((width, rows), bf16),
            pltpu.HBM((rows, width), bf16),
            pltpu.HBM((rows, 1), f32),
            pltpu.HBM(shape, bf16),
        ],
        scratch_shapes=[pltpu.VMEM(shape, bf16), pltpu.SemaphoreType.DMA((weights.count,))],
        cost_estimate=SMALL,
        mib=20,
        name="qkv",
    )
    return found + [w.reshape(width, 3 * half)]


def mean_of(v):
    return jnp.mean(v, axis=-1, keepdims=True)


def join(refs):
    return jnp.concatenate([r[...] for r in refs], axis=1)


def out_kernel(n, place, x_ref, w_ref, vec_ref, *refs):
    (after_ref, h2_ref, n2_ref, rstd_ref) = refs[2 * n :]
    a, b = halves(place, join(refs[:n]), join(refs[n : 2 * n]))
    after = x_ref[...].astype(f32) + mm(a, w_ref[0]) + mm(b, w_ref[1]) + vec_ref[2:3, :]
    after_ref[...] = after
    centered = after - mean_of(after)
    rstd = lax.rsqrt(mean_of(centered * centered) + NORM_EPS)
    n2 = centered * rstd
    n2_ref[...] = n2.astype(bf16)
    rstd_ref[...] = jnp.broadcast_to(rstd, rstd_ref.shape)
    h2_ref[...] = (n2 * vec_ref[3:4, :] + vec_ref[4:5, :]).astype(bf16)


def project_out(grid, x, mine, other, w, vec):
    rows, width = mine[0].shape[0], x.shape[1]
    block = 256 if rows % 256 == 0 else rows
    line = lambda n: pl.BlockSpec((block, n), lambda i, s: (i, 0))
    return call(
        functools.partial(out_kernel, len(mine)),
        grid.place,
        [x, w, vec] + mine + other,
        grid=(rows // block,),
        in_specs=[
            line(width),
            pl.BlockSpec(w.shape, lambda i, s: (0, 0, 0)),
            pl.BlockSpec(vec.shape, lambda i, s: (0, 0)),
        ]
        + [line(v.shape[1]) for v in mine + other],
        out_specs=[line(width), line(width), line(width), line(128)],
        out_shape=[
            pltpu.HBM((rows, width), f32),
            pltpu.HBM((rows, width), bf16),
            pltpu.HBM((rows, width), bf16),
            pltpu.HBM((rows, 128), f32),
        ],
        cost_estimate=SMALL,
        mib=16,
        name="out_proj",
    )


def norm_back(grad, normed, rstd, gain):
    e = grad * gain
    return (e - mean_of(e) - normed * mean_of(e * normed)) * rstd


def sum_rows(v):
    return jnp.sum(v, axis=0, keepdims=True)


def out_back_kernel(
    place, mine_ref, got_ref, dy_ref, n2_ref, rstd_ref, vec_ref, w_ref, after_ref, branch_ref, datt_ref, sums_ref
):
    d_h2 = mine_ref[...] + got_ref[...].astype(f32)
    dy = dy_ref[...].astype(f32)
    n2 = n2_ref[...].astype(f32)
    d_after = dy + norm_back(d_h2, n2, rstd_ref[:, 0:1], vec_ref[3:4, :])
    after_ref[...] = d_after
    branch = d_after.astype(bf16)
    branch_ref[...] = branch
    datt_ref[...] = mm(branch, w_ref[0], ((1,), (1,))).astype(bf16)
    rows = [sum_rows(branch.astype(f32)), sum_rows(d_h2 * n2), sum_rows(d_h2), sum_rows(dy)]
    sums = jnp.concatenate(rows + [jnp.zeros((4, dy.shape[1]), f32)], axis=0) * 0.5

    @pl.when(pl.program_id(0) == 0)
    def _():
        sums_ref[...] = jnp.zeros_like(sums_ref)

    sums_ref[...] += sums


def out_back(grid, mine, got, dy, n2, rstd, vec, w):
    rows, width = mine.shape
    block = 256 if rows % 256 == 0 else rows
    line = lambda n: pl.BlockSpec((block, n), lambda i, s: (i, 0))
    return call(
        out_back_kernel,
        grid.place,
        [mine, got, dy, n2, rstd, vec, w],
        grid=(rows // block,),
        in_specs=[
            line(width),
            line(width),
            line(width),
            line(width),
            line(128),
            pl.BlockSpec(vec.shape, lambda i, s: (0, 0)),
            pl.BlockSpec((1,) + w.shape[1:], lambda i, s: (s[3], 0, 0)),
        ],
        out_specs=[
            line(width),
            line(width),
            line(width // 2),
            pl.BlockSpec((8, width), lambda i, s: (0, 0)),
        ],
        out_shape=[
            pltpu.HBM((rows, width), f32),
            jax.ShapeDtypeStruct((rows, width), bf16),
            jax.ShapeDtypeStruct((rows, width // 2), bf16),
            jax.ShapeDtypeStruct((8, width), f32),
        ],
        cost_estimate=SMALL,
        mib=20,
        name="out_back",
    )


def store_rows(grid, place, ref, value, shard, slot):
    for i in range(grid.chips):
        column, z = grid.relative(place, i, True)
        ref[column, z, slot, 0:shard, :] = value[i * shard : (i + 1) * shard]


def matrix_grads_kernel(grid, fast, n, parts, place, h1t_ref, d_ref, *refs):
    g_ref = refs[-1]
    mine, other, refs = refs[:n], refs[n : 2 * n], refs[2 * n : -1]
    flat = refs
    shard = h1t_ref.shape[0] // grid.chips
    slot = 0
    for part in range(parts):
        dq_ref, dk_ref, dv_ref = flat[3 * part : 3 * part + 3]
        chip_rows = dq_ref.shape[0]
        for p in range(dq_ref.shape[1] // 128):
            cols = slice(p * 128, (p + 1) * 128)
            gq = mm(h1t_ref[:, :chip_rows], dq_ref[:, cols])
            gkv = mm(h1t_ref[...], jnp.concatenate([dk_ref[:, cols], dv_ref[:, cols]], axis=1))
            g = jnp.concatenate([gq, gkv], axis=1).astype(bf16)
            if fast:
                store_rows(grid, place, g_ref, g, shard, slot)
            else:
                g_ref[slot] = g
            slot += 1
    a, b = halves(place, join(mine), join(other))
    g = mm(jnp.concatenate([a, b], axis=1), d_ref[...], ((0,), (0,))).astype(bf16)
    if fast:
        store_rows(grid, place, g_ref, g, shard, slot)
    else:
        g_ref[slot] = g


def matrix_gradients(grid, fast, h1t, branch, mine, other, grads):
    width = h1t.shape[0]
    rows, half = branch.shape[0], branch.shape[1] // 2
    slots = half // 128 + 1
    if fast:
        shape = (2 * grid.q, grid.z, slots, width // grid.chips, half)
    else:
        shape = (slots, width, half)
    flat = [v for part in grads for v in part]
    whole = lambda v: pl.BlockSpec(v.shape, lambda i, s: (0, 0))
    return call(
        functools.partial(matrix_grads_kernel, grid, fast, len(mine), len(grads)),
        grid.place,
        [hbm(h1t), branch] + mine + other + flat,
        grid=(1,),
        in_specs=[whole(h1t), pl.BlockSpec((rows, half), lambda i, s: (0, s[3]))]
        + [whole(v) for v in mine + other + flat],
        out_specs=pl.BlockSpec(shape, lambda i, s: (0,) * len(shape)),
        out_shape=pltpu.HBM(shape, bf16),
        cost_estimate=SMALL,
        mib=30,
        name="matrix_grads",
    )


def input_back_kernel(parts, place, *refs):
    grads, (w_ref, n1_ref, sums_ref, up_ref) = refs[: 3 * parts], refs[3 * parts : 3 * parts + 4]
    mine_ref, other_ref, vec_ref = refs[3 * parts + 4 :]
    step, last = pl.program_id(0), pl.num_programs(0) - 1
    dq, dk, dv = (
        jnp.concatenate([grads[3 * p + i][...] for p in range(parts)], axis=1) for i in range(3)
    )
    half = dq.shape[1]
    local, width = n1_ref.shape
    local = local // 2
    dq = jnp.where(step < 1, dq, jnp.zeros_like(dq))
    d = mm(jnp.concatenate([dq, dk, dv], axis=1), w_ref[...], ((1,), (1,)))
    to = pl.ds(pl.multiple_of(step * local, local), local)
    a, b = halves(place, d[:local], d[local:])
    mine_ref[to, :] = a
    other_ref[to, :] = b.astype(bf16)
    none = jnp.zeros((1, half), f32)
    first = place[3] == 0

    def spread(v):
        v = sum_rows(v.astype(f32))
        return jnp.concatenate([jnp.where(first, v, none), jnp.where(first, none, v)], axis=1)

    top = jnp.concatenate([sum_rows(d * n1_ref[...].astype(f32)), sum_rows(d)], axis=0)
    low = jnp.concatenate([spread(dq), spread(dv)], axis=0)

    @pl.when(step == 0)
    def _():
        up, no = up_ref[...], jnp.zeros_like(up_ref[...])
        ups = [jnp.where(first, up, no), jnp.where(first, no, up), jnp.zeros((4, width), f32)]
        vec_ref[...] = jnp.concatenate([top, sums_ref[0:4, :], low] + ups, axis=0)

    @pl.when(step > 0)
    def _():
        vec_ref[0:2, :] += top
        vec_ref[6:8, :] += low

    @pl.when(step == last)
    def _():
        at = other_ref.shape[0] - 16
        other_ref[at:, :] = vec_ref[...].astype(bf16)


def input_back(grid, grads, w, n1, sums, ups, local):
    rows, width = n1.shape
    flat = [g for part in grads for g in part]
    specs = []
    for dq, dk, dv in grads:
        n = dq.shape[1]
        specs.append(pl.BlockSpec((2 * local, n), lambda i, s: (0, 0)))
        specs += [pl.BlockSpec((2 * local, n), lambda i, s: (i, 0))] * 2
    whole = lambda shape: pl.BlockSpec(shape, lambda i, s: (0, 0))
    mine, other, vec = (grid.q * local, width), (grid.q * local + 16, width), (16, width)
    return call(
        functools.partial(input_back_kernel, len(grads)),
        grid.place,
        flat + [hbm(w), hbm(n1), sums, ups],
        grid=(grid.q,),
        in_specs=specs
        + [whole(w.shape), pl.BlockSpec((2 * local, width), lambda i, s: (i, 0))]
        + [whole(sums.shape), whole(ups.shape)],
        out_specs=[whole(mine), whole(other), whole(vec)],
        out_shape=[
            pltpu.HBM(mine, f32),
            jax.ShapeDtypeStruct(other, bf16),
            jax.ShapeDtypeStruct(vec, f32),
        ],
        cost_estimate=SMALL,
        mib=30,
        name="input_back",
    )


def finish_kernel(n_got, place, *refs):
    mine_ref, got_ref = refs[:2]
    sides = refs[2 : 2 + n_got]
    n1_ref, rstd_ref, after_ref, vec_ref, out_ref = refs[2 + n_got :]
    d = mine_ref[...] + got_ref[...].astype(f32)
    for s in sides:
        d = d + s[...].astype(f32)
    out_ref[...] = after_ref[...] + norm_back(
        d, n1_ref[...].astype(f32), rstd_ref[...], vec_ref[0:1, :]
    )


def finish(grid, mine, got, sides, n1, rstd1, d_after, vec):
    rows, width = n1.shape[0] // 2 // grid.q, n1.shape[1]
    first = pl.BlockSpec((rows, width), lambda i, s: (0, 0))
    own = lambda n: pl.BlockSpec((rows, n), lambda i, s: (s[3], 0))
    return call(
        functools.partial(finish_kernel, len(sides)),
        grid.place,
        [hbm(mine), got] + sides + [hbm(n1), rstd1, hbm(d_after), vec],
        grid=(1,),
        in_specs=[first, first]
        + [pl.BlockSpec((rows, width), lambda i, s: (0, 0))] * len(sides)
        + [own(width), own(1), own(width), pl.BlockSpec(vec.shape, lambda i, s: (0, 0))],
        out_specs=pl.BlockSpec((rows, width), lambda i, s: (0, 0)),
        out_shape=jax.ShapeDtypeStruct((rows, width), f32),
        cost_estimate=SMALL,
        mib=20,
        name="finish",
    )


def ff_kernel(grid, ups, downs, place, h2_ref, dy_ref, vec_ref, *refs):
    fast = isinstance(ups, Pieces)
    n_up, n = len(ups.arrays), len(ups.arrays) + len(downs.arrays)
    pieces, refs = refs[:n], refs[n:]
    if fast:
        g_ref, refs = refs[0], refs[1:]
    else:
        (gdown_ref, gup_ref), refs = refs[:2], refs[2:]
    gbias_ref, out_ref, dh_ref, dhb_ref, act_s, dhid_s, h2t_s, up_s, down_s, sem, down_sem = refs
    step = pl.program_id(0)
    rows, width = h2_ref.shape
    units = act_s.shape[1]
    part = 256 if rows % 256 == 0 else rows

    @pl.when(step == 0)
    def _():
        if fast:
            r = up_s.shape[2]
            copies = ups.copies(
                place,
                pieces[:n_up],
                sem,
                [
                    (0, r, 0, width, lambda chip: up_s.at[0, chip]),
                    (r, r, 0, width, lambda chip: up_s.at[1, chip]),
                ],
            )
        else:
            tile = pl.ds(0, units), pl.ds(units, units)
            copies = [
                pltpu.make_async_copy(pieces[0].at[:, tile[i]], up_s.at[i, 0], sem.at[i])
                for i in range(2)
            ]
        copies.append(pltpu.make_async_copy(pieces[n_up].at[:, place[3], pl.ds(0, down_s.shape[1])], down_s, down_sem.at[0]))
        for c in copies:
            c.start()
        h2t_s[...] = h2_ref[...].T
        for c in copies:
            c.wait()

    w_up = up_s[step].reshape(width, units)
    d = down_s.shape[0] // 2
    w_down = down_s[pl.ds(step * d, d)].reshape(units, width)
    bias = jnp.where(step == 0, vec_ref[8:9, :], vec_ref[9:10, :])
    for at in range(0, rows, part):
        here = slice(at, at + part)
        for col in range(0, units, 256):
            cols = slice(col, col + 256)
            hidden = mm(h2_ref[here, :], w_up[:, cols]) + bias[:, cols]
            phi = 0.5 * (1.0 + lax.erf(hidden * (0.5**0.5)))
            dens = jnp.exp(-0.5 * hidden * hidden) * (1.0 / math.sqrt(2.0 * math.pi))
            act_s[here, cols] = (hidden * phi).astype(bf16)
            d_act = mm(dy_ref[here, :], w_down[cols, :], ((1,), (1,)))
            dhid_s[here, cols] = (d_act * (phi + hidden * dens)).astype(bf16)
    act, d_hidden = act_s[...], dhid_s[...]
    gdown = mm(act, dy_ref[...], ((0,), (0,))).astype(bf16)
    gup = mm(h2t_s[...], d_hidden).astype(bf16)
    gbias_ref[0] = sum_rows(d_hidden.astype(f32))
    out = mm(act, w_down)
    dh = mm(d_hidden, w_up, ((1,), (1,)))
    if fast:
        down_shard = 2 * units // grid.chips
        up_shard = width // grid.chips
        half = grid.chips // 2
        for i in range(half):
            column, z = grid.relative(place, step * half + i, True)
            g_ref[column, z, 0:down_shard, :] = gdown[i * down_shard : (i + 1) * down_shard]
        for i in range(grid.chips):
            column, z = grid.relative(place, i, True)
            to = pl.multiple_of(down_shard + step * up_shard, 16)
            g_ref[column, z, pl.ds(to, up_shard), :] = gup[i * up_shard : (i + 1) * up_shard]
    else:
        gdown_ref[...] = gdown
        gup_ref[...] = gup

    @pl.when(step == 0)
    def _():
        out_ref[...] = out
        dh_ref[...] = dh

    @pl.when(step == 1)
    def _():
        out_ref[...] += out
        total = dh_ref[...] + dh
        dh_ref[...] = total
        dhb_ref[...] = total.astype(bf16)


def feed_forward(grid, h2, dy, ups, downs, vec, units):
    fast = isinstance(ups, Pieces)
    rows, width = h2.shape
    tile = units // 2
    chips = grid.chips
    whole = pl.BlockSpec((rows, width), lambda j, s: (0, 0))
    cols = pl.BlockSpec((width, tile), lambda j, s: (0, j))
    lines = pl.BlockSpec((tile, width), lambda j, s: (j, 0))
    if fast:
        shape = (2 * grid.q, grid.z, (units + width * 2) // chips, width)
        g_specs = [pl.BlockSpec(shape, lambda j, s: (0, 0, 0, 0))]
        g_shapes = [pltpu.HBM(shape, bf16)]
        up_shape = (2, chips, width // chips, tile)
    else:
        g_specs = [lines, cols]
        g_shapes = [
            jax.ShapeDtypeStruct((units, width), bf16),
            jax.ShapeDtypeStruct((width, units), bf16),
        ]
        up_shape = (2, 1, width, tile)
    return call(
        functools.partial(ff_kernel, grid, ups, downs),
        grid.place,
        [hbm(h2), hbm(dy), vec] + [hbm(w) for w in ups.arrays + downs.arrays],
        grid=(2,),
        in_specs=[whole, whole, pl.BlockSpec(vec.shape, lambda j, s: (0, 0))]
        + [pl.BlockSpec(memory_space=pl.ANY)] * len(ups.arrays + downs.arrays),
        out_specs=g_specs
        + [pl.BlockSpec((1, 1, tile), lambda j, s: (j, 0, 0)), whole, whole, whole],
        out_shape=g_shapes
        + [
            jax.ShapeDtypeStruct((2, 1, tile), f32),
            pltpu.HBM((rows, width), f32),
            jax.ShapeDtypeStruct((rows, width), f32),
            jax.ShapeDtypeStruct((rows, width), bf16),
        ],
        scratch_shapes=[
            pltpu.VMEM((rows, tile), bf16),
            pltpu.VMEM((rows, tile), bf16),
            pltpu.VMEM((width, rows), bf16),
            pltpu.VMEM(up_shape, bf16),
            pltpu.VMEM((chips, units // chips, width), bf16),
            pltpu.SemaphoreType.DMA((2 * ups.count,)),
            pltpu.SemaphoreType.DMA((downs.count,)),
        ],
        cost_estimate=SMALL,
        mib=40,
        name="feed_forward",
    )


def mine_and_other(place, mine_ref, other_ref, slot, first, shard):
    at = pl.ds(pl.multiple_of(first + shard * place[3], 8), shard)
    return halves(place, mine_ref[slot, at, :], other_ref[slot, at, :].astype(f32))


def last_ff_kernel(grid, shard, place, ff_ref, other_ref, up_ref, down_ref):
    width = ff_ref.shape[1]
    per_chip = down_ref.shape[0]
    down_ref[...] = ff_ref[:per_chip, :]
    half = grid.chips // 2
    for h in range(2):
        first = 2 * shard * h
        at = lambda n: pl.ds(pl.multiple_of(n + first + shard * place[3], 8), shard)
        a, b = halves(place, ff_ref[at(per_chip), :], other_ref[at(0), :].astype(f32))
        for i in range(half):
            to = (h * half + i) * 2 * per_chip
            cols = slice(i * per_chip, (i + 1) * per_chip)
            up_ref[:, to : to + 2 * per_chip] = jnp.concatenate([a[:, cols], b[:, cols]], axis=1)


def last_ff(grid, ff, other, shard):
    rows, width = ff.shape
    whole = lambda shape: pl.BlockSpec(shape, lambda i, s: (0, 0))
    up, down = (shard, 4 * width * 2 // 2), (rows - 4 * shard, width)
    return call(
        functools.partial(last_ff_kernel, grid, shard),
        grid.place,
        [ff, other],
        grid=(1,),
        in_specs=[whole(ff.shape), whole(other.shape)],
        out_specs=[whole(up), whole(down)],
        out_shape=[jax.ShapeDtypeStruct(up, f32), jax.ShapeDtypeStruct(down, f32)],
        cost_estimate=SMALL,
        mib=8,
        name="last_ff",
    )


def last_rest_kernel(
    grid, shard, place, own_ref, other_ref, vec_ref, qkv_ref, out_ref, six_ref, qv_ref, up_ref
):
    pairs, half = own_ref.shape[0] - 1, own_ref.shape[2]
    for p in range(pairs + 1):
        both = mine_and_other(place, own_ref, other_ref, p, 0, shard)
        for core, value in enumerate(both):
            if p == pairs:
                out_ref[:, core * half : (core + 1) * half] = value
                continue
            for t in range(3):
                to = 2 * half * t + half * core + 128 * p
                qkv_ref[:, to : to + 128] = value[:, 128 * t : 128 * (t + 1)]
    width = 2 * half
    vec = jnp.concatenate([vec_ref[0:16, :], vec_ref[16:32, :]], axis=1)
    chip = (place[0] * grid.x + place[1]) * grid.q + place[2]

    def cut(rows, start):
        lane = lax.broadcasted_iota(jnp.int32, (width, 128), 0)
        to = lax.broadcasted_iota(jnp.int32, (width, 128), 1)
        take = (lane == to + start).astype(f32)
        return lax.dot_general(
            rows,
            take,
            (((1,), (0,)), ((), ())),
            precision=lax.Precision.HIGHEST,
            preferred_element_type=f32,
        )

    me = chip * 2 + place[3]
    six_ref[...] = cut(vec[0:8], me * shard)[:, :shard]

    def long(low, high, start, ref):
        n = ref.shape[1]
        rows = jnp.where(start >= width, high, low)
        start = jnp.where(start >= width, start - width, start)
        ref[...] = cut(jnp.broadcast_to(rows, (8, width)), start)[0:1, :n]

    long(vec[6:7], vec[7:8], me * 2 * shard, qv_ref)
    first = place[3] == 0
    low, high = jnp.where(first, vec[8:9], vec[10:11]), jnp.where(first, vec[9:10], vec[11:12])
    long(low, high, chip * up_ref.shape[1], up_ref)


def last_rest(grid, own, other, vec, shard, per_chip):
    half = own.shape[2]
    whole = lambda shape: pl.BlockSpec(shape, lambda i, s: (0,) * len(shape))
    shapes = [(shard, 6 * half), (shard, 2 * half), (8, shard), (1, 2 * shard), (1, per_chip)]
    return call(
        functools.partial(last_rest_kernel, grid, shard),
        grid.place,
        [own, other, vec],
        grid=(1,),
        in_specs=[whole(own.shape), whole(other.shape), whole(vec.shape)],
        out_specs=[whole(s) for s in shapes],
        out_shape=[jax.ShapeDtypeStruct(s, f32) for s in shapes],
        cost_estimate=SMALL,
        mib=8,
        name="last_rest",
    )


def in_order(first, mine, other):
    return jnp.stack([jnp.where(first, mine, other), jnp.where(first, other, mine)])


def body(
    dp,
    blk,
    inputs,
    clip_ids,
    ln1_gain,
    ln1_bias,
    w_qkv,
    qv_bias,
    w_out,
    out_bias,
    ln2_gain,
    ln2_bias,
    w_up,
    up_bias,
    w_down,
    down_bias,
    out_grad,
):
    grid = Grid(dp, blk)
    core = grid.me["c"]
    first = core == 0
    chips = grid.chips
    width = inputs.shape[2]
    half = width // 2
    local = inputs.shape[1]
    chip_rows = 2 * local
    units = w_up.shape[1] // 2
    shard = w_qkv.shape[0]
    per_chip = units // chips
    fast = shard % 8 == 0 and per_chip % 16 == 0
    swap = lambda v: grid.shift(v, "c", 1)
    at_core = lambda v, dim=0: lax.dynamic_index_in_dim(v, core, dim, keepdims=False)
    not_core = lambda v, dim=0: lax.dynamic_index_in_dim(v, 1 - core, dim, keepdims=False)

    pad = jnp.zeros((16, width), bf16).at[0, :local].set(clip_ids[0].astype(bf16))
    mine = jnp.concatenate([inputs[0], pad], axis=0)
    dy_mine = out_grad[0]
    if fast:
        put = lambda v, n: jnp.zeros((128,), bf16).at[:n].set(v)
        place_at = lambda v: jnp.where(first, jnp.pad(v, (0, v.size)), jnp.pad(v, (v.size, 0)))
        vecs = [ln1_gain, ln1_bias, out_bias, ln2_gain, ln2_bias, down_bias, qv_bias]
        rows = jnp.stack([jnp.pad(place_at(v), (0, 128 - 2 * v.size)) for v in vecs])
        up_row = put(up_bias, per_chip)[None]
        blank = jnp.zeros((8, 128), bf16)
        mine_small = jnp.concatenate([rows, up_row, blank])
        their_small = jnp.concatenate([rows, jnp.zeros_like(up_row), blank])
        widen = lambda v: jnp.pad(v, ((0, 0), (0, 3 * half - 128)))
        split = w_qkv.reshape(shard, 3, 2, half)
        my_qkv = at_core(split, 2).reshape(shard, 3 * half)
        to_qkv = not_core(split, 2).reshape(shard, 3 * half)
        up_split = w_up.reshape(shard, chips, 2, per_chip)
        my_up = at_core(up_split, 2).reshape(shard, units)
        to_up = not_core(up_split, 2).reshape(shard, units)
        got = swap(jnp.concatenate([to_qkv, widen(their_small)]))
        pair = in_order(first, my_qkv, got[:shard])
        small_chip = mine_small + got[shard:, :128]
        qkv_piece = jnp.concatenate([pair.reshape(2 * shard, 3 * half), widen(small_chip)])

        lines = lax.all_gather(jnp.concatenate([w_down, w_out]), AXES, axis=0, tiled=False)
        full_out = lines[:, per_chip:].reshape(width, width)
        downs = Whole([lines.reshape(chips, 2, per_chip + shard, width)])
        qkv_piece, x_sent = lock(qkv_piece, mine)
        qkv_z = grid.along(qkv_piece, "z")
        x_far = grid.along(x_sent, "q")
        x_near = swap(x_sent)
        up_pair = in_order(first, my_up, swap(to_up)).reshape(2 * shard, units)
        up_piece = jnp.concatenate([up_pair[:, :width], up_pair[:, width:]])

        qkv_z, x_far, x_near, up_piece = lock(qkv_z, x_far, x_near, up_piece)
        qkv_line = grid.line(qkv_piece, qkv_z)
        qkv_over, qkv_sides = grid.shift(qkv_line, "x", 1), grid.along(qkv_line, "q")
        up_line = grid.exchange(jnp.broadcast_to(up_piece, (grid.z,) + up_piece.shape))
        x_both = [(mine, x_near)] + [(v, swap(v)) for v in x_far]
        dy_near = swap(dy_mine)

        qkv_over, qkv_sides, x_both, dy_near = lock(qkv_over, qkv_sides, x_both, dy_near)
        found = grid.found(
            qkv_line, qkv_over, qkv_sides, grid.corner_pieces(qkv_over, qkv_sides)
        )
        qkv_weights = Pieces(grid, found)
        small_all = pick(grid, found, 2 * shard, 128)
        vec = vectors_of(grid, small_all.reshape(chips * 16, 128), width)
    else:
        whole = lambda v: lax.all_gather(v, AXES, axis=0, tiled=True)
        full_qkv = at_core(whole(w_qkv).reshape(width, 3, 2, half), 2).reshape(width, 3 * half)
        qkv_weights = Whole([full_qkv])
        full_out = whole(w_out)
        full_up = at_core(whole(w_up).reshape(width, chips, 2, per_chip), 2).reshape(width, units)
        full_down = whole(w_down).reshape(chips, 2, per_chip, width)
        ups, downs = Whole([full_up]), Whole([full_down])
        up_all = at_core(whole(up_bias).reshape(chips, 2, per_chip), 1).reshape(2, width)
        singles = [ln1_gain, ln1_bias, out_bias, ln2_gain, ln2_bias, down_bias]
        vec = jnp.concatenate(
            [whole(v)[None] for v in singles]
            + [whole(qv_bias).reshape(2, width), up_all, jnp.zeros((6, width), bf16)]
        ).astype(f32)
        x_both = [(v, swap(v)) for v in [mine] + grid.along(mine, "q")]
        dy_near = swap(dy_mine)

    both = [in_order(first, *v) for v in x_both]
    token_rows = jnp.concatenate([b[:, :local].reshape(chip_rows, width) for b in both])
    clips = jnp.concatenate([b[:, local, :local].reshape(chip_rows) for b in both])
    lane = lax.broadcasted_iota(jnp.int32, (1, 128), 1) % HEAD_DIM
    same = clips[:, None].astype(jnp.int32) == lane
    hot = same[:chip_rows].astype(bf16)
    pen = jnp.where(same | (lane >= 8), 0.0, -1e30).astype(bf16)
    dy = in_order(first, dy_mine, dy_near).reshape(chip_rows, width)

    queries, keys, values, h1t, n1, rstd1, full_qkv = project_qkv(
        grid, behind(token_rows, dy), vec, qkv_weights, local
    )
    pairs = half // 128
    if fast:
        queries, up_line = lock(queries, up_line)
        up_over, up_sides = grid.shift(up_line, "x", 1), grid.along(up_line, "q")
    queries, keys, values = hbm(queries), hbm(keys), hbm(values)
    attended, att, lse = attn_fwd(queries, keys, values, hot, pen, 0, pairs)
    if fast:
        up_over, up_sides = behind((up_over, up_sides), att)
        corners = grid.corner_pieces(up_over, up_sides)
        ups = Pieces(grid, grid.found(up_line, up_over, up_sides, corners, True))
    att_mine, att_other = [att], [swap(att)]
    out_rows = full_out.reshape(2, half, width)
    after, h2, n2, rstd2 = project_out(grid, token_rows, att_mine, att_other, out_rows, vec)

    *g_ff, gbias, ff_out, dh, dh_b = feed_forward(grid, h2, dy, ups, downs, vec, units)
    d_after, d_branch, d_att, sums2 = out_back(grid, dh, swap(dh_b), dy, n2, rstd2, vec, out_rows)

    def back(d, a, n):
        return attn_bwd(queries, keys, values, hot, pen, hbm(attended), d, lse, a, n)

    by_core = lambda v: v.reshape(2, local, width)
    up_sums = gbias.reshape(2, width)
    grads = [back(d_att, 0, 1)]
    if fast:
        ff_over, ff_sides = grid.corners(g_ff[0], grads[0])
        d_att = behind(d_att, ff_over, ff_sides)
    grads.append(back(d_att, 1, pairs - 1))
    g_all = matrix_gradients(grid, fast, h1t, d_branch, att_mine, att_other, grads)
    if fast:
        ff_own = grid.edges(g_ff[0], ff_over, ff_sides, g_all)
        grads, g_all, ff_own = lock(grads, g_all, ff_own)
        ff_z = [grid.shift(ff_own[k], "z", k) for k in range(1, grid.z)]
    else:
        grads, g_all = lock(grads, g_all)
    d_mine, d_other, sums = input_back(grid, grads, full_qkv, n1, sums2, up_sums, local)
    if fast:
        over, sides = grid.corners(g_all, d_other)
        middle = grid.z // 2 - 1
        ends = ff_z[:middle] + ff_z[middle + 1 :]
        d_other, over, sides, ends = lock(d_other, over, sides, ends)
    d_got = swap(d_other)
    sent = [
        total_of(*(v[k * local : (k + 1) * local] for v in (d_mine, d_got))).astype(bf16)
        for k in range(1, grid.q)
    ]
    got = [grid.shift(s, "q", grid.q - k) for k, s in enumerate(sent, 1)]
    if fast:
        vectors = sums + d_got[grid.q * local :].astype(f32)
    ff_out = behind(ff_out, sent)
    out_got = swap(not_core(by_core(ff_out)).astype(bf16)).astype(f32)
    result = at_core(by_core(ff_out)) + out_got + at_core(by_core(after)) + vec[5:6]
    output = result.astype(bf16)[None]
    input_grad = finish(grid, d_mine, d_got, got, n1, rstd1, d_after, vec)[None]

    if fast:
        own = grid.edges(g_all, over, sides, (vectors, sent))
        ff = total_of(ff_own[0], behind(ff_z[middle], own), *ends)
        vectors = jnp.concatenate([vectors[:, :half], vectors[:, half:]]).astype(bf16)
        own, vectors = lock(own, vectors)
        vectors = jnp.broadcast_to(vectors, (grid.z,) + vectors.shape)
        w_up_g, w_down_g = last_ff(grid, ff, swap(ff[per_chip:].astype(bf16)), shard)
        own, vectors = grid.column_near(own, vectors, (output, w_up_g))
        vectors = vectors + behind(grid.shift(vectors, "x", 1), input_grad)
        vectors = vectors + sum(grid.along(vectors, "q"))
        w_qkv_g, w_out_g, six, qv_g, up_g = last_rest(
            grid, own, swap(own.astype(bf16)), vectors, shard, per_chip
        )
        qv_g, up_g = qv_g[0], up_g[0]
    else:
        reduce = lambda v: lax.psum_scatter(v, AXES, scatter_dimension=0, tiled=True)

        def spread(v, dim):
            v = v.astype(f32)
            zero = jnp.zeros_like(v)
            return jnp.stack([jnp.where(first, v, zero), jnp.where(first, zero, v)], axis=dim)

        gdown, gup = g_ff
        w_down_g = reduce(
            spread(gdown.reshape(chips, per_chip, width), 1).reshape(2 * units, width)
        )
        w_up_g = reduce(spread(gup.reshape(width, chips, per_chip), 2).reshape(width, 2 * units))
        w_out_g = reduce(spread(g_all[pairs], 1).reshape(width, width))
        per_pair = g_all[:pairs].reshape(pairs, width, 3, 128)
        per_pair = jnp.transpose(per_pair, (1, 2, 0, 3)).reshape(width, 3, half)
        w_qkv_g = reduce(spread(per_pair, 2).reshape(width, 6 * half))
        sums = lax.psum(sums, AXES)
        me = (lax.axis_index("dp") * blk) + lax.axis_index("blk")
        six = lax.dynamic_slice(sums, (0, me * shard), (6, shard))
        qv_g = lax.dynamic_slice(sums[6:8].reshape(2 * width), (me * 2 * shard,), (2 * shard,))
        up_g = at_core(sums[8:12].reshape(2, units))
        up_g = lax.dynamic_slice(up_g, (me // 2 * per_chip,), (per_chip,))

    return (
        output,
        input_grad,
        six[0],
        six[1],
        w_qkv_g,
        qv_g,
        w_out_g,
        six[2],
        six[3],
        six[4],
        w_up_g,
        up_g,
        w_down_g,
        six[5],
    )


def solution(mesh):
    both = P(("dp", "blk"))
    rows = P(("dp", "blk"), None)
    tokens = P("dp", "blk", None)
    return jax.shard_map(
        functools.partial(body, mesh.shape["dp"], mesh.shape["blk"]),
        mesh=mesh,
        in_specs=(
            tokens,
            P("dp", "blk"),
            both,
            both,
            rows,
            both,
            rows,
            both,
            both,
            both,
            rows,
            both,
            rows,
            both,
            tokens,
        ),
        out_specs=(
            tokens,
            tokens,
            both,
            both,
            rows,
            both,
            rows,
            both,
            both,
            both,
            rows,
            both,
            rows,
            both,
        ),
        check_vma=False,
    )
```

```python
import functools
import itertools
import math

import jax
import jax.numpy as jnp
from jax import lax
from jax.experimental import pallas as pl
from jax.experimental.pallas import tpu as pltpu
from jax.sharding import PartitionSpec as P

HEAD_DIM = 64
NORM_EPS = 1e-06
LOG2E = math.log2(math.e)
f32 = jnp.float32
bf16 = jnp.bfloat16
AXES = ("dp", "blk")


def mm(a, b, dims=((1,), (0,))):
    return lax.dot_general(a, b, (dims, ((), ())), preferred_element_type=f32)


SMALL = pl.CostEstimate(flops=1000, bytes_accessed=1000, transcendentals=0)


class Grid:
    def __init__(self, dp, blk):
        self.size = {"z": dp // 2, "x": 2, "q": blk // 2, "c": 2}
        self.z, self.x, self.q = dp // 2, 2, blk // 2
        self.chips = self.z * 2 * self.q
        me_dp, me_blk = lax.axis_index("dp"), lax.axis_index("blk")
        self.me = {"z": me_dp // 2, "x": me_dp % 2, "q": me_blk // 2, "c": me_blk % 2}
        self.place = jnp.stack([self.me[a] for a in ("z", "x", "q", "c")]).astype(jnp.int32)

    def flat(self, at):
        return ((at["z"] * self.x + at["x"]) * self.q + at["q"]) * 2 + at["c"]

    def shift(self, value, axis, step):
        pairs = []
        for z in range(self.z):
            for x in range(self.x):
                for q in range(self.q):
                    for c in range(2):
                        at = {"z": z, "x": x, "q": q, "c": c}
                        to = dict(at)
                        to[axis] = (at[axis] + step) % self.size[axis]
                        pairs.append((self.flat(at), self.flat(to)))
        return lax.ppermute(value, AXES, pairs)

    def chip(self, place, dz, dx, dq):
        z = -1 - dz if dz < 0 else lax.rem(place[0] + (self.z - dz), self.z)
        x = lax.rem(place[1] + (self.x - dx), self.x)
        q = lax.rem(place[2] + (self.q - dq), self.q)
        return (z * self.x + x) * self.q + q

    def relative(self, place, chip, near=False):
        z, x, q = chip // (self.x * self.q), chip // self.q % self.x, chip % self.q
        dx = lax.rem(x + self.x - place[1], self.x)
        dq = lax.rem(q + self.q - place[2], self.q)
        if near:
            z = lax.rem(z + self.z - place[0], self.z)
        return dx * self.q + dq, z

    def along(self, value, axis):
        return [self.shift(value, axis, k) for k in range(1, self.size[axis])]

    def line(self, value, others):
        return jnp.stack([value] + others)

    def corner_pieces(self, over, sides):
        half = self.z // 2
        return [
            (self.shift(over[:half], "q", k), self.shift(side[half:], "x", 1))
            for k, side in enumerate(sides, 1)
        ]

    def found(self, line, over, sides, corners, plain=False):
        half = self.z // 2
        zs = [-1 - z if plain else z for z in range(self.z)]
        out = [(line, [(z, 0, 0) for z in zs]), (over, [(z, 1, 0) for z in zs])]
        for k, (side, (a, b)) in enumerate(zip(sides, corners), 1):
            out.append((side, [(z, 0, k) for z in zs]))
            out.append((a, [(z, 1, k) for z in zs[:half]]))
            out.append((b, [(z, 1, k) for z in zs[half:]]))
        return out

    def found_last(self, plane, others):
        at = [(x, q) for x in range(2) for q in range(self.q)]
        return [(p, [(z, x, q) for x, q in at]) for z, p in enumerate([plane] + others)]


    def corners(self, value, first=()):
        half = self.z // 2
        over = value[self.q]
        late, sides = [], []
        for k in range(1, self.q):
            corner = value[self.q + k]
            got = behind(self.shift(corner[:half], "x", 1), first)
            late.append(behind(self.shift(corner[half:], "q", k), first))
            side = value[k]
            sides.append(jnp.concatenate([total_of(side[:half], got).astype(bf16), side[half:]]))
        over = jnp.concatenate([over[:half], total_of(over[half:], *late).astype(bf16)])
        return over, sides

    def edges(self, value, over, sides, first=()):
        parts = [self.shift(over, "x", 1)]
        parts += [self.shift(s, "q", k) for k, s in enumerate(sides, 1)]
        parts = behind(parts, first)
        return total_of(value[0], *parts).astype(bf16)

    def column(self, own):
        return total_of(*self.exchange(own))

    def column_near(self, own, vectors, first=()):
        size = own.shape[1] * own.shape[2]
        rows = jnp.concatenate([own.reshape(self.z, size, own.shape[3])] + [vectors], axis=1)
        got = behind([self.shift(rows[k], "z", k) for k in range(1, self.z)], first)
        total = total_of(own[0], *(v[:size].reshape(own.shape[1:]) for v in got))
        return total, total_of(vectors[0], *(v[size:] for v in got))

    def groups(self, axes):
        names = ("z", "x", "q", "c")
        rest = [n for n in names if n not in axes]
        out = []
        for fixed in itertools.product(*(range(self.size[n]) for n in rest)):
            at = dict(zip(rest, fixed))
            out.append(
                [
                    self.flat({**at, **dict(zip(axes, v))})
                    for v in itertools.product(*(range(self.size[n]) for n in axes))
                ]
            )
        return out

    def exchange(self, blocks):
        return lax.all_to_all(
            blocks, AXES, 0, 0, axis_index_groups=self.groups(("z",)), tiled=True
        )

    def gather_chips(self, value):
        return lax.all_gather(
            value, AXES, axis=0, axis_index_groups=self.groups(("z", "x", "q")), tiled=True
        )


def total_of(*values):
    return sum(v.astype(f32) for v in values)


def lock(*values):
    return lax.optimization_barrier(values)


def behind(value, *others):
    return lax.optimization_barrier((value, others))[0]


def hbm(value):
    return pltpu.with_memory_space_constraint(value, pltpu.HBM)


def call(kernel, place, operands, **kw):
    spec = pltpu.PrefetchScalarGridSpec(
        num_scalar_prefetch=1,
        grid=kw.pop("grid"),
        in_specs=kw.pop("in_specs"),
        out_specs=kw.pop("out_specs"),
        scratch_shapes=kw.pop("scratch_shapes", []),
    )
    return pl.pallas_call(
        kernel,
        grid_spec=spec,
        compiler_params=pltpu.CompilerParams(vmem_limit_bytes=kw.pop("mib") * 2**20),
        **kw,
    )(place, *operands)


class Pieces:
    def __init__(self, grid, found):
        self.grid = grid
        self.found = found
        self.arrays = [f[0] for f in found]
        self.count = sum(f[0].shape[0] for f in found)

    def copies(self, place, refs, sem, moves):
        out = []
        for ref, (piece, at_chips) in zip(refs, self.found):
            for i, distance in enumerate(at_chips):
                chip = self.grid.chip(place, *distance)
                for at, rows, col, cols, to in moves:
                    source = ref.at[i, pl.ds(at, rows), pl.ds(col, cols)]
                    out.append(pltpu.make_async_copy(source, to(chip), sem.at[len(out)]))
        return out


class Whole:
    def __init__(self, arrays):
        self.arrays = arrays
        self.count = 1


def pick(grid, found, first, lanes):
    arrays = [f[0][:, first:, :lanes] for f in found]
    rows = arrays[0].shape[1]

    def kernel(place, *refs):
        for ref, (piece, at_chips) in zip(refs[:-1], found):
            for i, distance in enumerate(at_chips):
                refs[-1][grid.chip(place, *distance)] = ref[i]

    return call(
        kernel,
        grid.place,
        arrays,
        grid=(1,),
        in_specs=[pl.BlockSpec(a.shape, lambda i, s: (0, 0, 0)) for a in arrays],
        out_specs=pl.BlockSpec((grid.chips, rows, lanes), lambda i, s: (0, 0, 0)),
        out_shape=jax.ShapeDtypeStruct((grid.chips, rows, lanes), bf16),
        cost_estimate=SMALL,
        mib=8,
        name="pick",
    )


def vectors_kernel(place, small_ref, out_ref):
    rows, width = small_ref.shape[0], out_ref.shape[1]
    chips = rows // 16
    m = lax.broadcasted_iota(jnp.int32, (128, width), 0)
    j = lax.broadcasted_iota(jnp.int32, (128, width), 1)
    small = small_ref[...]
    narrow, wide = width // chips, 2 * width // chips
    spread = lambda n: mm(small, ((j % n) == m).astype(bf16)).reshape(chips, 16, width)
    one = lax.broadcasted_iota(jnp.int32, (chips, 16, width), 2)
    chip = lax.broadcasted_iota(jnp.int32, (chips, 16, width), 0)
    a, b = spread(narrow), spread(wide)
    plain = jnp.sum(jnp.where(one // narrow == chip, a, 0.0), axis=0)
    low = jnp.sum(jnp.where(one // wide == chip, b, 0.0), axis=0)
    high = jnp.sum(jnp.where(one // wide + chips // 2 == chip, b, 0.0), axis=0)
    out_ref[...] = jnp.concatenate(
        [plain[0:6], low[6:7], high[6:7], low[7:8], high[7:8], plain[0:6]], axis=0
    )


def vectors_of(grid, small, width):
    rows = small.shape[0]
    return call(
        vectors_kernel,
        grid.place,
        [small],
        grid=(1,),
        in_specs=[pl.BlockSpec((rows, 128), lambda i, s: (0, 0))],
        out_specs=pl.BlockSpec((16, width), lambda i, s: (0, 0)),
        out_shape=jax.ShapeDtypeStruct((16, width), f32),
        cost_estimate=SMALL,
        mib=8,
        name="vectors",
    )


def first_lanes(head):
    lane = lax.broadcasted_iota(jnp.int32, (1, 2 * HEAD_DIM), 1)
    return lane < HEAD_DIM if head == 0 else lane >= HEAD_DIM


def chunk_of(rows):
    return 1536 if rows % 1536 == 0 else rows


def attn_fwd_kernel(q_ref, k_ref, v_ref, hot_ref, pen_ref, o_ref, ob_ref, lse_ref):
    total_keys = k_ref.shape[0]
    chunk = chunk_of(total_keys)
    steps = total_keys // chunk
    query_rows = q_ref.shape[0]
    query, hot = q_ref[...], hot_ref[...]
    outs = []
    for head in range(2):
        sel = first_lanes(head)
        q_aug = jnp.where(sel, query, hot)

        def scores(rows):
            k_aug = jnp.where(sel, k_ref[rows, :], pen_ref[rows, :])
            return mm(k_aug, q_aug, ((1,), (1,)))

        def weigh(rows, s, top):
            p = jnp.exp2(s - top)
            added = mm(v_ref[rows, :], p.astype(bf16), ((0,), (0,)))
            return jnp.sum(p, axis=0, keepdims=True), added

        if steps == 1:
            s = scores(slice(0, chunk))
            top = jnp.max(s, axis=0, keepdims=True)
            total, acc = weigh(slice(0, chunk), s, top)
        else:

            def step(i, carry):
                top, total, acc = carry
                rows = pl.ds(pl.multiple_of(i * chunk, chunk), chunk)
                s = scores(rows)
                new_top = jnp.maximum(top, jnp.max(s, axis=0, keepdims=True))
                more, added = weigh(rows, s, new_top)
                fade = jnp.exp2(top - new_top)
                return new_top, total * fade + more, acc * fade + added

            top, total, acc = lax.fori_loop(
                0,
                steps,
                step,
                (
                    jnp.full((1, query_rows), -1e30, f32),
                    jnp.zeros((1, query_rows), f32),
                    jnp.zeros((2 * HEAD_DIM, query_rows), f32),
                ),
            )
        outs.append((acc / total)[head * HEAD_DIM : (head + 1) * HEAD_DIM])
        lse_ref[0, head : head + 1, :] = top + jnp.log2(total)
    out = jnp.concatenate(outs, axis=0).T
    o_ref[...] = out
    ob_ref[...] = out.astype(bf16)


def attn_fwd(queries, keys, values, hot, pen, start, pairs):
    rows, width = queries.shape[0], pairs * 128
    total_keys = keys.shape[0]
    pairs = width // 128
    block = rows
    cost = SMALL
    return pl.pallas_call(
        attn_fwd_kernel,
        grid=(pairs, rows // block),
        in_specs=[
            pl.BlockSpec((block, 128), lambda p, i: (i, p + start)),
            pl.BlockSpec((total_keys, 128), lambda p, i: (0, p + start)),
            pl.BlockSpec((total_keys, 128), lambda p, i: (0, p + start)),
            pl.BlockSpec((block, 128), lambda p, i: (i, 0)),
            pl.BlockSpec((total_keys, 128), lambda p, i: (0, 0)),
        ],
        out_specs=[
            pl.BlockSpec((block, 128), lambda p, i: (i, p)),
            pl.BlockSpec((block, 128), lambda p, i: (i, p)),
            pl.BlockSpec((1, 2, block), lambda p, i: (p, 0, i)),
        ],
        out_shape=[
            pltpu.HBM((rows, width), f32),
            jax.ShapeDtypeStruct((rows, width), bf16),
            jax.ShapeDtypeStruct((pairs, 2, rows), f32),
        ],
        compiler_params=pltpu.CompilerParams(vmem_limit_bytes=32 * 2**20),
        cost_estimate=cost,
        name="attn_fwd",
    )(queries, keys, values, hot, pen)


def attn_bwd_kernel(
    q_ref, k_ref, v_ref, hot_ref, pen_ref, o_ref, do_ref, lse_ref, dq_ref, dk_ref, dv_ref
):
    total_keys = k_ref.shape[0]
    chunk = chunk_of(total_keys)
    steps = total_keys // chunk
    query, hot, grad = q_ref[...], hot_ref[...], do_ref[...]
    flipped = (grad.astype(f32) * o_ref[...]).T
    zero = jnp.zeros_like(query)

    def step(rows):
        keys, values, pen = k_ref[rows, :], v_ref[rows, :], pen_ref[rows, :]
        dq, dk, dv = [], 0.0, 0.0
        for head in range(2):
            sel = first_lanes(head)
            lanes = slice(head * HEAD_DIM, (head + 1) * HEAD_DIM)
            delta = jnp.sum(flipped[lanes], axis=0, keepdims=True)
            k_aug = jnp.where(sel, keys, pen)
            s = mm(k_aug, jnp.where(sel, query, hot), ((1,), (1,)))
            p = jnp.exp2(s - lse_ref[0, head : head + 1, :])
            grad_h = jnp.where(sel, grad, zero)
            dp = mm(values, grad_h, ((1,), (1,)))
            ds = (p * (dp - delta)).astype(bf16)
            dv = dv + mm(p.astype(bf16), grad_h)
            dk = dk + mm(ds, jnp.where(sel, query, zero))
            dq.append(mm(keys, ds, ((0,), (0,)))[lanes])
        dk_ref[rows, :] = (dk * (1.0 / LOG2E)).astype(bf16)
        dv_ref[rows, :] = dv.astype(bf16)
        return jnp.concatenate(dq, axis=0)

    if steps == 1:
        dq = step(slice(0, chunk))
    else:
        dq = lax.fori_loop(
            0,
            steps,
            lambda i, total: total + step(pl.ds(pl.multiple_of(i * chunk, chunk), chunk)),
            jnp.zeros((2 * HEAD_DIM, query.shape[0]), f32),
        )
    dq_ref[...] = (dq.T * HEAD_DIM**-0.5).astype(bf16)


def attn_bwd(queries, keys, values, hot, pen, attended, d_attended, lse, start, pairs):
    rows = queries.shape[0]
    total_keys = keys.shape[0]
    block = rows
    by_query = pl.BlockSpec((block, 128), lambda p, i: (i, p + start))
    by_key = pl.BlockSpec((total_keys, 128), lambda p, i: (0, p + start))
    to_query = pl.BlockSpec((block, 128), lambda p, i: (i, p))
    to_key = pl.BlockSpec((total_keys, 128), lambda p, i: (0, p))
    width = pairs * 128
    cost = SMALL
    return pl.pallas_call(
        attn_bwd_kernel,
        grid=(pairs, rows // block),
        in_specs=[
            by_query,
            by_key,
            by_key,
            pl.BlockSpec((block, 128), lambda p, i: (i, 0)),
            pl.BlockSpec((total_keys, 128), lambda p, i: (0, 0)),
            by_query,
            by_query,
            pl.BlockSpec((1, 2, block), lambda p, i: (p + start, 0, i)),
        ],
        out_specs=[to_query, to_key, to_key],
        out_shape=[
            jax.ShapeDtypeStruct((rows, width), bf16),
            jax.ShapeDtypeStruct((total_keys, width), bf16),
            jax.ShapeDtypeStruct((total_keys, width), bf16),
        ],
        compiler_params=pltpu.CompilerParams(vmem_limit_bytes=40 * 2**20),
        cost_estimate=cost,
        name="attn_bwd",
    )(queries, keys, values, hot, pen, attended, d_attended, lse)


def halves(place, mine, other):
    first = place[3] == 0
    return jnp.where(first, mine, other), jnp.where(first, other, mine)


def load_all(copies):
    for c in copies:
        c.start()
    for c in copies:
        c.wait()


def qkv_kernel(weights, moves, place, x_ref, vec_ref, *refs):
    pieces, refs = refs[:-9], refs[-9:]
    q_ref, k_ref, v_ref, h1t_ref, n1_ref, rstd_ref, w_out, w_s, sem = refs
    half = q_ref.shape[1]
    width = x_ref.shape[1]
    step = pl.program_id(0)

    @pl.when(step == 0)
    def _():
        if isinstance(weights, Pieces):
            load_all(weights.copies(place, pieces, sem, moves(w_s)))
        else:
            load_all([pltpu.make_async_copy(pieces[0], w_s.at[0], sem.at[0])])
        w_out[...] = w_s[...]

    x = x_ref[...].astype(f32)
    centered = x - mean_of(x)
    rstd = lax.rsqrt(mean_of(centered * centered) + NORM_EPS)
    n1 = centered * rstd
    n1_ref[...] = n1.astype(bf16)
    rstd_ref[...] = rstd
    h1 = (n1 * vec_ref[0:1, :] + vec_ref[1:2, :]).astype(bf16)
    low, high = vec_ref[6:8, :half], vec_ref[6:8, half:]
    bias = jnp.where(place[3] == 0, low, high)
    w = w_s[...].reshape(width, 3 * half)

    @pl.when(step < 2)
    def _():
        q = mm(h1, w[:, :half]) + bias[0:1]
        q_ref[...] = (q * (LOG2E * HEAD_DIM**-0.5)).astype(bf16)

    kv = mm(h1, w[:, half:])
    k_ref[...] = kv[:, :half].astype(bf16)
    v_ref[...] = (kv[:, half:] + bias[1:2]).astype(bf16)
    h1t_ref[...] = h1.T


def project_qkv(grid, x, vec, weights, local):
    rows, width = x.shape
    half = width // 2
    if isinstance(weights, Pieces):
        r = width // grid.chips
        moves = lambda w: [(0, r, 0, 3 * half, lambda chip: w.at[chip])]
        shape = (grid.chips, r, 3 * half)
    else:
        moves = None
        shape = (1, width, 3 * half)
    *found, w = call(
        functools.partial(qkv_kernel, weights, moves),
        grid.place,
        [x, vec] + [hbm(w) for w in weights.arrays],
        grid=(rows // local,),
        in_specs=[
            pl.BlockSpec((local, width), lambda i, s: (i, 0)),
            pl.BlockSpec(vec.shape, lambda i, s: (0, 0)),
        ]
        + [pl.BlockSpec(memory_space=pl.ANY)] * len(weights.arrays),
        out_specs=[
            pl.BlockSpec((local, half), lambda i, s: (jnp.minimum(i, 1), 0)),
            pl.BlockSpec((local, half), lambda i, s: (i, 0)),
            pl.BlockSpec((local, half), lambda i, s: (i, 0)),
            pl.BlockSpec((width, local), lambda i, s: (0, i)),
            pl.BlockSpec((local, width), lambda i, s: (i, 0)),
            pl.BlockSpec((local, 1), lambda i, s: (i, 0)),
            pl.BlockSpec(shape, lambda i, s: (0, 0, 0)),
        ],
        out_shape=[
            pltpu.HBM((2 * local, half), bf16),
            pltpu.HBM((rows, half), bf16),
            pltpu.HBM((rows, half), bf16),
            pltpu.HBM((width, rows), bf16),
            pltpu.HBM((rows, width), bf16),
            pltpu.HBM((rows, 1), f32),
            pltpu.HBM(shape, bf16),
        ],
        scratch_shapes=[pltpu.VMEM(shape, bf16), pltpu.SemaphoreType.DMA((weights.count,))],
        cost_estimate=SMALL,
        mib=20,
        name="qkv",
    )
    return found + [w.reshape(width, 3 * half)]


def mean_of(v):
    return jnp.mean(v, axis=-1, keepdims=True)


def join(refs):
    return jnp.concatenate([r[...] for r in refs], axis=1)


def out_kernel(n, place, x_ref, w_ref, vec_ref, *refs):
    (after_ref, h2_ref, n2_ref, rstd_ref) = refs[2 * n :]
    a, b = halves(place, join(refs[:n]), join(refs[n : 2 * n]))
    after = x_ref[...].astype(f32) + mm(a, w_ref[0]) + mm(b, w_ref[1]) + vec_ref[2:3, :]
    after_ref[...] = after
    centered = after - mean_of(after)
    rstd = lax.rsqrt(mean_of(centered * centered) + NORM_EPS)
    n2 = centered * rstd
    n2_ref[...] = n2.astype(bf16)
    rstd_ref[...] = jnp.broadcast_to(rstd, rstd_ref.shape)
    h2_ref[...] = (n2 * vec_ref[3:4, :] + vec_ref[4:5, :]).astype(bf16)


def project_out(grid, x, mine, other, w, vec):
    rows, width = mine[0].shape[0], x.shape[1]
    block = 256 if rows % 256 == 0 else rows
    line = lambda n: pl.BlockSpec((block, n), lambda i, s: (i, 0))
    return call(
        functools.partial(out_kernel, len(mine)),
        grid.place,
        [x, w, vec] + mine + other,
        grid=(rows // block,),
        in_specs=[
            line(width),
            pl.BlockSpec(w.shape, lambda i, s: (0, 0, 0)),
            pl.BlockSpec(vec.shape, lambda i, s: (0, 0)),
        ]
        + [line(v.shape[1]) for v in mine + other],
        out_specs=[line(width), line(width), line(width), line(128)],
        out_shape=[
            pltpu.HBM((rows, width), f32),
            pltpu.HBM((rows, width), bf16),
            pltpu.HBM((rows, width), bf16),
            pltpu.HBM((rows, 128), f32),
        ],
        cost_estimate=SMALL,
        mib=16,
        name="out_proj",
    )


def norm_back(grad, normed, rstd, gain):
    e = grad * gain
    return (e - mean_of(e) - normed * mean_of(e * normed)) * rstd


def sum_rows(v):
    return jnp.sum(v, axis=0, keepdims=True)


def out_back_kernel(
    place, mine_ref, got_ref, dy_ref, n2_ref, rstd_ref, vec_ref, w_ref, after_ref, branch_ref, datt_ref, sums_ref
):
    d_h2 = mine_ref[...] + got_ref[...].astype(f32)
    dy = dy_ref[...].astype(f32)
    n2 = n2_ref[...].astype(f32)
    d_after = dy + norm_back(d_h2, n2, rstd_ref[:, 0:1], vec_ref[3:4, :])
    after_ref[...] = d_after
    branch = d_after.astype(bf16)
    branch_ref[...] = branch
    datt_ref[...] = mm(branch, w_ref[0], ((1,), (1,))).astype(bf16)
    rows = [sum_rows(branch.astype(f32)), sum_rows(d_h2 * n2), sum_rows(d_h2), sum_rows(dy)]
    sums = jnp.concatenate(rows + [jnp.zeros((4, dy.shape[1]), f32)], axis=0) * 0.5

    @pl.when(pl.program_id(0) == 0)
    def _():
        sums_ref[...] = jnp.zeros_like(sums_ref)

    sums_ref[...] += sums


def out_back(grid, mine, got, dy, n2, rstd, vec, w):
    rows, width = mine.shape
    block = 256 if rows % 256 == 0 else rows
    line = lambda n: pl.BlockSpec((block, n), lambda i, s: (i, 0))
    return call(
        out_back_kernel,
        grid.place,
        [mine, got, dy, n2, rstd, vec, w],
        grid=(rows // block,),
        in_specs=[
            line(width),
            line(width),
            line(width),
            line(width),
            line(128),
            pl.BlockSpec(vec.shape, lambda i, s: (0, 0)),
            pl.BlockSpec((1,) + w.shape[1:], lambda i, s: (s[3], 0, 0)),
        ],
        out_specs=[
            line(width),
            line(width),
            line(width // 2),
            pl.BlockSpec((8, width), lambda i, s: (0, 0)),
        ],
        out_shape=[
            pltpu.HBM((rows, width), f32),
            jax.ShapeDtypeStruct((rows, width), bf16),
            jax.ShapeDtypeStruct((rows, width // 2), bf16),
            jax.ShapeDtypeStruct((8, width), f32),
        ],
        cost_estimate=SMALL,
        mib=20,
        name="out_back",
    )


def store_rows(grid, place, ref, value, shard, slot):
    for i in range(grid.chips):
        column, z = grid.relative(place, i, True)
        ref[column, z, slot, 0:shard, :] = value[i * shard : (i + 1) * shard]


def matrix_grads_kernel(grid, fast, n, parts, place, h1t_ref, d_ref, *refs):
    g_ref = refs[-1]
    mine, other, refs = refs[:n], refs[n : 2 * n], refs[2 * n : -1]
    flat = refs
    shard = h1t_ref.shape[0] // grid.chips
    slot = 0
    for part in range(parts):
        dq_ref, dk_ref, dv_ref = flat[3 * part : 3 * part + 3]
        chip_rows = dq_ref.shape[0]
        for p in range(dq_ref.shape[1] // 128):
            cols = slice(p * 128, (p + 1) * 128)
            gq = mm(h1t_ref[:, :chip_rows], dq_ref[:, cols])
            gkv = mm(h1t_ref[...], jnp.concatenate([dk_ref[:, cols], dv_ref[:, cols]], axis=1))
            g = jnp.concatenate([gq, gkv], axis=1).astype(bf16)
            if fast:
                store_rows(grid, place, g_ref, g, shard, slot)
            else:
                g_ref[slot] = g
            slot += 1
    a, b = halves(place, join(mine), join(other))
    g = mm(jnp.concatenate([a, b], axis=1), d_ref[...], ((0,), (0,))).astype(bf16)
    if fast:
        store_rows(grid, place, g_ref, g, shard, slot)
    else:
        g_ref[slot] = g


def matrix_gradients(grid, fast, h1t, branch, mine, other, grads):
    width = h1t.shape[0]
    rows, half = branch.shape[0], branch.shape[1] // 2
    slots = half // 128 + 1
    if fast:
        shape = (2 * grid.q, grid.z, slots, width // grid.chips, half)
    else:
        shape = (slots, width, half)
    flat = [v for part in grads for v in part]
    whole = lambda v: pl.BlockSpec(v.shape, lambda i, s: (0, 0))
    return call(
        functools.partial(matrix_grads_kernel, grid, fast, len(mine), len(grads)),
        grid.place,
        [hbm(h1t), branch] + mine + other + flat,
        grid=(1,),
        in_specs=[whole(h1t), pl.BlockSpec((rows, half), lambda i, s: (0, s[3]))]
        + [whole(v) for v in mine + other + flat],
        out_specs=pl.BlockSpec(shape, lambda i, s: (0,) * len(shape)),
        out_shape=pltpu.HBM(shape, bf16),
        cost_estimate=SMALL,
        mib=30,
        name="matrix_grads",
    )


def input_back_kernel(parts, place, *refs):
    grads, (w_ref, n1_ref, sums_ref, up_ref) = refs[: 3 * parts], refs[3 * parts : 3 * parts + 4]
    mine_ref, other_ref, vec_ref = refs[3 * parts + 4 :]
    step, last = pl.program_id(0), pl.num_programs(0) - 1
    dq, dk, dv = (
        jnp.concatenate([grads[3 * p + i][...] for p in range(parts)], axis=1) for i in range(3)
    )
    half = dq.shape[1]
    local, width = n1_ref.shape
    local = local // 2
    dq = jnp.where(step < 1, dq, jnp.zeros_like(dq))
    d = mm(jnp.concatenate([dq, dk, dv], axis=1), w_ref[...], ((1,), (1,)))
    to = pl.ds(pl.multiple_of(step * local, local), local)
    a, b = halves(place, d[:local], d[local:])
    mine_ref[to, :] = a
    other_ref[to, :] = b.astype(bf16)
    none = jnp.zeros((1, half), f32)
    first = place[3] == 0

    def spread(v):
        v = sum_rows(v.astype(f32))
        return jnp.concatenate([jnp.where(first, v, none), jnp.where(first, none, v)], axis=1)

    top = jnp.concatenate([sum_rows(d * n1_ref[...].astype(f32)), sum_rows(d)], axis=0)
    low = jnp.concatenate([spread(dq), spread(dv)], axis=0)

    @pl.when(step == 0)
    def _():
        up, no = up_ref[...], jnp.zeros_like(up_ref[...])
        ups = [jnp.where(first, up, no), jnp.where(first, no, up), jnp.zeros((4, width), f32)]
        vec_ref[...] = jnp.concatenate([top, sums_ref[0:4, :], low] + ups, axis=0)

    @pl.when(step > 0)
    def _():
        vec_ref[0:2, :] += top
        vec_ref[6:8, :] += low

    @pl.when(step == last)
    def _():
        at = other_ref.shape[0] - 16
        other_ref[at:, :] = vec_ref[...].astype(bf16)


def input_back(grid, grads, w, n1, sums, ups, local):
    rows, width = n1.shape
    flat = [g for part in grads for g in part]
    specs = []
    for dq, dk, dv in grads:
        n = dq.shape[1]
        specs.append(pl.BlockSpec((2 * local, n), lambda i, s: (0, 0)))
        specs += [pl.BlockSpec((2 * local, n), lambda i, s: (i, 0))] * 2
    whole = lambda shape: pl.BlockSpec(shape, lambda i, s: (0, 0))
    mine, other, vec = (grid.q * local, width), (grid.q * local + 16, width), (16, width)
    return call(
        functools.partial(input_back_kernel, len(grads)),
        grid.place,
        flat + [hbm(w), hbm(n1), sums, ups],
        grid=(grid.q,),
        in_specs=specs
        + [whole(w.shape), pl.BlockSpec((2 * local, width), lambda i, s: (i, 0))]
        + [whole(sums.shape), whole(ups.shape)],
        out_specs=[whole(mine), whole(other), whole(vec)],
        out_shape=[
            pltpu.HBM(mine, f32),
            jax.ShapeDtypeStruct(other, bf16),
            jax.ShapeDtypeStruct(vec, f32),
        ],
        cost_estimate=SMALL,
        mib=30,
        name="input_back",
    )


def finish_kernel(n_got, place, *refs):
    mine_ref, got_ref = refs[:2]
    sides = refs[2 : 2 + n_got]
    n1_ref, rstd_ref, after_ref, vec_ref, out_ref = refs[2 + n_got :]
    d = mine_ref[...] + got_ref[...].astype(f32)
    for s in sides:
        d = d + s[...].astype(f32)
    out_ref[...] = after_ref[...] + norm_back(
        d, n1_ref[...].astype(f32), rstd_ref[...], vec_ref[0:1, :]
    )


def finish(grid, mine, got, sides, n1, rstd1, d_after, vec):
    rows, width = n1.shape[0] // 2 // grid.q, n1.shape[1]
    first = pl.BlockSpec((rows, width), lambda i, s: (0, 0))
    own = lambda n: pl.BlockSpec((rows, n), lambda i, s: (s[3], 0))
    return call(
        functools.partial(finish_kernel, len(sides)),
        grid.place,
        [hbm(mine), got] + sides + [n1, rstd1, hbm(d_after), vec],
        grid=(1,),
        in_specs=[first, first]
        + [pl.BlockSpec((rows, width), lambda i, s: (0, 0))] * len(sides)
        + [own(width), own(1), own(width), pl.BlockSpec(vec.shape, lambda i, s: (0, 0))],
        out_specs=pl.BlockSpec((rows, width), lambda i, s: (0, 0)),
        out_shape=jax.ShapeDtypeStruct((rows, width), f32),
        cost_estimate=SMALL,
        mib=20,
        name="finish",
    )


def ff_kernel(grid, ups, downs, place, h2_ref, dy_ref, vec_ref, *refs):
    fast = isinstance(ups, Pieces)
    n_up, n = len(ups.arrays), len(ups.arrays) + len(downs.arrays)
    pieces, refs = refs[:n], refs[n:]
    if fast:
        g_ref, refs = refs[0], refs[1:]
    else:
        (gdown_ref, gup_ref), refs = refs[:2], refs[2:]
    gbias_ref, out_ref, dh_ref, dhb_ref, act_s, dhid_s, h2t_s, up_s, down_s, sem, down_sem = refs
    step = pl.program_id(0)
    rows, width = h2_ref.shape
    units = act_s.shape[1]
    part = 256 if rows % 256 == 0 else rows

    @pl.when(step == 0)
    def _():
        if fast:
            r = up_s.shape[2]
            copies = ups.copies(
                place,
                pieces[:n_up],
                sem,
                [
                    (0, r, 0, width, lambda chip: up_s.at[0, chip]),
                    (r, r, 0, width, lambda chip: up_s.at[1, chip]),
                ],
            )
        else:
            tile = pl.ds(0, units), pl.ds(units, units)
            copies = [
                pltpu.make_async_copy(pieces[0].at[:, tile[i]], up_s.at[i, 0], sem.at[i])
                for i in range(2)
            ]
        copies.append(pltpu.make_async_copy(pieces[n_up].at[:, place[3], pl.ds(0, down_s.shape[1])], down_s, down_sem.at[0]))
        for c in copies:
            c.start()
        h2t_s[...] = h2_ref[...].T
        for c in copies:
            c.wait()

    w_up = up_s[step].reshape(width, units)
    d = down_s.shape[0] // 2
    w_down = down_s[pl.ds(step * d, d)].reshape(units, width)
    bias = jnp.where(step == 0, vec_ref[8:9, :], vec_ref[9:10, :])
    for at in range(0, rows, part):
        here = slice(at, at + part)
        for col in range(0, units, 256):
            cols = slice(col, col + 256)
            hidden = mm(h2_ref[here, :], w_up[:, cols]) + bias[:, cols]
            phi = 0.5 * (1.0 + lax.erf(hidden * (0.5**0.5)))
            dens = jnp.exp(-0.5 * hidden * hidden) * (1.0 / math.sqrt(2.0 * math.pi))
            act_s[here, cols] = (hidden * phi).astype(bf16)
            d_act = mm(dy_ref[here, :], w_down[cols, :], ((1,), (1,)))
            dhid_s[here, cols] = (d_act * (phi + hidden * dens)).astype(bf16)
    act, d_hidden = act_s[...], dhid_s[...]
    gdown = mm(act, dy_ref[...], ((0,), (0,))).astype(bf16)
    gup = mm(h2t_s[...], d_hidden).astype(bf16)
    gbias_ref[0] = sum_rows(d_hidden.astype(f32))
    out = mm(act, w_down)
    dh = mm(d_hidden, w_up, ((1,), (1,)))
    if fast:
        down_shard = 2 * units // grid.chips
        up_shard = width // grid.chips
        half = grid.chips // 2
        for i in range(half):
            column, z = grid.relative(place, step * half + i, True)
            g_ref[column, z, 0:down_shard, :] = gdown[i * down_shard : (i + 1) * down_shard]
        for i in range(grid.chips):
            column, z = grid.relative(place, i, True)
            to = pl.multiple_of(down_shard + step * up_shard, 16)
            g_ref[column, z, pl.ds(to, up_shard), :] = gup[i * up_shard : (i + 1) * up_shard]
    else:
        gdown_ref[...] = gdown
        gup_ref[...] = gup

    @pl.when(step == 0)
    def _():
        out_ref[...] = out
        dh_ref[...] = dh

    @pl.when(step == 1)
    def _():
        out_ref[...] += out
        total = dh_ref[...] + dh
        dh_ref[...] = total
        dhb_ref[...] = total.astype(bf16)


def feed_forward(grid, h2, dy, ups, downs, vec, units):
    fast = isinstance(ups, Pieces)
    rows, width = h2.shape
    tile = units // 2
    chips = grid.chips
    whole = pl.BlockSpec((rows, width), lambda j, s: (0, 0))
    cols = pl.BlockSpec((width, tile), lambda j, s: (0, j))
    lines = pl.BlockSpec((tile, width), lambda j, s: (j, 0))
    if fast:
        shape = (2 * grid.q, grid.z, (units + width * 2) // chips, width)
        g_specs = [pl.BlockSpec(shape, lambda j, s: (0, 0, 0, 0))]
        g_shapes = [pltpu.HBM(shape, bf16)]
        up_shape = (2, chips, width // chips, tile)
    else:
        g_specs = [lines, cols]
        g_shapes = [
            jax.ShapeDtypeStruct((units, width), bf16),
            jax.ShapeDtypeStruct((width, units), bf16),
        ]
        up_shape = (2, 1, width, tile)
    return call(
        functools.partial(ff_kernel, grid, ups, downs),
        grid.place,
        [hbm(h2), hbm(dy), vec] + [hbm(w) for w in ups.arrays + downs.arrays],
        grid=(2,),
        in_specs=[whole, whole, pl.BlockSpec(vec.shape, lambda j, s: (0, 0))]
        + [pl.BlockSpec(memory_space=pl.ANY)] * len(ups.arrays + downs.arrays),
        out_specs=g_specs
        + [pl.BlockSpec((1, 1, tile), lambda j, s: (j, 0, 0)), whole, whole, whole],
        out_shape=g_shapes
        + [
            jax.ShapeDtypeStruct((2, 1, tile), f32),
            pltpu.HBM((rows, width), f32),
            jax.ShapeDtypeStruct((rows, width), f32),
            jax.ShapeDtypeStruct((rows, width), bf16),
        ],
        scratch_shapes=[
            pltpu.VMEM((rows, tile), bf16),
            pltpu.VMEM((rows, tile), bf16),
            pltpu.VMEM((width, rows), bf16),
            pltpu.VMEM(up_shape, bf16),
            pltpu.VMEM((chips, units // chips, width), bf16),
            pltpu.SemaphoreType.DMA((2 * ups.count,)),
            pltpu.SemaphoreType.DMA((downs.count,)),
        ],
        cost_estimate=SMALL,
        mib=40,
        name="feed_forward",
    )


def mine_and_other(place, mine_ref, other_ref, slot, first, shard):
    at = pl.ds(pl.multiple_of(first + shard * place[3], 8), shard)
    return halves(place, mine_ref[slot, at, :], other_ref[slot, at, :].astype(f32))


def last_ff_kernel(grid, shard, place, ff_ref, other_ref, up_ref, down_ref):
    width = ff_ref.shape[1]
    per_chip = down_ref.shape[0]
    down_ref[...] = ff_ref[:per_chip, :]
    half = grid.chips // 2
    for h in range(2):
        first = 2 * shard * h
        at = lambda n: pl.ds(pl.multiple_of(n + first + shard * place[3], 8), shard)
        a, b = halves(place, ff_ref[at(per_chip), :], other_ref[at(0), :].astype(f32))
        for i in range(half):
            to = (h * half + i) * 2 * per_chip
            cols = slice(i * per_chip, (i + 1) * per_chip)
            up_ref[:, to : to + 2 * per_chip] = jnp.concatenate([a[:, cols], b[:, cols]], axis=1)


def last_ff(grid, ff, other, shard):
    rows, width = ff.shape
    whole = lambda shape: pl.BlockSpec(shape, lambda i, s: (0, 0))
    up, down = (shard, 4 * width * 2 // 2), (rows - 4 * shard, width)
    return call(
        functools.partial(last_ff_kernel, grid, shard),
        grid.place,
        [ff, other],
        grid=(1,),
        in_specs=[whole(ff.shape), whole(other.shape)],
        out_specs=[whole(up), whole(down)],
        out_shape=[jax.ShapeDtypeStruct(up, f32), jax.ShapeDtypeStruct(down, f32)],
        cost_estimate=SMALL,
        mib=8,
        name="last_ff",
    )


def last_rest_kernel(
    grid, shard, place, own_ref, other_ref, vec_ref, qkv_ref, out_ref, six_ref, qv_ref, up_ref
):
    pairs, half = own_ref.shape[0] - 1, own_ref.shape[2]
    for p in range(pairs + 1):
        both = mine_and_other(place, own_ref, other_ref, p, 0, shard)
        for core, value in enumerate(both):
            if p == pairs:
                out_ref[:, core * half : (core + 1) * half] = value
                continue
            for t in range(3):
                to = 2 * half * t + half * core + 128 * p
                qkv_ref[:, to : to + 128] = value[:, 128 * t : 128 * (t + 1)]
    width = 2 * half
    vec = jnp.concatenate([vec_ref[0:16, :], vec_ref[16:32, :]], axis=1)
    chip = (place[0] * grid.x + place[1]) * grid.q + place[2]

    def cut(rows, start):
        lane = lax.broadcasted_iota(jnp.int32, (width, 128), 0)
        to = lax.broadcasted_iota(jnp.int32, (width, 128), 1)
        take = (lane == to + start).astype(f32)
        return lax.dot_general(
            rows,
            take,
            (((1,), (0,)), ((), ())),
            precision=lax.Precision.HIGHEST,
            preferred_element_type=f32,
        )

    me = chip * 2 + place[3]
    six_ref[...] = cut(vec[0:8], me * shard)[:, :shard]

    def long(low, high, start, ref):
        n = ref.shape[1]
        rows = jnp.where(start >= width, high, low)
        start = jnp.where(start >= width, start - width, start)
        ref[...] = cut(jnp.broadcast_to(rows, (8, width)), start)[0:1, :n]

    long(vec[6:7], vec[7:8], me * 2 * shard, qv_ref)
    first = place[3] == 0
    low, high = jnp.where(first, vec[8:9], vec[10:11]), jnp.where(first, vec[9:10], vec[11:12])
    long(low, high, chip * up_ref.shape[1], up_ref)


def last_rest(grid, own, other, vec, shard, per_chip):
    half = own.shape[2]
    whole = lambda shape: pl.BlockSpec(shape, lambda i, s: (0,) * len(shape))
    shapes = [(shard, 6 * half), (shard, 2 * half), (8, shard), (1, 2 * shard), (1, per_chip)]
    return call(
        functools.partial(last_rest_kernel, grid, shard),
        grid.place,
        [own, other, vec],
        grid=(1,),
        in_specs=[whole(own.shape), whole(other.shape), whole(vec.shape)],
        out_specs=[whole(s) for s in shapes],
        out_shape=[jax.ShapeDtypeStruct(s, f32) for s in shapes],
        cost_estimate=SMALL,
        mib=8,
        name="last_rest",
    )


def in_order(first, mine, other):
    return jnp.stack([jnp.where(first, mine, other), jnp.where(first, other, mine)])


def body(
    dp,
    blk,
    inputs,
    clip_ids,
    ln1_gain,
    ln1_bias,
    w_qkv,
    qv_bias,
    w_out,
    out_bias,
    ln2_gain,
    ln2_bias,
    w_up,
    up_bias,
    w_down,
    down_bias,
    out_grad,
):
    grid = Grid(dp, blk)
    core = grid.me["c"]
    first = core == 0
    chips = grid.chips
    width = inputs.shape[2]
    half = width // 2
    local = inputs.shape[1]
    chip_rows = 2 * local
    units = w_up.shape[1] // 2
    shard = w_qkv.shape[0]
    per_chip = units // chips
    fast = shard % 8 == 0 and per_chip % 16 == 0
    swap = lambda v: grid.shift(v, "c", 1)
    at_core = lambda v, dim=0: lax.dynamic_index_in_dim(v, core, dim, keepdims=False)
    not_core = lambda v, dim=0: lax.dynamic_index_in_dim(v, 1 - core, dim, keepdims=False)

    pad = jnp.zeros((16, width), bf16).at[0, :local].set(clip_ids[0].astype(bf16))
    mine = jnp.concatenate([inputs[0], pad], axis=0)
    dy_mine = out_grad[0]
    if fast:
        put = lambda v, n: jnp.zeros((128,), bf16).at[:n].set(v)
        place_at = lambda v: jnp.where(first, jnp.pad(v, (0, v.size)), jnp.pad(v, (v.size, 0)))
        vecs = [ln1_gain, ln1_bias, out_bias, ln2_gain, ln2_bias, down_bias, qv_bias]
        rows = jnp.stack([jnp.pad(place_at(v), (0, 128 - 2 * v.size)) for v in vecs])
        up_row = put(up_bias, per_chip)[None]
        blank = jnp.zeros((8, 128), bf16)
        mine_small = jnp.concatenate([rows, up_row, blank])
        their_small = jnp.concatenate([rows, jnp.zeros_like(up_row), blank])
        widen = lambda v: jnp.pad(v, ((0, 0), (0, 3 * half - 128)))
        split = w_qkv.reshape(shard, 3, 2, half)
        my_qkv = at_core(split, 2).reshape(shard, 3 * half)
        to_qkv = not_core(split, 2).reshape(shard, 3 * half)
        up_split = w_up.reshape(shard, chips, 2, per_chip)
        my_up = at_core(up_split, 2).reshape(shard, units)
        to_up = not_core(up_split, 2).reshape(shard, units)
        got = swap(jnp.concatenate([to_qkv, widen(their_small)]))
        pair = in_order(first, my_qkv, got[:shard])
        small_chip = mine_small + got[shard:, :128]
        qkv_piece = jnp.concatenate([pair.reshape(2 * shard, 3 * half), widen(small_chip)])

        lines = lax.all_gather(jnp.concatenate([w_down, w_out]), AXES, axis=0, tiled=False)
        full_out = lines[:, per_chip:].reshape(width, width)
        downs = Whole([lines.reshape(chips, 2, per_chip + shard, width)])
        qkv_piece, x_sent = lock(qkv_piece, mine)
        qkv_z = grid.along(qkv_piece, "z")
        x_far = grid.along(x_sent, "q")
        x_near = swap(x_sent)
        up_pair = in_order(first, my_up, swap(to_up)).reshape(2 * shard, units)
        up_piece = jnp.concatenate([up_pair[:, :width], up_pair[:, width:]])

        qkv_z, x_far, x_near, up_piece = lock(qkv_z, x_far, x_near, up_piece)
        qkv_line = grid.line(qkv_piece, qkv_z)
        qkv_over, qkv_sides = grid.shift(qkv_line, "x", 1), grid.along(qkv_line, "q")
        up_line = grid.exchange(jnp.broadcast_to(up_piece, (grid.z,) + up_piece.shape))
        x_both = [(mine, x_near)] + [(v, swap(v)) for v in x_far]
        dy_near = swap(dy_mine)

        qkv_over, qkv_sides, x_both, dy_near = lock(qkv_over, qkv_sides, x_both, dy_near)
        found = grid.found(
            qkv_line, qkv_over, qkv_sides, grid.corner_pieces(qkv_over, qkv_sides)
        )
        qkv_weights = Pieces(grid, found)
        small_all = pick(grid, found, 2 * shard, 128)
        vec = vectors_of(grid, small_all.reshape(chips * 16, 128), width)
    else:
        whole = lambda v: lax.all_gather(v, AXES, axis=0, tiled=True)
        full_qkv = at_core(whole(w_qkv).reshape(width, 3, 2, half), 2).reshape(width, 3 * half)
        qkv_weights = Whole([full_qkv])
        full_out = whole(w_out)
        full_up = at_core(whole(w_up).reshape(width, chips, 2, per_chip), 2).reshape(width, units)
        full_down = whole(w_down).reshape(chips, 2, per_chip, width)
        ups, downs = Whole([full_up]), Whole([full_down])
        up_all = at_core(whole(up_bias).reshape(chips, 2, per_chip), 1).reshape(2, width)
        singles = [ln1_gain, ln1_bias, out_bias, ln2_gain, ln2_bias, down_bias]
        vec = jnp.concatenate(
            [whole(v)[None] for v in singles]
            + [whole(qv_bias).reshape(2, width), up_all, jnp.zeros((6, width), bf16)]
        ).astype(f32)
        x_both = [(v, swap(v)) for v in [mine] + grid.along(mine, "q")]
        dy_near = swap(dy_mine)

    both = [in_order(first, *v) for v in x_both]
    token_rows = jnp.concatenate([b[:, :local].reshape(chip_rows, width) for b in both])
    clips = jnp.concatenate([b[:, local, :local].reshape(chip_rows) for b in both])
    lane = lax.broadcasted_iota(jnp.int32, (1, 128), 1) % HEAD_DIM
    same = clips[:, None].astype(jnp.int32) == lane
    hot = same[:chip_rows].astype(bf16)
    pen = jnp.where(same | (lane >= 8), 0.0, -1e30).astype(bf16)
    dy = in_order(first, dy_mine, dy_near).reshape(chip_rows, width)

    queries, keys, values, h1t, n1, rstd1, full_qkv = project_qkv(
        grid, behind(token_rows, dy), vec, qkv_weights, local
    )
    pairs = half // 128
    if fast:
        queries, up_line = lock(queries, up_line)
        up_over, up_sides = grid.shift(up_line, "x", 1), grid.along(up_line, "q")
    queries, keys, values = hbm(queries), hbm(keys), hbm(values)
    attended, att, lse = attn_fwd(queries, keys, values, hot, pen, 0, pairs)
    if fast:
        up_over, up_sides = behind((up_over, up_sides), att)
        corners = grid.corner_pieces(up_over, up_sides)
        ups = Pieces(grid, grid.found(up_line, up_over, up_sides, corners, True))
    att_mine, att_other = [att], [swap(att)]
    out_rows = full_out.reshape(2, half, width)
    after, h2, n2, rstd2 = project_out(grid, token_rows, att_mine, att_other, out_rows, vec)

    *g_ff, gbias, ff_out, dh, dh_b = feed_forward(grid, h2, dy, ups, downs, vec, units)
    d_after, d_branch, d_att, sums2 = out_back(grid, dh, swap(dh_b), dy, n2, rstd2, vec, out_rows)

    def back(d, a, n):
        return attn_bwd(queries, keys, values, hot, pen, hbm(attended), d, lse, a, n)

    by_core = lambda v: v.reshape(2, local, width)
    up_sums = gbias.reshape(2, width)
    grads = [back(d_att, 0, 1)]
    if fast:
        ff_over, ff_sides = grid.corners(g_ff[0], grads[0])
        d_att = behind(d_att, ff_over, ff_sides)
    grads.append(back(d_att, 1, pairs - 1))
    g_all = matrix_gradients(grid, fast, h1t, d_branch, att_mine, att_other, grads)
    if fast:
        ff_own = grid.edges(g_ff[0], ff_over, ff_sides, g_all)
        grads, g_all, ff_own = lock(grads, g_all, ff_own)
        ff_z = [grid.shift(ff_own[k], "z", k) for k in range(1, grid.z)]
    else:
        grads, g_all = lock(grads, g_all)
    d_mine, d_other, sums = input_back(grid, grads, full_qkv, n1, sums2, up_sums, local)
    if fast:
        over, sides = grid.corners(g_all, d_other)
        middle = grid.z // 2 - 1
        ends = ff_z[:middle] + ff_z[middle + 1 :]
        d_other, over, sides, ends = lock(d_other, over, sides, ends)
    d_got = swap(d_other)
    sent = [
        total_of(*(v[k * local : (k + 1) * local] for v in (d_mine, d_got))).astype(bf16)
        for k in range(1, grid.q)
    ]
    got = [grid.shift(s, "q", grid.q - k) for k, s in enumerate(sent, 1)]
    if fast:
        vectors = sums + d_got[grid.q * local :].astype(f32)
    ff_out = behind(ff_out, sent)
    out_got = swap(not_core(by_core(ff_out)).astype(bf16)).astype(f32)
    result = at_core(by_core(ff_out)) + out_got + at_core(by_core(after)) + vec[5:6]
    output = result.astype(bf16)[None]
    input_grad = finish(grid, d_mine, d_got, got, n1, rstd1, d_after, vec)[None]

    if fast:
        own = grid.edges(g_all, over, sides, (vectors, sent))
        ff = total_of(ff_own[0], behind(ff_z[middle], own), *ends)
        vectors = jnp.concatenate([vectors[:, :half], vectors[:, half:]]).astype(bf16)
        own, vectors = lock(own, vectors)
        vectors = jnp.broadcast_to(vectors, (grid.z,) + vectors.shape)
        w_up_g, w_down_g = last_ff(grid, ff, swap(ff[per_chip:].astype(bf16)), shard)
        own, vectors = grid.column_near(own, vectors, (output, w_up_g, input_grad))
        vectors = vectors + grid.shift(vectors, "x", 1)
        vectors = vectors + sum(grid.along(vectors, "q"))
        w_qkv_g, w_out_g, six, qv_g, up_g = last_rest(
            grid, own, swap(own.astype(bf16)), vectors, shard, per_chip
        )
        qv_g, up_g = qv_g[0], up_g[0]
    else:
        reduce = lambda v: lax.psum_scatter(v, AXES, scatter_dimension=0, tiled=True)

        def spread(v, dim):
            v = v.astype(f32)
            zero = jnp.zeros_like(v)
            return jnp.stack([jnp.where(first, v, zero), jnp.where(first, zero, v)], axis=dim)

        gdown, gup = g_ff
        w_down_g = reduce(
            spread(gdown.reshape(chips, per_chip, width), 1).reshape(2 * units, width)
        )
        w_up_g = reduce(spread(gup.reshape(width, chips, per_chip), 2).reshape(width, 2 * units))
        w_out_g = reduce(spread(g_all[pairs], 1).reshape(width, width))
        per_pair = g_all[:pairs].reshape(pairs, width, 3, 128)
        per_pair = jnp.transpose(per_pair, (1, 2, 0, 3)).reshape(width, 3, half)
        w_qkv_g = reduce(spread(per_pair, 2).reshape(width, 6 * half))
        sums = lax.psum(sums, AXES)
        me = (lax.axis_index("dp") * blk) + lax.axis_index("blk")
        six = lax.dynamic_slice(sums, (0, me * shard), (6, shard))
        qv_g = lax.dynamic_slice(sums[6:8].reshape(2 * width), (me * 2 * shard,), (2 * shard,))
        up_g = at_core(sums[8:12].reshape(2, units))
        up_g = lax.dynamic_slice(up_g, (me // 2 * per_chip,), (per_chip,))

    return (
        output,
        input_grad,
        six[0],
        six[1],
        w_qkv_g,
        qv_g,
        w_out_g,
        six[2],
        six[3],
        six[4],
        w_up_g,
        up_g,
        w_down_g,
        six[5],
    )


def solution(mesh):
    both = P(("dp", "blk"))
    rows = P(("dp", "blk"), None)
    tokens = P("dp", "blk", None)
    return jax.shard_map(
        functools.partial(body, mesh.shape["dp"], mesh.shape["blk"]),
        mesh=mesh,
        in_specs=(
            tokens,
            P("dp", "blk"),
            both,
            both,
            rows,
            both,
            rows,
            both,
            both,
            both,
            rows,
            both,
            rows,
            both,
            tokens,
        ),
        out_specs=(
            tokens,
            tokens,
            both,
            both,
            rows,
            both,
            rows,
            both,
            both,
            both,
            rows,
            both,
            rows,
            both,
        ),
        check_vma=False,
    )
```
